128 devices in a mesh: section: 2 (over core), seq: 4 (over z), shard: 16 (over x, y).
Axes of the slice: x: 4, y: 4, z: 4, core: 2. Of those that a mesh axis runs over, the one named last changes fastest.
Arguments:
- inputs: bfloat16 [3, 16, 1024, 512], P(None, 'shard', 'seq'), may hold values from -6 to 6
- positions: int32 [3, 16, 1024], P(None, 'shard', 'seq'), may hold values from 0 to 1023, as said below
- cotangent: bfloat16 [3, 16, 1024, 512], P(None, 'shard', 'seq'), may hold values from -6 to 6
- qkv_weight: bfloat16 [2, 512, 1536], P('section', 'shard'), may hold values from -0.25 to 0.25
- proj_weight: bfloat16 [2, 512, 512], P('section', 'shard'), may hold values from -2 to 2
- up_weight: bfloat16 [2, 512, 2048], P('section', 'shard'), may hold values from -0.25 to 0.25
- down_weight: bfloat16 [2, 2048, 512], P('section', 'shard'), may hold values from -0.125 to 0.125
- norm_gain: bfloat16 [2, 2, 512], P('section', None, 'shard'), may hold values from 0.099609375 to 1.8984375
- norm_bias: bfloat16 [2, 2, 512], P('section', None, 'shard'), may hold values from -2 to 2
Outputs:
- activations: bfloat16 [2, 3, 16, 1024, 512], P('section', None, 'shard', 'seq')
- input_grads: bfloat16 [2, 3, 16, 1024, 512], P('section', None, 'shard', 'seq')
- qkv_grad: float32 [2, 512, 1536], P('section', 'shard')
- proj_grad: float32 [2, 512, 512], P('section', 'shard')
- up_grad: float32 [2, 512, 2048], P('section', 'shard')
- down_grad: float32 [2, 2048, 512], P('section', 'shard')
- gain_grad: float32 [2, 2, 512], P('section', None, 'shard')
- bias_grad: float32 [2, 2, 512], P('section', None, 'shard')
The draws below stay inside these ranges and needn't reach their ends.
Inputs may be any that keep to these rules, and one draw needn't show every extreme that they name: Each sequence is a pack of documents: positions count from 0 at a document's first token and rise by one; every sequence starts at 0; for every sequence index one of the 3 micro-batches holds that sequence as a single document of 1024 tokens.
All inputs are finite; a program needn't handle non-finite values.
Results may differ from the reference program's by a relative error of at most 0.018.
Values may be sent and summed in bfloat16 or wider, within the bound.
No kernel may reach another device: no remote copies, remote signals or barrier semaphores. Data moves between devices by JAX's collectives and lax.ppermute only.
A program may use at most 192 MiB of HBM per device.

```python
from functools import partial
import jax
import jax.numpy as jnp
from jax import lax

D = 512
HEADS = 8
HEAD = 64
FF = 2048
ROT = 16
MICRO = 3
SEQS = 16
LEN = 1024


def draw_positions(key, part):
    key = jax.random.fold_in(key, 5)
    first_key, second_key = jax.random.split(key)
    marks = jax.random.randint(first_key, (MICRO, SEQS, LEN), 0, LEN) < 6
    single_doc = jax.random.randint(second_key, (SEQS,), 0, MICRO)
    index_row = jnp.arange(LEN, dtype=jnp.int32)
    starts = jnp.where(marks | (index_row == 0), index_row, 0)
    latest = lax.cummax(starts, axis=2)
    single = jnp.arange(MICRO, dtype=jnp.int32)[:, None, None] == single_doc[None, :, None]
    return jnp.where(single, index_row, index_row - latest).astype(jnp.int32)


def level_of(key, shape, pieces, least, high):
    level, own = 1.0, jax.random.fold_in(key, 6)
    for position, shards_of in pieces:
        draws = jnp.exp(jax.random.uniform(jax.random.fold_in(own, position), (shards_of,), jnp.float32, least / len(pieces), high / len(pieces)))
        level = level * jnp.repeat(draws, shape[position] // shards_of).reshape([-1 if axis == position else 1 for axis in range(len(shape))])
    return level


def centred(stream_key, extent, deviation, limit, cuts=(), held_as=jnp.bfloat16):
    level = level_of(stream_key, extent, cuts, -0.22, 0.18) if cuts else 1.0
    values = jax.random.normal(stream_key, extent, jnp.float32) * deviation * level
    return jnp.minimum(jnp.maximum(values, -limit), limit).astype(held_as)


def setup_inputs(seed: int = 0) -> dict:
    key_list = jax.random.split(jax.random.key(seed), 10)
    return {
        "inputs": centred(key_list[0], (MICRO, SEQS, LEN, D), 1.0, 6.0, ((1, 16), (2, 4))),
        "positions": draw_positions(jax.random.fold_in(key_list[9], 71), 0),
        "cotangent": centred(key_list[2], (MICRO, SEQS, LEN, D), 1.0, 6.0, ((1, 16), (2, 4))),
        "qkv_weight": centred(key_list[3], (2, D, 3 * D), D ** -0.5, 0.25, ((0, 2), (1, 16))),
        "proj_weight": centred(key_list[4], (2, D, D), (D // 64) ** -0.5, 2.0, ((0, 2), (1, 16))),
        "up_weight": centred(key_list[5], (2, D, FF), D ** -0.5, 0.25, ((0, 2), (1, 16))),
        "down_weight": centred(key_list[6], (2, FF, D), FF ** -0.5, 0.125, ((0, 2), (1, 16))),
        "norm_gain": jnp.clip(1.0 + 0.18 * jax.random.normal(key_list[7], (2, 2, D), jnp.float32), 0.099609375, 1.8984375).astype(jnp.bfloat16),
        "norm_bias": centred(key_list[8], (2, 2, D), 0.3, 2.0, ((0, 2), (2, 16))),
    }


@jax.custom_vjp
def low(v):
    return lax.optimization_barrier(v.astype(jnp.bfloat16)).astype(jnp.float32)

@jax.custom_vjp
def low_back(v):
    return v

def low_keep(v):
    return (low(v), None)

def low_pass(kept, grad):
    return (grad,)

def back_keep(v):
    return (v, None)

def back_low(kept, grad):
    return (low(grad),)
low.defvjp(low_keep, low_pass)
low_back.defvjp(back_keep, back_low)
HIGHEST = lax.Precision.HIGHEST
NORM_EPS = 1e-05
MASKED = -1e+30

def angle_table(places):
    halfway = ROT // 2
    rates = 10000.0 ** (-jnp.arange(halfway, dtype=jnp.float32) * 2.0 / ROT)
    return places.astype(jnp.float32)[..., None] * rates

def rotary(values, angles):
    halfway = angles.shape[-1]
    cosine = jnp.cos(angles)[..., None, :]
    sine = jnp.sin(angles)[..., None, :]
    leading = values[..., :halfway]
    trailing = values[..., halfway:2 * halfway]
    return jnp.concatenate([leading * cosine - trailing * sine, trailing * cosine + leading * sine, values[..., 2 * halfway:]], axis=-1)

def layer_norm(values, gain_row, bias_row):
    centre = values - lax.optimization_barrier(jnp.mean(values, axis=-1, keepdims=True))
    spread = lax.optimization_barrier(jnp.mean(centre * centre, axis=-1, keepdims=True))
    return centre * lax.rsqrt(spread + NORM_EPS) * gain_row + bias_row

def one_layer(weights, packed):
    states, places = packed
    qkv_full, proj_full, up_full, down_full, gain_rows, bias_rows = weights
    seq_count, seq_len = places.shape
    attn_in = low(layer_norm(states, gain_rows[0], bias_rows[0]))
    mlp_in = low(layer_norm(states, gain_rows[1], bias_rows[1]))
    mixed = low_back(jnp.einsum('cld,de->cle', attn_in, qkv_full, precision=HIGHEST))
    mixed = mixed.reshape(seq_count, seq_len, 3, HEADS, HEAD)
    angles = angle_table(places)
    query_all = low(low_back(rotary(mixed[:, :, 0], angles)))
    keys_all = low(low_back(rotary(mixed[:, :, 1], angles)))
    values_all = low(low_back(mixed[:, :, 2]))
    scores = low_back(jnp.einsum('cqhd,ckhd->chqk', query_all, keys_all, precision=HIGHEST) * 0.125)
    index_row = jnp.arange(seq_len)
    starts = index_row[None, :] - places
    allowed = (index_row[None, None, :] <= index_row[None, :, None]) & (index_row[None, None, :] >= starts[:, :, None])
    scores = jnp.where(allowed[:, None], scores, MASKED)
    probs = low(jax.nn.softmax(scores, axis=-1))
    heads_out = jnp.einsum('chqk,ckhd->cqhd', probs, values_all, precision=HIGHEST)
    heads_out = low_back(low(heads_out)).reshape(seq_count, seq_len, D)
    attended = jnp.einsum('cld,de->cle', heads_out, proj_full, precision=HIGHEST)
    hidden = low_back(jnp.einsum('cld,df->clf', mlp_in, up_full, precision=HIGHEST))
    active = low(jax.nn.gelu(hidden, approximate=False))
    mlp_out = jnp.einsum('clf,fd->cld', active, down_full, precision=HIGHEST)
    return states + attended + mlp_out

def run_layer(states, places, weights):
    total_seqs = states.shape[0]
    grouped = states.reshape(total_seqs // 2, 2, LEN, D)
    grouped_places = places.reshape(total_seqs // 2, 2, LEN)
    result = lax.map(jax.checkpoint(partial(one_layer, weights)), (grouped, grouped_places))
    return result.reshape(total_seqs, LEN, D)

def reference(inputs, positions, cotangent, qkv_weight, proj_weight, up_weight, down_weight, norm_gain, norm_bias):
    source = inputs.reshape(MICRO * SEQS, LEN, D).astype(jnp.float32)
    places = positions.reshape(MICRO * SEQS, LEN).astype(jnp.int32)
    weights = tuple((weight.astype(jnp.float32) for weight in (qkv_weight, proj_weight, up_weight, down_weight, norm_gain, norm_bias)))
    probe = jnp.zeros((MICRO * SEQS, LEN, D), jnp.float32)

    def forward(source_in, probe_in, weights_in):
        first_weights = tuple((weight[0] for weight in weights_in))
        second_weights = tuple((weight[1] for weight in weights_in))
        first_out = low(run_layer(low_back(source_in), places, first_weights))
        second_out = low(run_layer(low_back(first_out + probe_in), places, second_weights))
        return (second_out, first_out)
    second_out, pullback, first_out = jax.vjp(forward, source, probe, weights, has_aux=True)
    source_grad, probe_grad, weight_grads = pullback(cotangent.reshape(MICRO * SEQS, LEN, D).astype(jnp.float32))
    out_shape = (2, MICRO, SEQS, LEN, D)
    activations = jnp.stack([first_out, second_out]).reshape(out_shape).astype(jnp.bfloat16)
    input_grads = jnp.stack([source_grad, probe_grad]).reshape(out_shape).astype(jnp.bfloat16)
    return (activations, input_grads, weight_grads[0], weight_grads[1], weight_grads[2], weight_grads[3], weight_grads[4], weight_grads[5])
```

```python
import functools

import jax
import jax.numpy as jnp
from jax import lax
from jax.experimental import pallas as pl
from jax.experimental.pallas import tpu as pltpu
from jax.sharding import PartitionSpec as P

D = 512
HEADS = 8
HEAD = 64
ROT = 16
MICRO = 3
BLOCK = 256
TOKENS = MICRO * BLOCK
NORM_EPS = 1e-05
MASKED = -1e30
BF = jnp.bfloat16
F32 = jnp.float32
SHIFTS = (0, 1, 2, 3)
VMEM_LIMIT = 40 * 1024 * 1024


def dims(left, right, left_dim, right_dim):
    return lax.dot_general(
        left, right, (((left_dim,), (right_dim,)), ((), ())), preferred_element_type=F32
    )


def struct(shape, dtype):
    return jax.ShapeDtypeStruct(shape, dtype)


def call(body, place, grid, ins, outs, scratch=(), flops=10**9, moved=4 * 10**6):
    specs = [pl.BlockSpec(block, index) for _, block, index in ins]
    out_specs = [pl.BlockSpec(block, index) for _, _, block, index in outs]
    return pl.pallas_call(
        body,
        out_shape=[struct(shape, dtype) for shape, dtype, _, _ in outs],
        grid_spec=pltpu.PrefetchScalarGridSpec(
            num_scalar_prefetch=1,
            grid=grid,
            in_specs=specs,
            out_specs=out_specs,
            scratch_shapes=list(scratch),
        ),
        compiler_params=pltpu.CompilerParams(
            vmem_limit_bytes=VMEM_LIMIT, dimension_semantics=("arbitrary",) * len(grid)
        ),
        cost_estimate=pl.CostEstimate(flops=flops, bytes_accessed=moved, transcendentals=0),
    )(place, *[array for array, _, _ in ins])


def whole(array):
    rank = array.ndim
    return (array, array.shape, lambda *_: (0,) * rank)


def whole_out(shape, dtype):
    rank = len(shape)
    return (shape, dtype, shape, lambda *_: (0,) * rank)


def rows(array):
    return (array, (BLOCK, array.shape[1]), lambda m, _: (m, 0))


def rows_out(width, dtype):
    return ((TOKENS, width), dtype, (BLOCK, width), lambda m, _: (m, 0))


def lanes(array):
    lead = array.shape[:-1]
    rank = len(lead)
    return (array, lead + (BLOCK,), lambda m, _: (0,) * rank + (m,))


def lanes_out(lead, dtype):
    rank = len(lead)
    return (lead + (TOKENS,), dtype, lead + (BLOCK,), lambda m, _: (0,) * rank + (m,))


def by_micro(array):
    rank = array.ndim - 1
    return (array, (1,) + array.shape[1:], lambda m, _: (m,) + (0,) * rank)


def by_micro_out(shape, dtype):
    rank = len(shape) - 1
    return (shape, dtype, (1,) + shape[1:], lambda m, _: (m,) + (0,) * rank)


def pack_body(place, qkv, proj, up, down, mine, other, held):
    low = lax.broadcasted_iota(jnp.int32, (32, 128), 1) < 64
    for half in range(2):
        for pair in range(8):
            first = up[:, 256 * pair : 256 * pair + 128].astype(F32)
            second = up[:, 256 * pair + 128 : 256 * pair + 256].astype(F32)
            if half == 0:
                cut = jnp.where(low, first, pltpu.roll(second, 64, 1))
            else:
                cut = jnp.where(low, pltpu.roll(first, 64, 1), second)
            at = 128 * (pair % 2)
            held[half, 32 * (pair // 2) : 32 * (pair // 2) + 32, at : at + 128] = cut.astype(BF)
        for side in range(2):
            held[half, 128 + 64 * side : 192 + 64 * side, :] = down[
                64 * half : 64 * half + 64, 256 * side : 256 * side + 256
            ]
            held[half, 256 + 32 * side : 288 + 32 * side, :] = proj[
                :, 256 * side : 256 * side + 256
            ]
        for part in range(3):
            at = 512 * part + 256 * half
            held[half, 320 + 32 * part : 352 + 32 * part, :] = qkv[:, at : at + 256]
    core = place[1]
    mine[...] = held[core]
    other[...] = held[1 - core]


def pack_weights(place, qkv, proj, up, down):
    return call(
        pack_body,
        place,
        (1,),
        [whole(qkv), whole(proj), whole(up), whole(down)],
        [whole_out((416, 256), BF), whole_out((416, 256), BF)],
        [pltpu.VMEM((2, 416, 256), BF)],
    )


def sort_body(place, mine, received, norms, early, middle, late):
    first = place[1] == 0
    kept = mine[...]
    came = received[...]
    layer0 = jnp.where(first, kept, came)
    layer1 = jnp.where(first, came, kept)
    early[0:96, :] = layer0[320:416]
    early[96:112, :] = norms[...]
    middle[0:320, :] = layer0[0:320]
    middle[320:416, :] = layer1[320:416]
    late[...] = layer1[0:320]


def sort_weights(place, mine, received, norms):
    return call(
        sort_body,
        place,
        (1,),
        [whole(mine), whole(received), whole(norms)],
        [whole_out((112, 256), BF), whole_out((416, 256), BF), whole_out((320, 256), BF)],
    )


def assemble_body(place, a, b, c, d, out):
    for step, ref in enumerate((a, b, c, d)):
        column = lax.rem(place[3] - step + 4, 4)
        for inner in range(4):
            row = lax.rem(place[2] - inner + 4, 4)
            out[row * 4 + column] = ref[inner]


def assemble(place, pieces):
    return call(
        assemble_body,
        place,
        (1,),
        [whole(piece) for piece in pieces],
        [whole_out((16, 112, 256), BF)],
    )[0]


def shift_x(value, step):
    pairs = [(x * 4 + y, (x + step) % 4 * 4 + y) for x in range(4) for y in range(4)]
    return lax.ppermute(value, "shard", pairs)


def shift_y(value, step):
    pairs = [(x * 4 + y, x * 4 + (y + step) % 4) for x in range(4) for y in range(4)]
    return lax.ppermute(value, "shard", pairs)


def shift_z(value, step):
    return lax.ppermute(value, "seq", [(z, (z + step) % 4) for z in range(4)])


def swap_core(value):
    return lax.ppermute(value, "section", [(0, 1), (1, 0)])


def gather_now(place, value):
    line = jnp.stack([value] + [shift_x(value, step) for step in (1, 3, 2)])
    line = [line[0], line[1], line[3], line[2]]
    line = jnp.stack(line)
    pieces = {0: line}
    for step in (1, 3, 2):
        pieces[step] = shift_y(line, step)
    return assemble(place, [pieces[step] for step in SHIFTS])


def regroup(values):
    got = {0: values[0]}
    for step in (1, 3, 2):
        got[step] = shift_z(values[step], step)
    return [got[step] for step in SHIFTS]


def unit_of(states):
    centre = states - jnp.mean(states, axis=-1, keepdims=True)
    scaled = lax.rsqrt(jnp.mean(centre * centre, axis=-1, keepdims=True) + NORM_EPS)
    return centre * scaled, scaled


def before_body(with_sum, place, *refs):
    refs = list(refs)
    states_ref = refs.pop(0)
    states = states_ref[...].astype(F32)
    if with_sum:
        part_a, part_b = refs.pop(0), refs.pop(0)
        states = (states + (part_a[...] + part_b[...])).astype(BF)
    wq, wk, wv, norms, turns = refs[:5]
    outs = refs[5:9]
    attn_ref, mlp_ref = refs[9:11]
    held = refs[-1]
    if with_sum:
        refs[11][...] = states
        states = states.astype(F32)
    unit, _ = unit_of(states)
    attn_in = (unit * norms[0:1, :] + norms[2:3, :]).astype(BF)
    attn_ref[...] = attn_in
    mlp_ref[...] = (unit * norms[1:2, :] + norms[3:4, :]).astype(BF)
    cosine, sine = turns[0], turns[1]
    for part, weight in enumerate((wq, wk, wv)):
        mixed = dims(weight[...].reshape(D, 256), attn_in, 0, 1)
        for head in range(4):
            block = mixed[64 * head : 64 * head + 64]
            if part < 2:
                a, b = block[0:8], block[8:16]
                block = jnp.concatenate(
                    [a * cosine - b * sine, b * cosine + a * sine, block[16:]], axis=0
                )
            if part == 0:
                block = block * 0.125
            held[head, 64 * part : 64 * part + 64, :] = block.astype(BF)
    for step in SHIFTS:
        outs[step][...] = held[lax.rem(place[0] + step, 4)]


def before_layer(place, states, parts, weights, norms, turns):
    array, first = weights
    ins = [rows(states)] + [rows(part) for part in parts]
    for part in range(3):
        ins.append(
            (array, (16, 32, 256), functools.partial(lambda at, m, _: (0, at, 0), first + part))
        )
    ins += [whole(norms), lanes(turns)]
    outs = [lanes_out((192,), BF) for _ in SHIFTS] + [rows_out(D, BF), rows_out(D, BF)]
    if parts:
        outs.append(rows_out(D, BF))
    return call(
        functools.partial(before_body, bool(parts)),
        place,
        (MICRO,),
        ins,
        outs,
        [pltpu.VMEM((4, 192, BLOCK), BF)],
        flops=1_200_000_000,
        moved=6_000_000,
    )


def mlp_body(place, mlp_in, up, down, out, active_ref, slope_ref):
    step = pl.program_id(0)
    hidden = jnp.dot(mlp_in[...], up[...].reshape(D, 256), preferred_element_type=F32)
    cdf = 0.5 * (1.0 + lax.erf(hidden * 0.7071067811865476))
    pdf = jnp.exp(-0.5 * hidden * hidden) * 0.3989422804014327
    active = (hidden * cdf).astype(BF)
    active_ref[...] = active
    slope_ref[...] = cdf + hidden * pdf
    lower = down[...]
    both = jnp.concatenate(
        [lower[:, 0:64].reshape(256, 256), lower[:, 64:128].reshape(256, 256)], axis=1
    )
    product = jnp.dot(active, both, preferred_element_type=F32)

    @pl.when(step == 0)
    def _():
        out[...] = product

    @pl.when(step > 0)
    def _():
        out[...] += product


def mlp_layer(place, mlp_in, weights):
    return call(
        mlp_body,
        place,
        (4,),
        [
            whole(mlp_in),
            (weights, (16, 32, 256), lambda b, _: (0, b, 0)),
            (weights, (4, 128, 256), lambda b, _: (b, 1, 0)),
        ],
        [
            whole_out((TOKENS, D), F32),
            ((TOKENS, 1024), BF, (TOKENS, 256), lambda b, _: (0, b)),
            ((TOKENS, 1024), F32, (TOKENS, 256), lambda b, _: (0, b)),
        ],
        flops=6_000_000_000,
        moved=12_000_000,
    )


def put_starts(place, places, starts):
    along = lax.broadcasted_iota(jnp.int32, (1, BLOCK), 1)
    for step in SHIFTS:
        source = lax.rem(place[0] - step + 4, 4)
        starts[source] = along + BLOCK * source - places[step][...]


def allowed_keys(starts, query_block, key_block):
    keys = lax.broadcasted_iota(jnp.int32, (BLOCK, BLOCK), 0) + BLOCK * key_block
    allowed = keys >= starts[query_block]
    if query_block == key_block:
        queries = lax.broadcasted_iota(jnp.int32, (BLOCK, BLOCK), 1) + BLOCK * query_block
        allowed = allowed & (keys <= queries)
    return allowed


def attend_body(place, *refs):
    came, places = refs[0:4], refs[4:8]
    outs = refs[8:12]
    kept, heads_out, log_total = refs[12:15]
    starts, keys = refs[15:17]
    for step in SHIFTS:
        source = lax.rem(place[0] - step + 4, 4)
        kept[0, source] = came[step][...]
    put_starts(place, places, starts)
    for j in range(4):
        keys[j] = kept[0, j, 64:128].T
    for i in range(4):
        query = kept[0, i, 0:64]
        scores = []
        for j in range(i + 1):
            raw = jnp.dot(keys[j], query, preferred_element_type=F32)
            scores.append(jnp.where(allowed_keys(starts, i, j), raw, MASKED))
        peak = functools.reduce(
            jnp.maximum, [jnp.max(s, axis=0, keepdims=True) for s in scores]
        )
        total = jnp.zeros((1, BLOCK), F32)
        acc = jnp.zeros((HEAD, BLOCK), F32)
        for j in range(i + 1):
            probs = jnp.exp(scores[j] - peak)
            total = total + jnp.sum(probs, axis=0, keepdims=True)
            acc = acc + jnp.dot(
                kept[0, j, 128:192], probs.astype(BF), preferred_element_type=F32
            )
        heads_out[0, i] = (acc / total).astype(BF)
        log_total[0, i] = peak + jnp.log(total)
    for step in SHIFTS:
        outs[step][...] = heads_out[0, lax.rem(place[0] + step, 4)]


def attend(place, came, places):
    return call(
        attend_body,
        place,
        (MICRO,),
        [lanes(piece) for piece in came] + [lanes(piece) for piece in places],
        [lanes_out((HEAD,), BF) for _ in SHIFTS]
        + [
            by_micro_out((MICRO, 4, 192, BLOCK), BF),
            by_micro_out((MICRO, 4, HEAD, BLOCK), BF),
            by_micro_out((MICRO, 4, 1, BLOCK), F32),
        ],
        [pltpu.VMEM((4, 1, BLOCK), jnp.int32), pltpu.VMEM((4, BLOCK, HEAD), BF)],
        flops=8_000_000_000,
        moved=4_000_000,
    )


def after_body(place, *refs):
    came = refs[0:4]
    proj, mlp_out, out, heads = refs[4:8]
    for step in SHIFTS:
        source = lax.rem(place[0] - step + 4, 4)
        at = pl.multiple_of(source * HEAD, HEAD)
        heads[pl.ds(at, HEAD), :] = came[step][...]
    held = heads[...]
    weight = proj[...]
    for side in range(2):
        span = slice(256 * side, 256 * side + 256)
        product = dims(held, weight[:, 32 * side : 32 * side + 32].reshape(256, 256), 0, 0)
        out[:, span] = mlp_out[:, span] + product


def after_layer(place, came, weights, mlp_out):
    return call(
        after_body,
        place,
        (MICRO,),
        [lanes(piece) for piece in came]
        + [(weights, (8, 64, 256), lambda m, place: (place[1], 4, 0)), rows(mlp_out)],
        [rows_out(D, F32), lanes_out((256,), BF)],
        flops=800_000_000,
        moved=4_000_000,
    )


def heads_grad_body(place, grad, proj, *refs):
    outs, held = refs[0:4], refs[4]
    weight = proj[...]
    total = dims(weight[:, 0:32].reshape(256, 256), grad[:, 0:256], 1, 1) + dims(
        weight[:, 32:64].reshape(256, 256), grad[:, 256:512], 1, 1
    )
    for head in range(4):
        held[head] = total[64 * head : 64 * head + 64].astype(BF)
    for step in SHIFTS:
        outs[step][...] = held[lax.rem(place[0] + step, 4)]


def heads_grad(place, grad, weights):
    return call(
        heads_grad_body,
        place,
        (MICRO,),
        [rows(grad), (weights, (8, 64, 256), lambda m, place: (place[1], 4, 0))],
        [lanes_out((HEAD,), BF) for _ in SHIFTS],
        [pltpu.VMEM((4, HEAD, BLOCK), BF)],
        flops=800_000_000,
        moved=2_000_000,
    )


def mlp_back_body(place, grad, active, slope, mlp_in, up, down, out, pack):
    step = pl.program_id(0)
    lower = down[...]
    both = jnp.concatenate(
        [lower[:, 0:64].reshape(256, 256), lower[:, 64:128].reshape(256, 256)], axis=1
    )
    active_grad = dims(grad[...], both, 1, 1)
    hidden_grad = (active_grad * slope[...]).astype(BF)
    product = dims(hidden_grad, up[...].reshape(D, 256), 1, 1)

    @pl.when(step == 0)
    def _():
        out[...] = product

    @pl.when(step > 0)
    def _():
        out[...] += product

    up_part = dims(mlp_in[...], hidden_grad, 0, 0).astype(BF).reshape(16, 32, 256)
    at = pl.multiple_of(32 * lax.rem(step, 2), 32)
    pack[lax.div(step, 2), :, pl.ds(at, 32), :] = up_part
    down_part = dims(active[...], grad[...], 0, 0).astype(BF)
    for side in range(2):
        pack[2 + side, pl.ds(4 * step, 4)] = down_part[:, 256 * side : 256 * side + 256].reshape(
            4, 64, 256
        )


def mlp_back(place, grad, active, slope, mlp_in, weights):
    return call(
        mlp_back_body,
        place,
        (4,),
        [
            whole(grad),
            (active, (TOKENS, 256), lambda b, _: (0, b)),
            (slope, (TOKENS, 256), lambda b, _: (0, b)),
            whole(mlp_in),
            (weights, (16, 32, 256), lambda b, _: (0, b, 0)),
            (weights, (4, 128, 256), lambda b, _: (b, 1, 0)),
        ],
        [whole_out((TOKENS, D), F32), whole_out((4, 16, 64, 256), BF)],
        flops=8_000_000_000,
        moved=14_000_000,
    )


def attend_back_body(place, *refs):
    came, places = refs[0:4], refs[4:8]
    kept_ref, heads_out, log_total = refs[8:11]
    outs = refs[11:15]
    starts, keys, values, grads, acc = refs[15:20]
    for step in SHIFTS:
        source = lax.rem(place[0] - step + 4, 4)
        grads[source] = came[step][...]
    put_starts(place, places, starts)
    acc[...] = jnp.zeros_like(acc)
    for j in range(4):
        keys[j] = kept_ref[0, j, 64:128].T
        values[j] = kept_ref[0, j, 128:192].T
    for i in range(4):
        query = kept_ref[0, i, 0:64]
        grad = grads[i]
        log_row = log_total[0, i]
        centre = jnp.sum(
            grad.astype(F32) * heads_out[0, i].astype(F32), axis=0, keepdims=True
        )
        query_grad = jnp.zeros((HEAD, BLOCK), F32)
        for j in range(i + 1):
            raw = jnp.dot(keys[j], query, preferred_element_type=F32)
            probs = jnp.where(allowed_keys(starts, i, j), jnp.exp(raw - log_row), 0.0)
            probs_grad = jnp.dot(values[j], grad, preferred_element_type=F32)
            scores_grad = (probs * (probs_grad - centre)).astype(BF)
            acc[j, 128:192, :] += dims(grad, probs.astype(BF), 1, 1)
            acc[j, 64:128, :] += dims(query, scores_grad, 1, 1)
            query_grad = query_grad + jnp.dot(
                kept_ref[0, j, 64:128], scores_grad, preferred_element_type=F32
            )
        acc[i, 0:64, :] = query_grad * 0.125
    for step in SHIFTS:
        outs[step][...] = acc[lax.rem(place[0] + step, 4)].astype(BF)


def attend_back(place, came, places, kept, heads_out, log_total):
    return call(
        attend_back_body,
        place,
        (MICRO,),
        [lanes(piece) for piece in came]
        + [lanes(piece) for piece in places]
        + [by_micro(kept), by_micro(heads_out), by_micro(log_total)],
        [lanes_out((192,), BF) for _ in SHIFTS],
        [
            pltpu.VMEM((4, 1, BLOCK), jnp.int32),
            pltpu.VMEM((4, BLOCK, HEAD), BF),
            pltpu.VMEM((4, BLOCK, HEAD), BF),
            pltpu.VMEM((4, HEAD, BLOCK), BF),
            pltpu.VMEM((4, 192, BLOCK), F32),
        ],
        flops=16_000_000_000,
        moved=5_000_000,
    )


def mixed_back_body(place, *refs):
    came = refs[0:4]
    wq, wk, wv, norms, turns, states, mlp_grad = refs[4:11]
    out, mixed_ref, sums = refs[11:14]
    cosine, sine = turns[0], turns[1]
    for step in SHIFTS:
        head = lax.rem(place[0] - step + 4, 4)
        at = pl.multiple_of(head * HEAD, HEAD)
        for part in range(3):
            block = came[step][64 * part : 64 * part + 64]
            if part < 2:
                a, b = block[0:8].astype(F32), block[8:16].astype(F32)
                turned = jnp.concatenate(
                    [a * cosine + b * sine, b * cosine - a * sine], axis=0
                ).astype(BF)
                block = jnp.concatenate([turned, block[16:]], axis=0)
            mixed_ref[part, pl.ds(at, HEAD), :] = block
    attn_grad = jnp.zeros((BLOCK, D), F32)
    for part, weight in enumerate((wq, wk, wv)):
        attn_grad = attn_grad + dims(mixed_ref[part], weight[...].reshape(D, 256), 0, 1)
    unit, _ = unit_of(states[...].astype(F32))
    other_grad = mlp_grad[...]
    out[...] = attn_grad * norms[0:1, :] + other_grad * norms[1:2, :]

    @pl.when(pl.program_id(0) == 0)
    def _():
        sums[...] = jnp.zeros_like(sums)

    sums[0:1, :] += jnp.sum(attn_grad * unit, axis=0, keepdims=True)
    sums[1:2, :] += jnp.sum(other_grad * unit, axis=0, keepdims=True)
    sums[2:3, :] += jnp.sum(attn_grad, axis=0, keepdims=True)
    sums[3:4, :] += jnp.sum(other_grad, axis=0, keepdims=True)


def mixed_back(place, came, weights, norms, turns, states, mlp_grad):
    array, first = weights
    ins = [lanes(piece) for piece in came]
    for part in range(3):
        ins.append(
            (array, (16, 32, 256), functools.partial(lambda at, m, _: (0, at, 0), first + part))
        )
    ins += [whole(norms), lanes(turns), rows(states), rows(mlp_grad)]
    return call(
        mixed_back_body,
        place,
        (MICRO,),
        ins,
        [
            rows_out(D, F32),
            lanes_out((3, 256), BF),
            whole_out((8, D), F32),
        ],
        flops=1_500_000_000,
        moved=6_000_000,
    )


def weight_back_body(place, attn_in, mixed, heads, grad, pack):
    for part in range(3):
        product = dims(attn_in[...], mixed[part], 0, 1)
        pack[part] = product.astype(BF).reshape(16, 32, 256)
    product = jnp.dot(heads[...], grad[...], preferred_element_type=F32)
    pack[3] = product.astype(BF).reshape(16, 32, 256)


def weight_back(place, attn_in, mixed, heads, grad):
    return call(
        weight_back_body,
        place,
        (1,),
        [
            whole(attn_in),
            whole(mixed),
            whole(heads),
            (grad, (TOKENS, 256), lambda m, place: (0, place[1])),
        ],
        [whole_out((4, 16, 32, 256), BF)],
        flops=2_000_000_000,
        moved=6_000_000,
    )[0]


def end_body(place, states, grad, own, came, out):
    unit, scaled = unit_of(states[...].astype(F32))
    through = own[...] + came[...]
    back = scaled * (
        through
        - jnp.mean(through, axis=-1, keepdims=True)
        - unit * jnp.mean(through * unit, axis=-1, keepdims=True)
    )
    out[...] = (grad[...].astype(F32) + back).astype(BF)


def end_back(place, states, grad, own, came):
    return call(
        end_body,
        place,
        (MICRO,),
        [rows(states), rows(grad), rows(own), rows(came)],
        [rows_out(D, BF)],
        flops=100_000_000,
        moved=5_000_000,
    )[0]


def scatter_sum(pack):
    depth = pack.shape[2]
    flat = pack.reshape(64, depth, 256)
    got = lax.all_to_all(flat, ("seq", "shard"), 0, 0, tiled=True)
    return jnp.sum(got.astype(F32), axis=0).astype(BF)


def unpack_body(place, a, b, c, d, qkv, proj, up, down, held):
    for step, ref in enumerate((a, b, c, d)):
        held[lax.rem(place[0] - step + 4, 4)] = ref[...].astype(F32)
    low = lax.broadcasted_iota(jnp.int32, (32, 128), 1) < 64
    for half in range(2):
        for part in range(3):
            at = 512 * part + 256 * half
            qkv[:, at : at + 256] = held[part, half, 64:96]
        proj[:, 256 * half : 256 * half + 256] = held[3, half, 64:96]
        for side in range(2):
            down[64 * half : 64 * half + 64, 256 * side : 256 * side + 256] = held[
                2 + side, half, 0:64
            ]
    for tile in range(16):
        block = tile // 4
        at = 128 * (tile % 4 // 2)
        row = 32 * (block % 2)
        left = held[block // 2, 0, row : row + 32, at : at + 128]
        right = held[block // 2, 1, row : row + 32, at : at + 128]
        if tile % 2 == 0:
            joined = jnp.where(low, left, pltpu.roll(right, 64, 1))
        else:
            joined = jnp.where(low, pltpu.roll(left, 64, 1), right)
        up[:, 128 * tile : 128 * tile + 128] = joined


def unpack(place, pieces):
    return call(
        unpack_body,
        place,
        (1,),
        [whole(piece) for piece in pieces],
        [
            whole_out((32, 1536), F32),
            whole_out((32, 512), F32),
            whole_out((32, 2048), F32),
            whole_out((128, 512), F32),
        ],
        [pltpu.VMEM((4, 2, 96, 256), F32)],
    )


def on_device(
    inputs,
    positions,
    cotangent,
    qkv_weight,
    proj_weight,
    up_weight,
    down_weight,
    norm_gain,
    norm_bias,
):
    core = lax.axis_index("section")
    chip_z = lax.axis_index("seq")
    shard = lax.axis_index("shard")
    first = core == 0
    place = jnp.stack([chip_z, core, shard // 4, shard % 4]).astype(jnp.int32)

    mine, other = pack_weights(
        place, qkv_weight[0], proj_weight[0], up_weight[0], down_weight[0]
    )
    own_norms = jnp.concatenate([norm_gain[0], norm_bias[0]], axis=0).reshape(1, 128)
    other_norms = swap_core(jnp.broadcast_to(own_norms, (16, 128)))[0:1]
    both_norms = jnp.where(
        first,
        jnp.concatenate([own_norms, other_norms], axis=1),
        jnp.concatenate([other_norms, own_norms], axis=1),
    )
    early, middle, late = sort_weights(
        place, mine, swap_core(other), jnp.broadcast_to(both_norms, (16, 256))
    )
    gathered = gather_now(place, early)
    middle_all = lax.all_gather(middle, "shard")
    late_all = lax.all_gather(late, "shard")
    norms = (
        gathered[:, 96, :]
        .reshape(16, 2, 4, 32)
        .transpose(1, 2, 0, 3)
        .reshape(2, 4, D)
        .astype(F32)
    )
    qkv_of = ((gathered, 0), (middle_all, 10))
    rest_of = (middle_all, late_all)

    places_row = positions.reshape(1, TOKENS)
    places = regroup([places_row] * 4)
    rates = 10000.0 ** (-jnp.arange(ROT // 2, dtype=F32) * 2.0 / ROT)
    angles = rates[:, None] * places_row.astype(F32)
    turns = jnp.stack([jnp.cos(angles), jnp.sin(angles)])

    states = inputs.reshape(TOKENS, D)
    parts = ()
    saved = []
    for layer in range(2):
        done = before_layer(place, states, parts, qkv_of[layer], norms[layer], turns)
        sent, attn_in, mlp_in = done[0:4], done[4], done[5]
        if parts:
            states = done[6]
        came = regroup(sent)
        mlp_out, active, slope = mlp_layer(place, mlp_in, rest_of[layer])
        done = attend(place, came, places)
        kept, heads_out, log_total = done[4:7]
        part, heads = after_layer(place, regroup(done[0:4]), rest_of[layer], mlp_out)
        parts = (part, swap_core(part))
        other_heads = swap_core(heads)
        all_heads = jnp.where(
            first,
            jnp.concatenate([heads, other_heads], axis=0),
            jnp.concatenate([other_heads, heads], axis=0),
        )
        saved.append(
            (states, attn_in, mlp_in, active, slope, kept, heads_out, log_total, all_heads)
        )
    result = (states.astype(F32) + (parts[0] + parts[1])).astype(BF)
    layer_out = jnp.where(first, saved[1][0], result)

    grad = cotangent.reshape(TOKENS, D)
    grads = [None, None]
    reduced = [None, None]
    sums = [None, None]
    for layer in (1, 0):
        states, attn_in, mlp_in, active, slope, kept, heads_out, log_total, all_heads = saved[
            layer
        ]
        came = regroup(heads_grad(place, grad, rest_of[layer]))
        mlp_grad, pack_a = mlp_back(place, grad, active, slope, mlp_in, rest_of[layer])
        sent = attend_back(place, came, places, kept, heads_out, log_total)
        through, mixed, norm_sums = mixed_back(
            place, regroup(sent), qkv_of[layer], norms[layer], turns, states, mlp_grad
        )
        pack_b = weight_back(place, attn_in, mixed, all_heads, grad)
        reduced[layer] = (scatter_sum(pack_a), scatter_sum(pack_b))
        sums[layer] = lax.psum(norm_sums[0:4], ("section", "seq", "shard"))
        grad = end_back(place, states, grad, through, swap_core(through))
        grads[layer] = grad
    grads_out = jnp.where(first, grads[0], grads[1])

    layer_sums = [jnp.concatenate(reduced[layer], axis=0) for layer in range(2)]
    keep = jnp.where(first, layer_sums[0], layer_sums[1])
    got = swap_core(jnp.where(first, layer_sums[1], layer_sums[0]))
    halves = jnp.where(first, jnp.stack([keep, got]), jnp.stack([got, keep]))
    qkv_grad, proj_grad, up_grad, down_grad = unpack(place, regroup([halves] * 4))
    own_sums = jnp.where(first, sums[0], sums[1])
    own_sums = lax.dynamic_slice_in_dim(own_sums, 32 * shard, 32, axis=1)
    return (
        layer_out.reshape(1, MICRO, 1, BLOCK, D),
        grads_out.reshape(1, MICRO, 1, BLOCK, D),
        qkv_grad[None],
        proj_grad[None],
        up_grad[None],
        down_grad[None],
        own_sums[None, 0:2],
        own_sums[None, 2:4],
    )


def solution(mesh):
    placed = (
        P(None, "shard", "seq", None),
        P(None, "shard", "seq"),
        P(None, "shard", "seq", None),
        P("section", "shard", None),
        P("section", "shard", None),
        P("section", "shard", None),
        P("section", "shard", None),
        P("section", None, "shard"),
        P("section", None, "shard"),
    )
    return jax.shard_map(
        on_device,
        mesh=mesh,
        in_specs=placed,
        out_specs=(
            P("section", None, "shard", "seq", None),
            P("section", None, "shard", "seq", None),
            P("section", "shard", None),
            P("section", "shard", None),
            P("section", "shard", None),
            P("section", "shard", None),
            P("section", None, "shard"),
            P("section", None, "shard"),
        ),
        check_vma=False,
    )
```

```python
import functools

import jax
import jax.numpy as jnp
from jax import lax
from jax.experimental import pallas as pl
from jax.experimental.pallas import tpu as pltpu
from jax.sharding import PartitionSpec as P

D = 512
HEADS = 8
HEAD = 64
ROT = 16
MICRO = 3
BLOCK = 256
TOKENS = MICRO * BLOCK
NORM_EPS = 1e-05
MASKED = -1e30
BF = jnp.bfloat16
F32 = jnp.float32
SHIFTS = (0, 1, 2, 3)
VMEM_LIMIT = 24 * 1024 * 1024


def dims(left, right, left_dim, right_dim):
    return lax.dot_general(
        left, right, (((left_dim,), (right_dim,)), ((), ())), preferred_element_type=F32
    )


def struct(shape, dtype):
    return jax.ShapeDtypeStruct(shape, dtype)


def call(body, place, grid, ins, outs, scratch=(), flops=10**9, moved=4 * 10**6):
    specs = [pl.BlockSpec(block, index) for _, block, index in ins]
    out_specs = [pl.BlockSpec(out[2], out[3]) for out in outs]
    return pl.pallas_call(
        body,
        out_shape=[
            (pltpu.HBM if out[4:] else struct)(out[0], out[1]) for out in outs
        ],
        grid_spec=pltpu.PrefetchScalarGridSpec(
            num_scalar_prefetch=1,
            grid=grid,
            in_specs=specs,
            out_specs=out_specs,
            scratch_shapes=list(scratch),
        ),
        compiler_params=pltpu.CompilerParams(
            vmem_limit_bytes=VMEM_LIMIT, dimension_semantics=("arbitrary",) * len(grid)
        ),
        cost_estimate=pl.CostEstimate(flops=flops, bytes_accessed=moved, transcendentals=0),
    )(place, *[array for array, _, _ in ins])


def whole(array):
    rank = array.ndim
    return (array, array.shape, lambda *_: (0,) * rank)


def whole_out(shape, dtype):
    rank = len(shape)
    return (shape, dtype, shape, lambda *_: (0,) * rank)


def kept_in_hbm(out):
    return out + (True,)


def rows(array):
    return (array, (BLOCK, array.shape[1]), lambda m, _: (m, 0))


def rows_out(width, dtype):
    return ((TOKENS, width), dtype, (BLOCK, width), lambda m, _: (m, 0))


def lanes(array):
    lead = array.shape[:-1]
    rank = len(lead)
    return (array, lead + (BLOCK,), lambda m, _: (0,) * rank + (m,))


def lanes_out(lead, dtype):
    rank = len(lead)
    return (lead + (TOKENS,), dtype, lead + (BLOCK,), lambda m, _: (0,) * rank + (m,))


def by_micro(array):
    rank = array.ndim - 1
    return (array, (1,) + array.shape[1:], lambda m, _: (m,) + (0,) * rank)


def by_micro_out(shape, dtype):
    rank = len(shape) - 1
    return (shape, dtype, (1,) + shape[1:], lambda m, _: (m,) + (0,) * rank)


def pack_body(place, qkv, proj, up, down, mine, other, held):
    low = lax.broadcasted_iota(jnp.int32, (32, 128), 1) < 64
    for half in range(2):
        for pair in range(8):
            first = up[:, 256 * pair : 256 * pair + 128].astype(F32)
            second = up[:, 256 * pair + 128 : 256 * pair + 256].astype(F32)
            if half == 0:
                cut = jnp.where(low, first, pltpu.roll(second, 64, 1))
            else:
                cut = jnp.where(low, pltpu.roll(first, 64, 1), second)
            at = 128 * (pair % 2)
            held[half, 32 * (pair // 2) : 32 * (pair // 2) + 32, at : at + 128] = cut.astype(BF)
        for side in range(2):
            held[half, 128 + 64 * side : 192 + 64 * side, :] = down[
                64 * half : 64 * half + 64, 256 * side : 256 * side + 256
            ]
            held[half, 256 + 32 * side : 288 + 32 * side, :] = proj[
                :, 256 * side : 256 * side + 256
            ]
        for part in range(3):
            at = 512 * part + 256 * half
            held[half, 320 + 32 * part : 352 + 32 * part, :] = qkv[:, at : at + 256]
    core = place[1]
    mine[...] = held[core]
    other[...] = held[1 - core]


def pack_weights(place, qkv, proj, up, down):
    return call(
        pack_body,
        place,
        (1,),
        [whole(qkv), whole(proj), whole(up), whole(down)],
        [whole_out((416, 256), BF), whole_out((416, 256), BF)],
        [pltpu.VMEM((2, 416, 256), BF)],
    )


def sort_body(place, mine, received, norms, early, middle, late):
    first = place[1] == 0
    kept = mine[...]
    came = received[...]
    layer0 = jnp.where(first, kept, came)
    layer1 = jnp.where(first, came, kept)
    early[0:96, :] = layer0[320:416]
    early[96:112, :] = norms[...]
    middle[0:320, :] = layer0[0:320]
    middle[320:480, :] = layer1[256:416]
    late[...] = layer1[0:256]


def sort_weights(place, mine, received, norms):
    return call(
        sort_body,
        place,
        (1,),
        [whole(mine), whole(received), whole(norms)],
        [whole_out((depth, 256), BF) for depth in (112, 480, 256)],
    )


def shift_z(value, step):
    return lax.ppermute(value, "seq", [(z, (z + step) % 4) for z in range(4)])


def swap_core(value):
    return lax.ppermute(value, "section", [(0, 1), (1, 0)])


def gather_now(value):
    copies = jnp.broadcast_to(value, (16,) + value.shape)
    return lax.all_to_all(copies, "shard", 0, 0, tiled=True)


def after(value, *others):
    return lax.optimization_barrier((value, others))[0]


def regroup(values):
    got = {0: values[0]}
    for step in (1, 3, 2):
        got[step] = shift_z(values[step], step)
    return [got[step] for step in SHIFTS]


def unit_of(states):
    centre = states - jnp.mean(states, axis=-1, keepdims=True)
    scaled = lax.rsqrt(jnp.mean(centre * centre, axis=-1, keepdims=True) + NORM_EPS)
    return centre * scaled, scaled


def qkv_rows(weights):
    array, first = weights
    return [
        (array, (16, 32, 256), functools.partial(lambda at, m, _: (0, at, 0), first + part))
        for part in range(3)
    ]


def proj_rows(weights):
    array, first = weights
    return (array, (8, 64, 256), lambda m, place: (place[1], first, 0))


def put_heads_grad(grad, proj, held, first):
    weight = proj[...]
    total = dims(weight[:, 0:32].reshape(256, 256), grad[:, 0:256], 1, 1) + dims(
        weight[:, 32:64].reshape(256, 256), grad[:, 256:512], 1, 1
    )
    for head in range(4):
        held[head, first : first + 64, :] = total[64 * head : 64 * head + 64].astype(BF)


def before_body(second, place, *refs):
    refs = list(refs)
    states = refs.pop(0)[...].astype(F32)
    if second:
        part_a, part_b, grad, proj = [refs.pop(0) for _ in range(4)]
        states = (states + (part_a[...] + part_b[...])).astype(BF)
    wq, wk, wv, norms, turns = refs[:5]
    outs = refs[5:9]
    attn_ref, mlp_ref = refs[9:11]
    held = refs[-1]
    if second:
        refs[11][...] = states
        states = states.astype(F32)
    unit, _ = unit_of(states)
    attn_in = (unit * norms[0:1, :] + norms[2:3, :]).astype(BF)
    attn_ref[...] = attn_in
    mlp_ref[...] = (unit * norms[1:2, :] + norms[3:4, :]).astype(BF)
    cosine, sine = turns[0], turns[1]
    for part, weight in enumerate((wq, wk, wv)):
        mixed = dims(weight[...].reshape(D, 256), attn_in, 0, 1)
        for head in range(4):
            block = mixed[64 * head : 64 * head + 64]
            if part < 2:
                a, b = block[0:8], block[8:16]
                block = jnp.concatenate(
                    [a * cosine - b * sine, b * cosine + a * sine, block[16:]], axis=0
                )
            if part == 0:
                block = block * 0.125
            held[head, 64 * part : 64 * part + 64, :] = block.astype(BF)
    if second:
        put_heads_grad(grad, proj, held, 192)
    for step in SHIFTS:
        outs[step][...] = held[lax.rem(place[0] + step, 4)]


def before_layer(place, states, extra, weights, norms, turns):
    array, first = weights
    ins = [rows(states)]
    depth = 192
    if extra:
        parts, grad, proj = extra
        ins += [rows(parts[0]), rows(parts[1]), rows(grad), proj_rows(proj)]
        depth = 256
    ins += qkv_rows(weights)
    ins += [whole(norms), lanes(turns)]
    outs = [lanes_out((depth,), BF) for _ in SHIFTS]
    outs += [kept_in_hbm(rows_out(D, BF)), kept_in_hbm(rows_out(D, BF))]
    if extra:
        outs.append(kept_in_hbm(rows_out(D, BF)))
    return call(
        functools.partial(before_body, bool(extra)),
        place,
        (MICRO,),
        ins,
        outs,
        [pltpu.VMEM((4, depth, BLOCK), BF)],
        flops=1_200_000_000,
        moved=6_000_000,
    )


def mlp_body(place, mlp_in, up, down, out, active_ref, slope_ref):
    step = pl.program_id(0)
    hidden = jnp.dot(mlp_in[...], up[...].reshape(D, 256), preferred_element_type=F32)
    cdf = 0.5 * (1.0 + lax.erf(hidden * 0.7071067811865476))
    pdf = jnp.exp(-0.5 * hidden * hidden) * 0.3989422804014327
    active = (hidden * cdf).astype(BF)
    active_ref[...] = active
    slope_ref[...] = cdf + hidden * pdf
    lower = down[...]
    both = jnp.concatenate(
        [lower[:, 0:64].reshape(256, 256), lower[:, 64:128].reshape(256, 256)], axis=1
    )
    product = jnp.dot(active, both, preferred_element_type=F32)

    @pl.when(step == 0)
    def _():
        out[...] = product

    @pl.when(step > 0)
    def _():
        out[...] += product


def mlp_layer(place, mlp_in, weights):
    return call(
        mlp_body,
        place,
        (4,),
        [
            whole(mlp_in),
            (weights, (16, 32, 256), lambda b, _: (0, b, 0)),
            (weights, (4, 128, 256), lambda b, _: (b, 1, 0)),
        ],
        [
            whole_out((TOKENS, D), F32),
            kept_in_hbm(((TOKENS, 1024), BF, (TOKENS, 256), lambda b, _: (0, b))),
            kept_in_hbm(((TOKENS, 1024), F32, (TOKENS, 256), lambda b, _: (0, b))),
        ],
        flops=6_000_000_000,
        moved=12_000_000,
    )


def put_starts(place, places, starts):
    along = lax.broadcasted_iota(jnp.int32, (1, BLOCK), 1)
    for step in SHIFTS:
        source = lax.rem(place[0] - step + 4, 4)
        starts[source] = along + BLOCK * source - places[step][...]


def allowed_keys(starts, query_block, key_block):
    keys = lax.broadcasted_iota(jnp.int32, (BLOCK, BLOCK), 0) + BLOCK * key_block
    allowed = keys >= starts[query_block]
    if query_block == key_block:
        queries = lax.broadcasted_iota(jnp.int32, (BLOCK, BLOCK), 1) + BLOCK * query_block
        allowed = allowed & (keys <= queries)
    return allowed


def attend_body(place, *refs):
    came, places = refs[0:4], refs[4:8]
    outs = refs[8:12]
    kept, heads_out, log_total = refs[12:15]
    starts, keys = refs[15:17]
    for step in SHIFTS:
        source = lax.rem(place[0] - step + 4, 4)
        kept[0, source] = came[step][...]
    put_starts(place, places, starts)
    for j in range(4):
        keys[j] = kept[0, j, 64:128].T
    for i in range(4):
        query = kept[0, i, 0:64]
        scores = []
        for j in range(i + 1):
            raw = jnp.dot(keys[j], query, preferred_element_type=F32)
            scores.append(jnp.where(allowed_keys(starts, i, j), raw, MASKED))
        peak = functools.reduce(
            jnp.maximum, [jnp.max(s, axis=0, keepdims=True) for s in scores]
        )
        total = jnp.zeros((1, BLOCK), F32)
        acc = jnp.zeros((HEAD, BLOCK), F32)
        for j in range(i + 1):
            probs = jnp.exp(scores[j] - peak)
            total = total + jnp.sum(probs, axis=0, keepdims=True)
            acc = acc + jnp.dot(
                kept[0, j, 128:192], probs.astype(BF), preferred_element_type=F32
            )
        heads_out[0, i] = (acc / total).astype(BF)
        log_total[0, i] = peak + jnp.log(total)
    for step in SHIFTS:
        outs[step][...] = heads_out[0, lax.rem(place[0] + step, 4)]


def attend(place, came, places):
    return call(
        attend_body,
        place,
        (MICRO,),
        [lanes(piece) for piece in came] + [lanes(piece) for piece in places],
        [lanes_out((HEAD,), BF) for _ in SHIFTS]
        + [
            kept_in_hbm(by_micro_out((MICRO, 4, 192, BLOCK), BF)),
            kept_in_hbm(by_micro_out((MICRO, 4, HEAD, BLOCK), BF)),
            kept_in_hbm(by_micro_out((MICRO, 4, 1, BLOCK), F32)),
        ],
        [pltpu.VMEM((4, 1, BLOCK), jnp.int32), pltpu.VMEM((4, BLOCK, HEAD), BF)],
        flops=8_000_000_000,
        moved=4_000_000,
    )


def after_body(place, *refs):
    came = refs[0:4]
    proj, mlp_out, out, heads = refs[4:8]
    for step in SHIFTS:
        source = lax.rem(place[0] - step + 4, 4)
        at = pl.multiple_of(source * HEAD, HEAD)
        heads[pl.ds(at, HEAD), :] = came[step][...]
    held = heads[...]
    weight = proj[...]
    for side in range(2):
        span = slice(256 * side, 256 * side + 256)
        product = dims(held, weight[:, 32 * side : 32 * side + 32].reshape(256, 256), 0, 0)
        out[:, span] = mlp_out[:, span] + product


def after_layer(place, came, first, proj, mlp_out):
    return call(
        after_body,
        place,
        (MICRO,),
        [(piece, (HEAD, BLOCK), lambda m, _: (first, m)) for piece in came]
        + [proj_rows(proj), rows(mlp_out)],
        [rows_out(D, F32), lanes_out((256,), BF)],
        flops=800_000_000,
        moved=4_000_000,
    )


def heads_grad_body(place, grad, proj, *refs):
    outs, held = refs[0:4], refs[4]
    put_heads_grad(grad, proj, held, 0)
    for step in SHIFTS:
        outs[step][...] = held[lax.rem(place[0] + step, 4)]


def heads_grad(place, grad, proj):
    return call(
        heads_grad_body,
        place,
        (MICRO,),
        [rows(grad), proj_rows(proj)],
        [lanes_out((HEAD,), BF) for _ in SHIFTS],
        [pltpu.VMEM((4, HEAD, BLOCK), BF)],
        flops=800_000_000,
        moved=2_000_000,
    )


def put_proj(core, heads, grad, pack, first):
    product = jnp.dot(heads[...], grad[...], preferred_element_type=F32).astype(BF)
    for side in range(2):
        span = pl.ds(first + 32 * side, 32)
        part = product[:, 256 * side : 256 * side + 256].reshape(8, 32, 256)
        pack[pl.ds(8 * core, 8), span, :] = part
        pack[pl.ds(8 - 8 * core, 8), span, :] = jnp.zeros_like(part)


def mlp_back_body(with_proj, place, grad, active, slope, mlp_in, up, down, *refs):
    out, pack = refs[-2:]
    step = pl.program_id(0)
    lower = down[...]
    both = jnp.concatenate(
        [lower[:, 0:64].reshape(256, 256), lower[:, 64:128].reshape(256, 256)], axis=1
    )
    active_grad = dims(grad[...], both, 1, 1)
    hidden_grad = (active_grad * slope[...]).astype(BF)
    product = dims(hidden_grad, up[...].reshape(D, 256), 1, 1)

    @pl.when(step == 0)
    def _():
        out[...] = product
        if with_proj:
            put_proj(place[1], refs[0], grad, pack, 256)

    @pl.when(step > 0)
    def _():
        out[...] += product

    up_part = dims(mlp_in[...], hidden_grad, 0, 0).astype(BF).reshape(16, 32, 256)
    pack[:, pl.ds(pl.multiple_of(32 * step, 32), 32), :] = up_part
    down_part = dims(active[...], grad[...], 0, 0).astype(BF)
    for side in range(2):
        pack[pl.ds(4 * step, 4), 128 + 64 * side : 192 + 64 * side, :] = down_part[
            :, 256 * side : 256 * side + 256
        ].reshape(4, 64, 256)


def mlp_back(place, grad, active, slope, mlp_in, weights, heads=None):
    ins = [
        whole(grad),
        (active, (TOKENS, 256), lambda b, _: (0, b)),
        (slope, (TOKENS, 256), lambda b, _: (0, b)),
        whole(mlp_in),
        (weights, (16, 32, 256), lambda b, _: (0, b, 0)),
        (weights, (4, 128, 256), lambda b, _: (b, 1, 0)),
    ]
    depth = 256
    if heads is not None:
        ins.append(whole(heads))
        depth = 320
    return call(
        functools.partial(mlp_back_body, heads is not None),
        place,
        (4,),
        ins,
        [whole_out((TOKENS, D), F32), whole_out((16, depth, 256), BF)],
        flops=8_000_000_000,
        moved=14_000_000,
    )


def attend_back_body(place, *refs):
    came, places = refs[0:4], refs[4:8]
    kept_ref, heads_out, log_total = refs[8:11]
    outs = refs[11:15]
    starts, keys, values, grads, acc = refs[15:20]
    for step in SHIFTS:
        source = lax.rem(place[0] - step + 4, 4)
        grads[source] = came[step][...]
    put_starts(place, places, starts)
    acc[...] = jnp.zeros_like(acc)
    for j in range(4):
        keys[j] = kept_ref[0, j, 64:128].T
        values[j] = kept_ref[0, j, 128:192].T
    for i in range(4):
        query = kept_ref[0, i, 0:64]
        grad = grads[i]
        log_row = log_total[0, i]
        centre = jnp.sum(
            grad.astype(F32) * heads_out[0, i].astype(F32), axis=0, keepdims=True
        )
        query_grad = jnp.zeros((HEAD, BLOCK), F32)
        for j in range(i + 1):
            raw = jnp.dot(keys[j], query, preferred_element_type=F32)
            probs = jnp.where(allowed_keys(starts, i, j), jnp.exp(raw - log_row), 0.0)
            probs_grad = jnp.dot(values[j], grad, preferred_element_type=F32)
            scores_grad = (probs * (probs_grad - centre)).astype(BF)
            acc[j, 128:192, :] += dims(grad, probs.astype(BF), 1, 1)
            acc[j, 64:128, :] += dims(query, scores_grad, 1, 1)
            query_grad = query_grad + jnp.dot(
                kept_ref[0, j, 64:128], scores_grad, preferred_element_type=F32
            )
        acc[i, 0:64, :] = query_grad * 0.125
    for step in SHIFTS:
        outs[step][...] = acc[lax.rem(place[0] + step, 4)].astype(BF)


def attend_back(place, came, places, kept, heads_out, log_total):
    return call(
        attend_back_body,
        place,
        (MICRO,),
        [lanes(piece) for piece in came]
        + [lanes(piece) for piece in places]
        + [by_micro(kept), by_micro(heads_out), by_micro(log_total)],
        [lanes_out((192,), BF) for _ in SHIFTS],
        [
            pltpu.VMEM((4, 1, BLOCK), jnp.int32),
            pltpu.VMEM((4, BLOCK, HEAD), BF),
            pltpu.VMEM((4, BLOCK, HEAD), BF),
            pltpu.VMEM((4, HEAD, BLOCK), BF),
            pltpu.VMEM((4, 192, BLOCK), F32),
        ],
        flops=16_000_000_000,
        moved=5_000_000,
    )


def attend_both_body(place, *refs):
    came, places, outs = refs[0:4], refs[4:8], refs[8:12]
    starts, kept, keys, values, acc, out = refs[12:18]
    for step in SHIFTS:
        source = lax.rem(place[0] - step + 4, 4)
        kept[source] = came[step][...]
    put_starts(place, places, starts)
    acc[...] = jnp.zeros_like(acc)
    for j in range(4):
        keys[j] = kept[j, 64:128].T
        values[j] = kept[j, 128:192].T
    for i in range(4):
        query = kept[i, 0:64]
        grad = kept[i, 192:256]
        scores = []
        for j in range(i + 1):
            raw = jnp.dot(keys[j], query, preferred_element_type=F32)
            scores.append(jnp.where(allowed_keys(starts, i, j), raw, MASKED))
        peak = functools.reduce(
            jnp.maximum, [jnp.max(s, axis=0, keepdims=True) for s in scores]
        )
        exps = [jnp.exp(s - peak) for s in scores]
        total = functools.reduce(jnp.add, [jnp.sum(e, axis=0, keepdims=True) for e in exps])
        inverse = 1.0 / total
        result = jnp.zeros((HEAD, BLOCK), F32)
        probs = []
        for j in range(i + 1):
            prob = exps[j] * inverse
            low = prob.astype(BF)
            probs.append(prob)
            result = result + jnp.dot(kept[j, 128:192], low, preferred_element_type=F32)
            acc[j, 128:192, :] += dims(grad, low, 1, 1)
        out[i] = result.astype(BF)
        centre = jnp.sum(grad.astype(F32) * result, axis=0, keepdims=True)
        query_grad = jnp.zeros((HEAD, BLOCK), F32)
        for j in range(i + 1):
            probs_grad = jnp.dot(values[j], grad, preferred_element_type=F32)
            scores_grad = (probs[j] * (probs_grad - centre)).astype(BF)
            acc[j, 64:128, :] += dims(query, scores_grad, 1, 1)
            query_grad = query_grad + jnp.dot(
                kept[j, 64:128], scores_grad, preferred_element_type=F32
            )
        acc[i, 0:64, :] = query_grad * 0.125
    for step in SHIFTS:
        other = lax.rem(place[0] + step, 4)
        outs[step][0:192, :] = acc[other].astype(BF)
        outs[step][192:256, :] = out[other]


def attend_both(place, came, places):
    return call(
        attend_both_body,
        place,
        (MICRO,),
        [lanes(piece) for piece in came] + [lanes(piece) for piece in places],
        [lanes_out((256,), BF) for _ in SHIFTS],
        [
            pltpu.VMEM((4, 1, BLOCK), jnp.int32),
            pltpu.VMEM((4, 256, BLOCK), BF),
            pltpu.VMEM((4, BLOCK, HEAD), BF),
            pltpu.VMEM((4, BLOCK, HEAD), BF),
            pltpu.VMEM((4, 192, BLOCK), F32),
            pltpu.VMEM((4, HEAD, BLOCK), BF),
        ],
        flops=18_000_000_000,
        moved=5_000_000,
    )


def mixed_back_body(place, *refs):
    came = refs[0:4]
    wq, wk, wv, norms, turns, states, mlp_grad = refs[4:11]
    out, mixed_ref, sums = refs[11:14]
    cosine, sine = turns[0], turns[1]
    for step in SHIFTS:
        head = lax.rem(place[0] - step + 4, 4)
        at = pl.multiple_of(head * HEAD, HEAD)
        for part in range(3):
            block = came[step][64 * part : 64 * part + 64]
            if part < 2:
                a, b = block[0:8].astype(F32), block[8:16].astype(F32)
                turned = jnp.concatenate(
                    [a * cosine + b * sine, b * cosine - a * sine], axis=0
                ).astype(BF)
                block = jnp.concatenate([turned, block[16:]], axis=0)
            mixed_ref[part, pl.ds(at, HEAD), :] = block
    attn_grad = jnp.zeros((BLOCK, D), F32)
    for part, weight in enumerate((wq, wk, wv)):
        attn_grad = attn_grad + dims(mixed_ref[part], weight[...].reshape(D, 256), 0, 1)
    unit, _ = unit_of(states[...].astype(F32))
    other_grad = mlp_grad[...]
    out[...] = attn_grad * norms[0:1, :] + other_grad * norms[1:2, :]

    @pl.when(pl.program_id(0) == 0)
    def _():
        sums[...] = jnp.zeros_like(sums)

    sums[0:1, :] += jnp.sum(attn_grad * unit, axis=0, keepdims=True)
    sums[1:2, :] += jnp.sum(other_grad * unit, axis=0, keepdims=True)
    sums[2:3, :] += jnp.sum(attn_grad, axis=0, keepdims=True)
    sums[3:4, :] += jnp.sum(other_grad, axis=0, keepdims=True)


def mixed_back(place, came, weights, norms, turns, states, mlp_grad):
    ins = [(piece, (192, BLOCK), lambda m, _: (0, m)) for piece in came]
    ins += qkv_rows(weights)
    ins += [whole(norms), lanes(turns), rows(states), rows(mlp_grad)]
    return call(
        mixed_back_body,
        place,
        (MICRO,),
        ins,
        [
            rows_out(D, F32),
            lanes_out((3, 256), BF),
            whole_out((8, D), F32),
        ],
        flops=1_500_000_000,
        moved=6_000_000,
    )


def weight_back_body(with_rest, place, attn_in, mixed, sums, *refs):
    pack = refs[-1]
    first = 0
    if with_rest:
        rest, heads, grad = refs[:3]
        pack[:, 0:256, :] = rest[...]
        put_proj(place[1], heads, grad, pack, 256)
        first = 320
    for part in range(3):
        product = dims(attn_in[...], mixed[part], 0, 1)
        at = first + 32 * part
        pack[:, at : at + 32, :] = product.astype(BF).reshape(16, 32, 256)
    at = first + 96
    pack[:, at : at + 16, :] = jnp.zeros((16, 16, 256), BF)
    for owner in range(16):
        tile, shift = owner // 4, owner % 4 * 32
        lines = sums[:, 128 * tile : 128 * tile + 128]
        if shift:
            lines = pltpu.roll(lines, 128 - shift, 1)
        lines = jnp.concatenate([lines, jnp.zeros_like(lines)], axis=0).astype(BF)
        pack[owner, at : at + 16, 0:128] = lines


def weight_back(place, attn_in, mixed, sums, rest=()):
    return call(
        functools.partial(weight_back_body, bool(rest)),
        place,
        (1,),
        [whole(attn_in), whole(mixed), whole(sums)] + [whole(array) for array in rest],
        [whole_out((16, 432 if rest else 112, 256), BF)],
        flops=2_000_000_000,
        moved=6_000_000,
    )[0]


def end_body(place, states, grad, own, came, out):
    unit, scaled = unit_of(states[...].astype(F32))
    through = own[...] + came[...]
    back = scaled * (
        through
        - jnp.mean(through, axis=-1, keepdims=True)
        - unit * jnp.mean(through * unit, axis=-1, keepdims=True)
    )
    out[...] = (grad[...].astype(F32) + back).astype(BF)


def end_back(place, states, grad, own, came):
    return call(
        end_body,
        place,
        (MICRO,),
        [rows(states), rows(grad), rows(own), rows(came)],
        [rows_out(D, BF)],
        flops=100_000_000,
        moved=5_000_000,
    )[0]


def scatter_sum(pack):
    got = lax.all_to_all(pack, "shard", 0, 0, tiled=True)
    return jnp.sum(got.astype(F32), axis=0).astype(BF)


def choose_body(place, *refs):
    keep, send = refs[12:14]
    total = []
    for group in range(3):
        held = refs[4 * group][...].astype(F32)
        for step in range(1, 4):
            held = held + refs[4 * group + step][...].astype(F32)
        total.append(held)
    layer1 = total[0]
    layer0 = jnp.concatenate([total[1], total[2]], axis=0)
    first = place[1] == 0
    keep[...] = jnp.where(first, layer0, layer1)
    send[...] = jnp.where(first, layer1, layer0).astype(BF)


def choose(place, pieces):
    return call(
        choose_body,
        place,
        (1,),
        [whole(piece) for piece in pieces],
        [whole_out((432, 256), F32), whole_out((432, 256), BF)],
    )


def unpack_body(place, keep, got, qkv, proj, up, down, sums, total):
    core = place[1]
    total[core] = keep[...]
    total[1 - core] = got[...].astype(F32)
    low = lax.broadcasted_iota(jnp.int32, (32, 128), 1) < 64
    sums[...] = total[0, 416:424, 0:128] + total[1, 416:424, 0:128]
    for half in range(2):
        for part in range(3):
            at = 512 * part + 256 * half
            qkv[:, at : at + 256] = total[half, 320 + 32 * part : 352 + 32 * part]
        at = 256 + 32 * half
        proj[:, 256 * half : 256 * half + 256] = total[0, at : at + 32] + total[1, at : at + 32]
        for side in range(2):
            down[64 * half : 64 * half + 64, 256 * side : 256 * side + 256] = total[
                half, 128 + 64 * side : 192 + 64 * side
            ]
    for tile in range(16):
        row = 32 * (tile // 4)
        at = 128 * (tile % 4 // 2)
        left = total[0, row : row + 32, at : at + 128]
        right = total[1, row : row + 32, at : at + 128]
        if tile % 2 == 0:
            joined = jnp.where(low, left, pltpu.roll(right, 64, 1))
        else:
            joined = jnp.where(low, pltpu.roll(left, 64, 1), right)
        up[:, 128 * tile : 128 * tile + 128] = joined


def unpack(place, keep, got):
    return call(
        unpack_body,
        place,
        (1,),
        [whole(keep), whole(got)],
        [
            whole_out((32, 1536), F32),
            whole_out((32, 512), F32),
            whole_out((32, 2048), F32),
            whole_out((128, 512), F32),
            whole_out((8, 128), F32),
        ],
        [pltpu.VMEM((2, 432, 256), F32)],
    )


def on_device(
    inputs,
    positions,
    cotangent,
    qkv_weight,
    proj_weight,
    up_weight,
    down_weight,
    norm_gain,
    norm_bias,
):
    core = lax.axis_index("section")
    chip_z = lax.axis_index("seq")
    shard = lax.axis_index("shard")
    first = core == 0
    place = jnp.stack([chip_z, core, shard // 4, shard % 4]).astype(jnp.int32)

    mine, other = pack_weights(
        place, qkv_weight[0], proj_weight[0], up_weight[0], down_weight[0]
    )
    own_norms = jnp.concatenate([norm_gain[0], norm_bias[0]], axis=0).reshape(1, 128)
    other_norms = swap_core(jnp.broadcast_to(own_norms, (16, 128)))[0:1]
    both_norms = jnp.where(
        first,
        jnp.concatenate([own_norms, other_norms], axis=1),
        jnp.concatenate([other_norms, own_norms], axis=1),
    )
    early, middle, late = sort_weights(
        place, mine, swap_core(other), jnp.broadcast_to(both_norms, (16, 256))
    )
    places_row = positions.reshape(1, TOKENS)
    gathered, places = lax.optimization_barrier(
        (gather_now(early), regroup([places_row] * 4))
    )
    middle_all = lax.all_gather(middle, "shard")
    late_all = lax.all_gather(late, "shard")
    norms = (
        gathered[:, 96, :]
        .reshape(16, 2, 4, 32)
        .transpose(1, 2, 0, 3)
        .reshape(2, 4, D)
        .astype(F32)
    )
    qkv_of = ((gathered, 0), (middle_all, 12))
    proj_of = ((middle_all, 4), (middle_all, 5))
    mlp_of = (middle_all, late_all)
    rates = 10000.0 ** (-jnp.arange(ROT // 2, dtype=F32) * 2.0 / ROT)
    angles = rates[:, None] * places_row.astype(F32)
    turns = jnp.stack([jnp.cos(angles), jnp.sin(angles)])

    states = inputs.reshape(TOKENS, D)
    grad = cotangent.reshape(TOKENS, D)
    extra = ()
    saved = []
    for layer in range(2):
        done = before_layer(place, states, extra, qkv_of[layer], norms[layer], turns)
        sent, attn_in, mlp_in = done[0:4], done[4], done[5]
        if layer == 1:
            states = done[6]
        came = regroup(sent)
        if layer == 1:
            sent = attend_both(place, came, places)
            mlp_in = after(mlp_in, sent)
            came = regroup(sent)
        mlp_out, active, slope = mlp_layer(place, mlp_in, mlp_of[layer])
        if layer == 0:
            done = attend(place, came, places)
            kept, heads_out, log_total = done[4:7]
            came = regroup(done[0:4])
        part, heads = after_layer(place, came, 3 * layer, proj_of[layer], mlp_out)
        parts = (part, swap_core(part))
        extra = (parts, grad, proj_of[1])
        saved.append((states, attn_in, mlp_in, active, slope, heads))
    result = (states.astype(F32) + (parts[0] + parts[1])).astype(BF)
    layer_out = jnp.where(first, saved[1][0], result)

    grads = [None, None]
    for layer in (1, 0):
        states, attn_in, mlp_in, active, slope, heads = saved[layer]
        if layer == 1:
            mlp_grad, pack = mlp_back(place, grad, active, slope, mlp_in, mlp_of[1])
        else:
            sent = heads_grad(place, grad, proj_of[0])
            came = regroup(sent)
            mlp_grad, pack = mlp_back(
                place, after(grad, sent), active, slope, mlp_in, mlp_of[0], heads
            )
            came = after(came, pack)
            sent = attend_back(place, came, places, kept, heads_out, log_total)
            sum_a = scatter_sum(pack)
            came = regroup(sent)
        through, mixed, norm_sums = mixed_back(
            place, came, qkv_of[layer], norms[layer], turns, states, mlp_grad
        )
        if layer == 1:
            pack = weight_back(place, attn_in, mixed, norm_sums, (pack, heads, grad))
            total = lax.psum_scatter(pack, "shard", scatter_dimension=0, tiled=False)
            through = after(through, pack)
        else:
            pack, sum_a = lax.optimization_barrier(
                (weight_back(place, attn_in, mixed, norm_sums), sum_a)
            )
            pieces_a = regroup([sum_a] * 4)
            pieces_b = regroup([scatter_sum(pack)] * 4)
        grad = end_back(place, states, grad, through, swap_core(through))
        grads[layer] = grad
    grads_out = jnp.where(first, grads[0], grads[1])

    keep, send = choose(place, regroup([total] * 4) + pieces_a + pieces_b)
    qkv_grad, proj_grad, up_grad, down_grad, norm_sums = unpack(place, keep, swap_core(send))
    return (
        layer_out.reshape(1, MICRO, 1, BLOCK, D),
        grads_out.reshape(1, MICRO, 1, BLOCK, D),
        qkv_grad[None],
        proj_grad[None],
        up_grad[None],
        down_grad[None],
        norm_sums[None, 0:2, 0:32],
        norm_sums[None, 2:4, 0:32],
    )


def solution(mesh):
    placed = (
        P(None, "shard", "seq", None),
        P(None, "shard", "seq"),
        P(None, "shard", "seq", None),
        P("section", "shard", None),
        P("section", "shard", None),
        P("section", "shard", None),
        P("section", "shard", None),
        P("section", None, "shard"),
        P("section", None, "shard"),
    )
    return jax.shard_map(
        on_device,
        mesh=mesh,
        in_specs=placed,
        out_specs=(
            P("section", None, "shard", "seq", None),
            P("section", None, "shard", "seq", None),
            P("section", "shard", None),
            P("section", "shard", None),
            P("section", "shard", None),
            P("section", "shard", None),
            P("section", None, "shard"),
            P("section", None, "shard"),
        ),
        check_vma=False,
    )
```

```python
import functools

import jax
import jax.numpy as jnp
from jax import lax
from jax.experimental import pallas as pl
from jax.experimental.pallas import tpu as pltpu
from jax.sharding import PartitionSpec as P

D = 512
HEADS = 8
HEAD = 64
ROT = 16
MICRO = 3
BLOCK = 256
TOKENS = MICRO * BLOCK
NORM_EPS = 1e-05
MASKED = -1e30
BF = jnp.bfloat16
F32 = jnp.float32
SHIFTS = (0, 1, 2, 3)
VMEM_LIMIT = 24 * 1024 * 1024


def dims(left, right, left_dim, right_dim):
    return lax.dot_general(
        left, right, (((left_dim,), (right_dim,)), ((), ())), preferred_element_type=F32
    )


def struct(shape, dtype):
    return jax.ShapeDtypeStruct(shape, dtype)


def in_hbm(array):
    return pltpu.with_memory_space_constraint(array, pltpu.HBM)


def call(body, place, grid, ins, outs, scratch=(), flops=10**9, moved=4 * 10**6):
    specs = [pl.BlockSpec(block, index) for _, block, index in ins]
    out_specs = [pl.BlockSpec(out[2], out[3]) for out in outs]
    return pl.pallas_call(
        body,
        out_shape=[
            (pltpu.HBM if out[4:] else struct)(out[0], out[1]) for out in outs
        ],
        grid_spec=pltpu.PrefetchScalarGridSpec(
            num_scalar_prefetch=1,
            grid=grid,
            in_specs=specs,
            out_specs=out_specs,
            scratch_shapes=list(scratch),
        ),
        compiler_params=pltpu.CompilerParams(
            vmem_limit_bytes=VMEM_LIMIT, dimension_semantics=("arbitrary",) * len(grid)
        ),
        cost_estimate=pl.CostEstimate(flops=flops, bytes_accessed=moved, transcendentals=0),
    )(place, *[array for array, _, _ in ins])


def whole(array):
    rank = array.ndim
    return (array, array.shape, lambda *_: (0,) * rank)


def whole_out(shape, dtype):
    rank = len(shape)
    return (shape, dtype, shape, lambda *_: (0,) * rank)


def kept_in_hbm(out):
    return out + (True,)


def rows(array):
    return (array, (BLOCK, array.shape[1]), lambda m, _: (m, 0))


def rows_out(width, dtype):
    return ((TOKENS, width), dtype, (BLOCK, width), lambda m, _: (m, 0))


def lanes(array):
    lead = array.shape[:-1]
    rank = len(lead)
    return (array, lead + (BLOCK,), lambda m, _: (0,) * rank + (m,))


def lanes_out(lead, dtype):
    rank = len(lead)
    return (lead + (TOKENS,), dtype, lead + (BLOCK,), lambda m, _: (0,) * rank + (m,))


def by_micro(array):
    rank = array.ndim - 1
    return (array, (1,) + array.shape[1:], lambda m, _: (m,) + (0,) * rank)


def by_micro_out(shape, dtype):
    rank = len(shape) - 1
    return (shape, dtype, (1,) + shape[1:], lambda m, _: (m,) + (0,) * rank)


def pack_body(place, qkv, proj, up, down, norms, mine, other, held):
    low = lax.broadcasted_iota(jnp.int32, (32, 128), 1) < 64
    for half in range(2):
        for pair in range(8):
            first = up[:, 256 * pair : 256 * pair + 128].astype(F32)
            second = up[:, 256 * pair + 128 : 256 * pair + 256].astype(F32)
            if half == 0:
                cut = jnp.where(low, first, pltpu.roll(second, 64, 1))
            else:
                cut = jnp.where(low, pltpu.roll(first, 64, 1), second)
            at = 128 * (pair % 2)
            held[half, 32 * (pair // 2) : 32 * (pair // 2) + 32, at : at + 128] = cut.astype(BF)
        for side in range(2):
            held[half, 128 + 64 * side : 192 + 64 * side, :] = down[
                64 * half : 64 * half + 64, 256 * side : 256 * side + 256
            ]
            held[half, 256 + 32 * side : 288 + 32 * side, :] = proj[
                :, 256 * side : 256 * side + 256
            ]
        for part in range(3):
            at = 512 * part + 256 * half
            held[half, 320 + 32 * part : 352 + 32 * part, :] = qkv[:, at : at + 256]
        held[half, 416:432, 0:128] = norms[...]
        held[half, 416:432, 128:256] = norms[...]
    core = place[1]
    mine[...] = held[core]
    other[...] = held[1 - core]


def pack_weights(place, qkv, proj, up, down, norms):
    return call(
        pack_body,
        place,
        (1,),
        [whole(qkv), whole(proj), whole(up), whole(down), whole(norms)],
        [whole_out((432, 256), BF), whole_out((432, 256), BF)],
        [pltpu.VMEM((2, 432, 256), BF)],
    )


def sort_body(place, mine, received, early, middle, late):
    first = place[1] == 0
    kept = mine[...]
    came = received[...]
    layer0 = jnp.where(first, kept, came)
    layer1 = jnp.where(first, came, kept)
    norms = jnp.concatenate([layer0[416:432, 0:128], layer1[416:432, 0:128]], axis=1)
    for peer in range(16):
        early[peer, 0:96, :] = layer0[320:416]
        early[peer, 96:112, :] = norms
    middle[0:320, :] = layer0[0:320]
    middle[320:480, :] = layer1[256:416]
    late[...] = layer1[0:256]


def sort_weights(place, mine, received):
    return call(
        sort_body,
        place,
        (1,),
        [whole(mine), whole(received)],
        [whole_out(shape, BF) for shape in ((16, 112, 256), (480, 256), (256, 256))],
    )


def shift_z(value, step):
    return lax.ppermute(value, "seq", [(z, (z + step) % 4) for z in range(4)])


def swap_core(value):
    return lax.ppermute(value, "section", [(0, 1), (1, 0)])


def to_owners(pack):
    return lax.all_to_all(pack, "shard", 0, 0, tiled=True)


def after(value, *others):
    return lax.optimization_barrier((value, others))[0]


def regroup(values):
    got = {0: values[0]}
    for step in (1, 3, 2):
        got[step] = shift_z(values[step], step)
    return [got[step] for step in SHIFTS]


def unit_of(states):
    centre = states - jnp.mean(states, axis=-1, keepdims=True)
    scaled = lax.rsqrt(jnp.mean(centre * centre, axis=-1, keepdims=True) + NORM_EPS)
    return centre * scaled, scaled


def qkv_rows(weights):
    array, first = weights
    return [
        (array, (16, 32, 256), functools.partial(lambda at, m, _: (0, at, 0), first + part))
        for part in range(3)
    ]


def proj_rows(weights):
    array, first = weights
    return (array, (8, 64, 256), lambda m, place: (place[1], first, 0))


def put_heads_grad(grad, proj, held, first):
    weight = proj[...]
    total = dims(weight[:, 0:32].reshape(256, 256), grad[:, 0:256], 1, 1) + dims(
        weight[:, 32:64].reshape(256, 256), grad[:, 256:512], 1, 1
    )
    for head in range(4):
        held[head, first : first + 64, :] = total[64 * head : 64 * head + 64].astype(BF)


def before_body(second, place, *refs):
    refs = list(refs)
    states = refs.pop(0)[...].astype(F32)
    if second:
        part_a, part_b, grad, proj = [refs.pop(0) for _ in range(4)]
        states = (states + (part_a[...] + part_b[...])).astype(BF)
    wq, wk, wv, norms, turns = refs[:5]
    outs = refs[5:9]
    attn_ref, mlp_ref = refs[9:11]
    held = refs[-1]
    if second:
        refs[11][...] = states
        states = states.astype(F32)
    unit, _ = unit_of(states)
    attn_in = (unit * norms[0:1, :] + norms[2:3, :]).astype(BF)
    attn_ref[...] = attn_in
    mlp_ref[...] = (unit * norms[1:2, :] + norms[3:4, :]).astype(BF)
    cosine, sine = turns[0], turns[1]
    for part, weight in enumerate((wq, wk, wv)):
        mixed = dims(weight[...].reshape(D, 256), attn_in, 0, 1)
        for head in range(4):
            block = mixed[64 * head : 64 * head + 64]
            if part < 2:
                a, b = block[0:8], block[8:16]
                block = jnp.concatenate(
                    [a * cosine - b * sine, b * cosine + a * sine, block[16:]], axis=0
                )
            if part == 0:
                block = block * 0.125
            held[head, 64 * part : 64 * part + 64, :] = block.astype(BF)
    if second:
        put_heads_grad(grad, proj, held, 192)
    for step in SHIFTS:
        outs[step][...] = held[lax.rem(place[0] + step, 4)]


def before_layer(place, states, extra, weights, norms, turns):
    array, first = weights
    ins = [rows(states)]
    depth = 192
    if extra:
        parts, grad, proj = extra
        ins += [rows(parts[0]), rows(parts[1]), rows(grad), proj_rows(proj)]
        depth = 256
    ins += qkv_rows(weights)
    ins += [whole(norms), lanes(turns)]
    outs = [lanes_out((depth,), BF) for _ in SHIFTS]
    outs += [kept_in_hbm(rows_out(D, BF)), kept_in_hbm(rows_out(D, BF))]
    if extra:
        outs.append(kept_in_hbm(rows_out(D, BF)))
    return call(
        functools.partial(before_body, bool(extra)),
        place,
        (MICRO,),
        ins,
        outs,
        [pltpu.VMEM((4, depth, BLOCK), BF)],
        flops=1_200_000_000,
        moved=6_000_000,
    )


def mlp_body(place, mlp_in, up, down, out, active_ref, slope_ref):
    step = pl.program_id(0)
    hidden = jnp.dot(mlp_in[...], up[...].reshape(D, 256), preferred_element_type=F32)
    cdf = 0.5 * (1.0 + lax.erf(hidden * 0.7071067811865476))
    pdf = jnp.exp(-0.5 * hidden * hidden) * 0.3989422804014327
    active = (hidden * cdf).astype(BF)
    active_ref[...] = active
    slope_ref[...] = cdf + hidden * pdf
    lower = down[...]
    both = jnp.concatenate(
        [lower[:, 0:64].reshape(256, 256), lower[:, 64:128].reshape(256, 256)], axis=1
    )
    product = jnp.dot(active, both, preferred_element_type=F32)

    @pl.when(step == 0)
    def _():
        out[...] = product

    @pl.when(step > 0)
    def _():
        out[...] += product


def mlp_layer(place, mlp_in, weights):
    return call(
        mlp_body,
        place,
        (4,),
        [
            whole(mlp_in),
            (weights, (16, 32, 256), lambda b, _: (0, b, 0)),
            (weights, (4, 128, 256), lambda b, _: (b, 1, 0)),
        ],
        [
            whole_out((TOKENS, D), F32),
            kept_in_hbm(((TOKENS, 1024), BF, (TOKENS, 256), lambda b, _: (0, b))),
            kept_in_hbm(((TOKENS, 1024), F32, (TOKENS, 256), lambda b, _: (0, b))),
        ],
        flops=6_000_000_000,
        moved=12_000_000,
    )


def put_starts(place, places, starts):
    along = lax.broadcasted_iota(jnp.int32, (1, BLOCK), 1)
    for step in SHIFTS:
        source = lax.rem(place[0] - step + 4, 4)
        starts[source] = along + BLOCK * source - places[step][...]


def allowed_keys(starts, query_block, key_block):
    keys = lax.broadcasted_iota(jnp.int32, (BLOCK, BLOCK), 0) + BLOCK * key_block
    allowed = keys >= starts[query_block]
    if query_block == key_block:
        queries = lax.broadcasted_iota(jnp.int32, (BLOCK, BLOCK), 1) + BLOCK * query_block
        allowed = allowed & (keys <= queries)
    return allowed


def attend_body(place, *refs):
    came, places = refs[0:4], refs[4:8]
    outs = refs[8:12]
    kept, heads_out, log_total = refs[12:15]
    starts, keys = refs[15:17]
    for step in SHIFTS:
        source = lax.rem(place[0] - step + 4, 4)
        kept[0, source] = came[step][...]
    put_starts(place, places, starts)
    for j in range(4):
        keys[j] = kept[0, j, 64:128].T
    for i in range(4):
        query = kept[0, i, 0:64]
        scores = []
        for j in range(i + 1):
            raw = jnp.dot(keys[j], query, preferred_element_type=F32)
            scores.append(jnp.where(allowed_keys(starts, i, j), raw, MASKED))
        peak = functools.reduce(
            jnp.maximum, [jnp.max(s, axis=0, keepdims=True) for s in scores]
        )
        total = jnp.zeros((1, BLOCK), F32)
        acc = jnp.zeros((HEAD, BLOCK), F32)
        for j in range(i + 1):
            probs = jnp.exp(scores[j] - peak)
            total = total + jnp.sum(probs, axis=0, keepdims=True)
            acc = acc + jnp.dot(
                kept[0, j, 128:192], probs.astype(BF), preferred_element_type=F32
            )
        heads_out[0, i] = (acc / total).astype(BF)
        log_total[0, i] = peak + jnp.log(total)
    for step in SHIFTS:
        outs[step][...] = heads_out[0, lax.rem(place[0] + step, 4)]


def attend(place, came, places):
    return call(
        attend_body,
        place,
        (MICRO,),
        [lanes(piece) for piece in came] + [lanes(piece) for piece in places],
        [lanes_out((HEAD,), BF) for _ in SHIFTS]
        + [
            kept_in_hbm(by_micro_out((MICRO, 4, 192, BLOCK), BF)),
            kept_in_hbm(by_micro_out((MICRO, 4, HEAD, BLOCK), BF)),
            kept_in_hbm(by_micro_out((MICRO, 4, 1, BLOCK), F32)),
        ],
        [pltpu.VMEM((4, 1, BLOCK), jnp.int32), pltpu.VMEM((4, BLOCK, HEAD), BF)],
        flops=8_000_000_000,
        moved=4_000_000,
    )


def after_body(place, *refs):
    came = refs[0:4]
    proj, mlp_out, out, heads = refs[4:8]
    for step in SHIFTS:
        source = lax.rem(place[0] - step + 4, 4)
        at = pl.multiple_of(source * HEAD, HEAD)
        heads[pl.ds(at, HEAD), :] = came[step][...]
    held = heads[...]
    weight = proj[...]
    for side in range(2):
        span = slice(256 * side, 256 * side + 256)
        product = dims(held, weight[:, 32 * side : 32 * side + 32].reshape(256, 256), 0, 0)
        out[:, span] = mlp_out[:, span] + product


def after_layer(place, came, first, proj, mlp_out):
    return call(
        after_body,
        place,
        (MICRO,),
        [(piece, (HEAD, BLOCK), lambda m, _: (first, m)) for piece in came]
        + [proj_rows(proj), rows(mlp_out)],
        [rows_out(D, F32), lanes_out((256,), BF)],
        flops=800_000_000,
        moved=4_000_000,
    )


def heads_grad_body(place, grad, proj, *refs):
    outs, held = refs[0:4], refs[4]
    put_heads_grad(grad, proj, held, 0)
    for step in SHIFTS:
        outs[step][...] = held[lax.rem(place[0] + step, 4)]


def heads_grad(place, grad, proj):
    return call(
        heads_grad_body,
        place,
        (MICRO,),
        [rows(grad), proj_rows(proj)],
        [lanes_out((HEAD,), BF) for _ in SHIFTS],
        [pltpu.VMEM((4, HEAD, BLOCK), BF)],
        flops=800_000_000,
        moved=2_000_000,
    )


def put_proj(core, heads, grad, pack, first):
    product = jnp.dot(heads[...], grad[...], preferred_element_type=F32).astype(BF)
    for side in range(2):
        span = pl.ds(first + 32 * side, 32)
        part = product[:, 256 * side : 256 * side + 256].reshape(8, 32, 256)
        pack[pl.ds(8 * core, 8), span, :] = part
        pack[pl.ds(8 - 8 * core, 8), span, :] = jnp.zeros_like(part)


def mlp_back_body(with_proj, place, grad, active, slope, mlp_in, up, down, *refs):
    out, pack = refs[-2:]
    step = pl.program_id(0)
    lower = down[...]
    both = jnp.concatenate(
        [lower[:, 0:64].reshape(256, 256), lower[:, 64:128].reshape(256, 256)], axis=1
    )
    active_grad = dims(grad[...], both, 1, 1)
    hidden_grad = (active_grad * slope[...]).astype(BF)
    product = dims(hidden_grad, up[...].reshape(D, 256), 1, 1)

    @pl.when(step == 0)
    def _():
        out[...] = product
        if with_proj:
            put_proj(place[1], refs[0], grad, pack, 256)

    @pl.when(step > 0)
    def _():
        out[...] += product

    up_part = dims(mlp_in[...], hidden_grad, 0, 0).astype(BF).reshape(16, 32, 256)
    pack[:, pl.ds(pl.multiple_of(32 * step, 32), 32), :] = up_part
    down_part = dims(active[...], grad[...], 0, 0).astype(BF)
    for side in range(2):
        pack[pl.ds(4 * step, 4), 128 + 64 * side : 192 + 64 * side, :] = down_part[
            :, 256 * side : 256 * side + 256
        ].reshape(4, 64, 256)


def mlp_back(place, grad, active, slope, mlp_in, weights, heads=None):
    ins = [
        whole(grad),
        (in_hbm(active), (TOKENS, 256), lambda b, _: (0, b)),
        (in_hbm(slope), (TOKENS, 256), lambda b, _: (0, b)),
        whole(mlp_in),
        (weights, (16, 32, 256), lambda b, _: (0, b, 0)),
        (weights, (4, 128, 256), lambda b, _: (b, 1, 0)),
    ]
    depth = 256
    if heads is not None:
        ins.append(whole(heads))
        depth = 320
    return call(
        functools.partial(mlp_back_body, heads is not None),
        place,
        (4,),
        ins,
        [whole_out((TOKENS, D), F32), whole_out((16, depth, 256), BF)],
        flops=8_000_000_000,
        moved=14_000_000,
    )


def attend_back_body(place, *refs):
    came, places = refs[0:4], refs[4:8]
    kept_ref, heads_out, log_total = refs[8:11]
    outs = refs[11:15]
    starts, keys, values, grads, acc = refs[15:20]
    for step in SHIFTS:
        source = lax.rem(place[0] - step + 4, 4)
        grads[source] = came[step][...]
    put_starts(place, places, starts)
    acc[...] = jnp.zeros_like(acc)
    for j in range(4):
        keys[j] = kept_ref[0, j, 64:128].T
        values[j] = kept_ref[0, j, 128:192].T
    for i in range(4):
        query = kept_ref[0, i, 0:64]
        grad = grads[i]
        log_row = log_total[0, i]
        centre = jnp.sum(
            grad.astype(F32) * heads_out[0, i].astype(F32), axis=0, keepdims=True
        )
        query_grad = jnp.zeros((HEAD, BLOCK), F32)
        for j in range(i + 1):
            raw = jnp.dot(keys[j], query, preferred_element_type=F32)
            probs = jnp.where(allowed_keys(starts, i, j), jnp.exp(raw - log_row), 0.0)
            probs_grad = jnp.dot(values[j], grad, preferred_element_type=F32)
            scores_grad = (probs * (probs_grad - centre)).astype(BF)
            acc[j, 128:192, :] += dims(grad, probs.astype(BF), 1, 1)
            acc[j, 64:128, :] += dims(query, scores_grad, 1, 1)
            query_grad = query_grad + jnp.dot(
                kept_ref[0, j, 64:128], scores_grad, preferred_element_type=F32
            )
        acc[i, 0:64, :] = query_grad * 0.125
    for step in SHIFTS:
        outs[step][...] = acc[lax.rem(place[0] + step, 4)].astype(BF)


def attend_back(place, came, places, kept, heads_out, log_total):
    return call(
        attend_back_body,
        place,
        (MICRO,),
        [lanes(piece) for piece in came]
        + [lanes(piece) for piece in places]
        + [by_micro(in_hbm(array)) for array in (kept, heads_out, log_total)],
        [lanes_out((192,), BF) for _ in SHIFTS],
        [
            pltpu.VMEM((4, 1, BLOCK), jnp.int32),
            pltpu.VMEM((4, BLOCK, HEAD), BF),
            pltpu.VMEM((4, BLOCK, HEAD), BF),
            pltpu.VMEM((4, HEAD, BLOCK), BF),
            pltpu.VMEM((4, 192, BLOCK), F32),
        ],
        flops=16_000_000_000,
        moved=5_000_000,
    )


def attend_both_body(place, *refs):
    came, places, outs = refs[0:4], refs[4:8], refs[8:12]
    starts, kept, keys, values, acc, out = refs[12:18]
    for step in SHIFTS:
        source = lax.rem(place[0] - step + 4, 4)
        kept[source] = came[step][...]
    put_starts(place, places, starts)
    acc[...] = jnp.zeros_like(acc)
    for j in range(4):
        keys[j] = kept[j, 64:128].T
        values[j] = kept[j, 128:192].T
    for i in range(4):
        query = kept[i, 0:64]
        grad = kept[i, 192:256]
        scores = []
        for j in range(i + 1):
            raw = jnp.dot(keys[j], query, preferred_element_type=F32)
            scores.append(jnp.where(allowed_keys(starts, i, j), raw, MASKED))
        peak = functools.reduce(
            jnp.maximum, [jnp.max(s, axis=0, keepdims=True) for s in scores]
        )
        exps = [jnp.exp(s - peak) for s in scores]
        total = functools.reduce(jnp.add, [jnp.sum(e, axis=0, keepdims=True) for e in exps])
        inverse = 1.0 / total
        result = jnp.zeros((HEAD, BLOCK), F32)
        probs = []
        for j in range(i + 1):
            prob = exps[j] * inverse
            low = prob.astype(BF)
            probs.append(prob)
            result = result + jnp.dot(kept[j, 128:192], low, preferred_element_type=F32)
            acc[j, 128:192, :] += dims(grad, low, 1, 1)
        out[i] = result.astype(BF)
        centre = jnp.sum(grad.astype(F32) * result, axis=0, keepdims=True)
        query_grad = jnp.zeros((HEAD, BLOCK), F32)
        for j in range(i + 1):
            probs_grad = jnp.dot(values[j], grad, preferred_element_type=F32)
            scores_grad = (probs[j] * (probs_grad - centre)).astype(BF)
            acc[j, 64:128, :] += dims(query, scores_grad, 1, 1)
            query_grad = query_grad + jnp.dot(
                kept[j, 64:128], scores_grad, preferred_element_type=F32
            )
        acc[i, 0:64, :] = query_grad * 0.125
    for step in SHIFTS:
        other = lax.rem(place[0] + step, 4)
        outs[step][0:192, :] = acc[other].astype(BF)
        outs[step][192:256, :] = out[other]


def attend_both(place, came, places):
    return call(
        attend_both_body,
        place,
        (MICRO,),
        [lanes(piece) for piece in came] + [lanes(piece) for piece in places],
        [lanes_out((256,), BF) for _ in SHIFTS],
        [
            pltpu.VMEM((4, 1, BLOCK), jnp.int32),
            pltpu.VMEM((4, 256, BLOCK), BF),
            pltpu.VMEM((4, BLOCK, HEAD), BF),
            pltpu.VMEM((4, BLOCK, HEAD), BF),
            pltpu.VMEM((4, 192, BLOCK), F32),
            pltpu.VMEM((4, HEAD, BLOCK), BF),
        ],
        flops=18_000_000_000,
        moved=5_000_000,
    )


def mixed_back_body(with_heads, place, *refs):
    came = refs[0:4]
    wq, wk, wv, norms, turns, states, mlp_grad = refs[4:11]
    out, mixed_ref, sums = refs[11:14]
    cosine, sine = turns[0], turns[1]
    for step in SHIFTS:
        head = lax.rem(place[0] - step + 4, 4)
        at = pl.multiple_of(head * HEAD, HEAD)
        for part in range(3):
            block = came[step][64 * part : 64 * part + 64]
            if part < 2:
                a, b = block[0:8].astype(F32), block[8:16].astype(F32)
                turned = jnp.concatenate(
                    [a * cosine + b * sine, b * cosine - a * sine], axis=0
                ).astype(BF)
                block = jnp.concatenate([turned, block[16:]], axis=0)
            mixed_ref[part, pl.ds(at, HEAD), :] = block
        if with_heads:
            refs[14][pl.ds(at, HEAD), :] = came[step][192:256]
    attn_grad = jnp.zeros((BLOCK, D), F32)
    for part, weight in enumerate((wq, wk, wv)):
        attn_grad = attn_grad + dims(mixed_ref[part], weight[...].reshape(D, 256), 0, 1)
    unit, _ = unit_of(states[...].astype(F32))
    other_grad = mlp_grad[...]
    out[...] = attn_grad * norms[0:1, :] + other_grad * norms[1:2, :]

    @pl.when(pl.program_id(0) == 0)
    def _():
        sums[...] = jnp.zeros_like(sums)

    sums[0:1, :] += jnp.sum(attn_grad * unit, axis=0, keepdims=True)
    sums[1:2, :] += jnp.sum(other_grad * unit, axis=0, keepdims=True)
    sums[2:3, :] += jnp.sum(attn_grad, axis=0, keepdims=True)
    sums[3:4, :] += jnp.sum(other_grad, axis=0, keepdims=True)


def mixed_back(place, came, weights, norms, turns, states, mlp_grad):
    with_heads = came[0].shape[0] == 256
    ins = [lanes(piece) for piece in came]
    ins += qkv_rows(weights)
    ins += [whole(norms), lanes(turns), rows(states), rows(mlp_grad)]
    return call(
        functools.partial(mixed_back_body, with_heads),
        place,
        (MICRO,),
        ins,
        [
            rows_out(D, F32),
            lanes_out((3, 256), BF),
            whole_out((8, D), F32),
        ]
        + [lanes_out((256,), BF)] * with_heads,
        flops=1_500_000_000,
        moved=6_000_000,
    )


def weight_back_body(with_rest, place, attn_in, mixed, sums, *refs):
    pack = refs[-1]
    first = 0
    if with_rest:
        rest, heads, grad = refs[:3]
        pack[:, 0:256, :] = rest[...]
        put_proj(place[1], heads, grad, pack, 256)
        first = 320
    for part in range(3):
        product = dims(attn_in[...], mixed[part], 0, 1)
        at = first + 32 * part
        pack[:, at : at + 32, :] = product.astype(BF).reshape(16, 32, 256)
    at = first + 96
    pack[:, at : at + 16, :] = jnp.zeros((16, 16, 256), BF)
    for owner in range(16):
        tile, shift = owner // 4, owner % 4 * 32
        lines = sums[:, 128 * tile : 128 * tile + 128]
        if shift:
            lines = pltpu.roll(lines, 128 - shift, 1)
        lines = jnp.concatenate([lines, jnp.zeros_like(lines)], axis=0).astype(BF)
        pack[owner, at : at + 16, 0:128] = lines


def weight_back(place, attn_in, mixed, sums, rest=()):
    return call(
        functools.partial(weight_back_body, bool(rest)),
        place,
        (1,),
        [whole(attn_in), whole(mixed), whole(sums)] + [whole(array) for array in rest],
        [whole_out((16, 432 if rest else 112, 256), BF)],
        flops=2_000_000_000,
        moved=6_000_000,
    )[0]


def end_body(place, states, grad, own, came, out):
    unit, scaled = unit_of(states[...].astype(F32))
    through = own[...] + came[...]
    back = scaled * (
        through
        - jnp.mean(through, axis=-1, keepdims=True)
        - unit * jnp.mean(through * unit, axis=-1, keepdims=True)
    )
    out[...] = (grad[...].astype(F32) + back).astype(BF)


def end_back(place, states, grad, own, came):
    return call(
        end_body,
        place,
        (MICRO,),
        [rows(states), rows(grad), rows(own), rows(came)],
        [rows_out(D, BF)],
        flops=100_000_000,
        moved=5_000_000,
    )[0]


def scatter_sum(pack):
    return jnp.sum(to_owners(pack).astype(F32), axis=0).astype(BF)


def choose_body(place, *refs):
    keep, send = refs[12:14]
    total = []
    for group in range(3):
        held = refs[4 * group][...].astype(F32)
        for step in range(1, 4):
            held = held + refs[4 * group + step][...].astype(F32)
        total.append(held)
    layer1 = total[0]
    layer0 = jnp.concatenate([total[1], total[2]], axis=0)
    first = place[1] == 0
    keep[...] = jnp.where(first, layer0, layer1)
    send[...] = jnp.where(first, layer1, layer0).astype(BF)


def choose(place, pieces):
    return call(
        choose_body,
        place,
        (1,),
        [whole(piece) for piece in pieces],
        [whole_out((432, 256), F32), whole_out((432, 256), BF)],
    )


def unpack_body(place, keep, got, qkv, proj, up, down, sums, total):
    core = place[1]
    total[core] = keep[...]
    total[1 - core] = got[...].astype(F32)
    low = lax.broadcasted_iota(jnp.int32, (32, 128), 1) < 64
    sums[...] = total[0, 416:424, 0:128] + total[1, 416:424, 0:128]
    for half in range(2):
        for part in range(3):
            at = 512 * part + 256 * half
            qkv[:, at : at + 256] = total[half, 320 + 32 * part : 352 + 32 * part]
        at = 256 + 32 * half
        proj[:, 256 * half : 256 * half + 256] = total[0, at : at + 32] + total[1, at : at + 32]
        for side in range(2):
            down[64 * half : 64 * half + 64, 256 * side : 256 * side + 256] = total[
                half, 128 + 64 * side : 192 + 64 * side
            ]
    for tile in range(16):
        row = 32 * (tile // 4)
        at = 128 * (tile % 4 // 2)
        left = total[0, row : row + 32, at : at + 128]
        right = total[1, row : row + 32, at : at + 128]
        if tile % 2 == 0:
            joined = jnp.where(low, left, pltpu.roll(right, 64, 1))
        else:
            joined = jnp.where(low, pltpu.roll(left, 64, 1), right)
        up[:, 128 * tile : 128 * tile + 128] = joined


def unpack(place, keep, got):
    return call(
        unpack_body,
        place,
        (1,),
        [whole(keep), whole(got)],
        [
            whole_out((32, 1536), F32),
            whole_out((32, 512), F32),
            whole_out((32, 2048), F32),
            whole_out((128, 512), F32),
            whole_out((8, 128), F32),
        ],
        [pltpu.VMEM((2, 432, 256), F32)],
    )


def on_device(
    inputs,
    positions,
    cotangent,
    qkv_weight,
    proj_weight,
    up_weight,
    down_weight,
    norm_gain,
    norm_bias,
):
    core = lax.axis_index("section")
    chip_z = lax.axis_index("seq")
    shard = lax.axis_index("shard")
    first = core == 0
    place = jnp.stack([chip_z, core, shard // 4, shard % 4]).astype(jnp.int32)

    own_norms = jnp.concatenate([norm_gain[0], norm_bias[0]], axis=0).reshape(1, 128)
    mine, other = pack_weights(
        place,
        qkv_weight[0],
        proj_weight[0],
        up_weight[0],
        down_weight[0],
        jnp.broadcast_to(own_norms, (16, 128)),
    )
    early, middle, late = sort_weights(place, mine, swap_core(other))
    places_row = positions.reshape(1, TOKENS)
    gathered, places = lax.optimization_barrier(
        (to_owners(early), regroup([places_row] * 4))
    )
    middle_all = lax.all_gather(middle, "shard")
    late_all = lax.all_gather(late, "shard")
    norms = (
        gathered[:, 96, :]
        .reshape(16, 2, 4, 32)
        .transpose(1, 2, 0, 3)
        .reshape(2, 4, D)
        .astype(F32)
    )
    qkv_of = ((gathered, 0), (middle_all, 12))
    proj_of = ((middle_all, 4), (middle_all, 5))
    mlp_of = (middle_all, late_all)
    rates = 10000.0 ** (-jnp.arange(ROT // 2, dtype=F32) * 2.0 / ROT)
    angles = rates[:, None] * places_row.astype(F32)
    turns = jnp.stack([jnp.cos(angles), jnp.sin(angles)])

    states = inputs.reshape(TOKENS, D)
    grad = cotangent.reshape(TOKENS, D)
    extra = ()
    saved = []
    for layer in range(2):
        done = before_layer(place, states, extra, qkv_of[layer], norms[layer], turns)
        sent, attn_in, mlp_in = done[0:4], done[4], done[5]
        if layer == 1:
            states = done[6]
        came = regroup(sent)
        if layer == 1:
            sent = attend_both(place, came, places)
            mlp_in = after(mlp_in, sent)
            came = regroup(sent)
        mlp_out, active, slope = mlp_layer(place, mlp_in, mlp_of[layer])
        if layer == 0:
            done = attend(place, came, places)
            kept, heads_out, log_total = done[4:7]
            came = regroup(done[0:4])
        part, heads = after_layer(place, came, 3 * layer, proj_of[layer], mlp_out)
        parts = (part, swap_core(part))
        extra = (parts, grad, proj_of[1])
        saved.append((states, attn_in, mlp_in, active, slope, heads))
    result = (states.astype(F32) + (parts[0] + parts[1])).astype(BF)
    layer_out = jnp.where(first, saved[1][0], result)

    grads = [None, None]
    for layer in (1, 0):
        states, attn_in, mlp_in, active, slope, heads = saved[layer]
        if layer == 1:
            mlp_grad, pack = mlp_back(place, grad, active, slope, mlp_in, mlp_of[1])
        else:
            sent = heads_grad(place, grad, proj_of[0])
            came = regroup(sent)
            mlp_grad, pack = mlp_back(
                place, after(grad, sent), active, slope, mlp_in, mlp_of[0], heads
            )
            came = after(came, pack)
            sent = attend_back(place, came, places, kept, heads_out, log_total)
            sum_a = scatter_sum(pack)
            came = regroup(sent)
        through, mixed, norm_sums, *heads_of = mixed_back(
            place, came, qkv_of[layer], norms[layer], turns, states, mlp_grad
        )
        if layer == 1:
            pack = weight_back(place, attn_in, mixed, norm_sums, (pack, *heads_of, grad))
            total = lax.psum_scatter(pack, "shard", scatter_dimension=0, tiled=False)
            through = after(through, pack)
        else:
            pack, sum_a = lax.optimization_barrier(
                (weight_back(place, attn_in, mixed, norm_sums), sum_a)
            )
            pieces_a = regroup([sum_a] * 4)
            pieces_b = regroup([scatter_sum(pack)] * 4)
        grad = end_back(place, states, grad, through, swap_core(through))
        grads[layer] = grad
    grads_out = jnp.where(first, grads[0], grads[1])

    keep, send = choose(place, regroup([total] * 4) + pieces_a + pieces_b)
    qkv_grad, proj_grad, up_grad, down_grad, norm_sums = unpack(place, keep, swap_core(send))
    return (
        layer_out.reshape(1, MICRO, 1, BLOCK, D),
        grads_out.reshape(1, MICRO, 1, BLOCK, D),
        qkv_grad[None],
        proj_grad[None],
        up_grad[None],
        down_grad[None],
        norm_sums[None, 0:2, 0:32],
        norm_sums[None, 2:4, 0:32],
    )


def solution(mesh):
    placed = (
        P(None, "shard", "seq", None),
        P(None, "shard", "seq"),
        P(None, "shard", "seq", None),
        P("section", "shard", None),
        P("section", "shard", None),
        P("section", "shard", None),
        P("section", "shard", None),
        P("section", None, "shard"),
        P("section", None, "shard"),
    )
    return jax.shard_map(
        on_device,
        mesh=mesh,
        in_specs=placed,
        out_specs=(
            P("section", None, "shard", "seq", None),
            P("section", None, "shard", "seq", None),
            P("section", "shard", None),
            P("section", "shard", None),
            P("section", "shard", None),
            P("section", "shard", None),
            P("section", None, "shard"),
            P("section", None, "shard"),
        ),
        check_vma=False,
    )
```

```python
import functools

import jax
import jax.numpy as jnp
from jax import lax
from jax.experimental import pallas as pl
from jax.experimental.pallas import tpu as pltpu
from jax.sharding import PartitionSpec as P

D = 512
HEADS = 8
HEAD = 64
ROT = 16
MICRO = 3
BLOCK = 256
TOKENS = MICRO * BLOCK
NORM_EPS = 1e-05
MASKED = -1e30
BF = jnp.bfloat16
F32 = jnp.float32
SHIFTS = (0, 1, 2, 3)
VMEM_LIMIT = 24 * 1024 * 1024


def dims(left, right, left_dim, right_dim):
    return lax.dot_general(
        left, right, (((left_dim,), (right_dim,)), ((), ())), preferred_element_type=F32
    )


def struct(shape, dtype):
    return jax.ShapeDtypeStruct(shape, dtype)


def in_hbm(array):
    return pltpu.with_memory_space_constraint(array, pltpu.HBM)


def call(body, place, grid, ins, outs, scratch=(), flops=10**9, moved=4 * 10**6):
    specs = [pl.BlockSpec(block, index) for _, block, index in ins]
    out_specs = [pl.BlockSpec(out[2], out[3]) for out in outs]
    return pl.pallas_call(
        body,
        out_shape=[
            (pltpu.HBM if out[4:] else struct)(out[0], out[1]) for out in outs
        ],
        grid_spec=pltpu.PrefetchScalarGridSpec(
            num_scalar_prefetch=1,
            grid=grid,
            in_specs=specs,
            out_specs=out_specs,
            scratch_shapes=list(scratch),
        ),
        compiler_params=pltpu.CompilerParams(
            vmem_limit_bytes=VMEM_LIMIT, dimension_semantics=("arbitrary",) * len(grid)
        ),
        cost_estimate=pl.CostEstimate(flops=flops, bytes_accessed=moved, transcendentals=0),
    )(place, *[array for array, _, _ in ins])


def whole(array):
    rank = array.ndim
    return (array, array.shape, lambda *_: (0,) * rank)


def whole_out(shape, dtype):
    rank = len(shape)
    return (shape, dtype, shape, lambda *_: (0,) * rank)


def kept_in_hbm(out):
    return out + (True,)


def rows(array):
    return (array, (BLOCK, array.shape[1]), lambda m, _: (m, 0))


def rows_out(width, dtype):
    return ((TOKENS, width), dtype, (BLOCK, width), lambda m, _: (m, 0))


def lanes(array):
    lead = array.shape[:-1]
    rank = len(lead)
    return (array, lead + (BLOCK,), lambda m, _: (0,) * rank + (m,))


def lanes_out(lead, dtype):
    rank = len(lead)
    return (lead + (TOKENS,), dtype, lead + (BLOCK,), lambda m, _: (0,) * rank + (m,))


def by_micro(array):
    rank = array.ndim - 1
    return (array, (1,) + array.shape[1:], lambda m, _: (m,) + (0,) * rank)


def by_micro_out(shape, dtype):
    rank = len(shape) - 1
    return (shape, dtype, (1,) + shape[1:], lambda m, _: (m,) + (0,) * rank)


def pack_body(place, qkv, proj, up, down, norms, mine, other, held):
    low = lax.broadcasted_iota(jnp.int32, (32, 128), 1) < 64
    for half in range(2):
        for pair in range(8):
            first = up[:, 256 * pair : 256 * pair + 128].astype(F32)
            second = up[:, 256 * pair + 128 : 256 * pair + 256].astype(F32)
            if half == 0:
                cut = jnp.where(low, first, pltpu.roll(second, 64, 1))
            else:
                cut = jnp.where(low, pltpu.roll(first, 64, 1), second)
            at = 128 * (pair % 2)
            held[half, 32 * (pair // 2) : 32 * (pair // 2) + 32, at : at + 128] = cut.astype(BF)
        for side in range(2):
            held[half, 128 + 64 * side : 192 + 64 * side, :] = down[
                64 * half : 64 * half + 64, 256 * side : 256 * side + 256
            ]
            held[half, 256 + 32 * side : 288 + 32 * side, :] = proj[
                :, 256 * side : 256 * side + 256
            ]
        for part in range(3):
            at = 512 * part + 256 * half
            held[half, 320 + 32 * part : 352 + 32 * part, :] = qkv[:, at : at + 256]
        held[half, 416:432, 0:128] = norms[...]
        held[half, 416:432, 128:256] = norms[...]
    core = place[1]
    mine[...] = held[core]
    other[...] = held[1 - core]


def pack_weights(place, qkv, proj, up, down, norms):
    return call(
        pack_body,
        place,
        (1,),
        [whole(in_hbm(array)) for array in (qkv, proj, up, down)] + [whole(norms)],
        [whole_out((432, 256), BF), whole_out((432, 256), BF)],
        [pltpu.VMEM((2, 432, 256), BF)],
    )


def sort_body(place, mine, received, early, middle, late):
    first = place[1] == 0
    kept = mine[...]
    came = received[...]
    layer0 = jnp.where(first, kept, came)
    layer1 = jnp.where(first, came, kept)
    norms = jnp.concatenate([layer0[416:432, 0:128], layer1[416:432, 0:128]], axis=1)
    for peer in range(16):
        early[peer, 0:96, :] = layer0[320:416]
        early[peer, 96:112, :] = norms
    middle[0:320, :] = layer0[0:320]
    middle[320:480, :] = layer1[256:416]
    late[...] = layer1[0:256]


def sort_weights(place, mine, received):
    return call(
        sort_body,
        place,
        (1,),
        [whole(mine), whole(received)],
        [whole_out(shape, BF) for shape in ((16, 112, 256), (480, 256), (256, 256))],
    )


def shift_z(value, step):
    return lax.ppermute(value, "seq", [(z, (z + step) % 4) for z in range(4)])


def swap_core(value):
    return lax.ppermute(value, "section", [(0, 1), (1, 0)])


def to_owners(pack):
    return lax.all_to_all(pack, "shard", 0, 0, tiled=True)


def after(value, *others):
    return lax.optimization_barrier((value, others))[0]


def regroup(values):
    got = {0: values[0]}
    for step in (1, 3, 2):
        got[step] = shift_z(values[step], step)
    return [got[step] for step in SHIFTS]


def unit_of(states):
    centre = states - jnp.mean(states, axis=-1, keepdims=True)
    scaled = lax.rsqrt(jnp.mean(centre * centre, axis=-1, keepdims=True) + NORM_EPS)
    return centre * scaled, scaled


def qkv_rows(weights):
    array, first = weights
    return [
        (array, (16, 32, 256), functools.partial(lambda at, m, _: (0, at, 0), first + part))
        for part in range(3)
    ]


def proj_rows(weights):
    array, first = weights
    return (array, (8, 64, 256), lambda m, place: (place[1], first, 0))


def put_heads_grad(grad, proj, held, first):
    weight = proj[...]
    total = dims(weight[:, 0:32].reshape(256, 256), grad[:, 0:256], 1, 1) + dims(
        weight[:, 32:64].reshape(256, 256), grad[:, 256:512], 1, 1
    )
    for head in range(4):
        held[head, first : first + 64, :] = total[64 * head : 64 * head + 64].astype(BF)


def before_body(second, place, *refs):
    refs = list(refs)
    states = refs.pop(0)[...].astype(F32)
    if second:
        part_a, part_b, grad, proj = [refs.pop(0) for _ in range(4)]
        states = (states + (part_a[...] + part_b[...])).astype(BF)
    wq, wk, wv, norms, turns = refs[:5]
    outs = refs[5:9]
    attn_ref, mlp_ref = refs[9:11]
    held = refs[-1]
    if second:
        refs[11][...] = states
        states = states.astype(F32)
    unit, _ = unit_of(states)
    attn_in = (unit * norms[0:1, :] + norms[2:3, :]).astype(BF)
    attn_ref[...] = attn_in
    mlp_ref[...] = (unit * norms[1:2, :] + norms[3:4, :]).astype(BF)
    cosine, sine = turns[0], turns[1]
    for part, weight in enumerate((wq, wk, wv)):
        mixed = dims(weight[...].reshape(D, 256), attn_in, 0, 1)
        for head in range(4):
            block = mixed[64 * head : 64 * head + 64]
            if part < 2:
                a, b = block[0:8], block[8:16]
                block = jnp.concatenate(
                    [a * cosine - b * sine, b * cosine + a * sine, block[16:]], axis=0
                )
            if part == 0:
                block = block * 0.125
            held[head, 64 * part : 64 * part + 64, :] = block.astype(BF)
    if second:
        put_heads_grad(grad, proj, held, 192)
    for step in SHIFTS:
        outs[step][...] = held[lax.rem(place[0] + step, 4)]


def before_layer(place, states, extra, weights, norms, turns):
    array, first = weights
    ins = [rows(states)]
    depth = 192
    if extra:
        parts, grad, proj = extra
        ins += [rows(parts[0]), rows(parts[1]), rows(grad), proj_rows(proj)]
        depth = 256
    ins += qkv_rows(weights)
    ins += [whole(norms), lanes(turns)]
    outs = [lanes_out((depth,), BF) for _ in SHIFTS]
    outs += [kept_in_hbm(rows_out(D, BF)), kept_in_hbm(rows_out(D, BF))]
    if extra:
        outs.append(kept_in_hbm(rows_out(D, BF)))
    return call(
        functools.partial(before_body, bool(extra)),
        place,
        (MICRO,),
        ins,
        outs,
        [pltpu.VMEM((4, depth, BLOCK), BF)],
        flops=1_200_000_000,
        moved=6_000_000,
    )


def mlp_body(place, mlp_in, up, down, out, active_ref, slope_ref):
    step = pl.program_id(0)
    hidden = jnp.dot(mlp_in[...], up[...].reshape(D, 256), preferred_element_type=F32)
    cdf = 0.5 * (1.0 + lax.erf(hidden * 0.7071067811865476))
    pdf = jnp.exp(-0.5 * hidden * hidden) * 0.3989422804014327
    active = (hidden * cdf).astype(BF)
    active_ref[...] = active
    slope_ref[...] = cdf + hidden * pdf
    lower = down[...]
    both = jnp.concatenate(
        [lower[:, 0:64].reshape(256, 256), lower[:, 64:128].reshape(256, 256)], axis=1
    )
    product = jnp.dot(active, both, preferred_element_type=F32)

    @pl.when(step == 0)
    def _():
        out[...] = product

    @pl.when(step > 0)
    def _():
        out[...] += product


def mlp_layer(place, mlp_in, weights):
    return call(
        mlp_body,
        place,
        (4,),
        [
            whole(mlp_in),
            (in_hbm(weights), (16, 32, 256), lambda b, _: (0, b, 0)),
            (in_hbm(weights), (4, 128, 256), lambda b, _: (b, 1, 0)),
        ],
        [
            whole_out((TOKENS, D), F32),
            kept_in_hbm(((TOKENS, 1024), BF, (TOKENS, 256), lambda b, _: (0, b))),
            kept_in_hbm(((TOKENS, 1024), F32, (TOKENS, 256), lambda b, _: (0, b))),
        ],
        flops=6_000_000_000,
        moved=12_000_000,
    )


def put_starts(place, places, starts):
    along = lax.broadcasted_iota(jnp.int32, (1, BLOCK), 1)
    for step in SHIFTS:
        source = lax.rem(place[0] - step + 4, 4)
        starts[source] = along + BLOCK * source - places[step][...]


def allowed_keys(starts, query_block, key_block):
    keys = lax.broadcasted_iota(jnp.int32, (BLOCK, BLOCK), 0) + BLOCK * key_block
    allowed = keys >= starts[query_block]
    if query_block == key_block:
        queries = lax.broadcasted_iota(jnp.int32, (BLOCK, BLOCK), 1) + BLOCK * query_block
        allowed = allowed & (keys <= queries)
    return allowed


def attend_body(place, *refs):
    came, places = refs[0:4], refs[4:8]
    outs = refs[8:12]
    kept, heads_out, log_total = refs[12:15]
    starts, keys = refs[15:17]
    for step in SHIFTS:
        source = lax.rem(place[0] - step + 4, 4)
        kept[0, source] = came[step][...]
    put_starts(place, places, starts)
    for j in range(4):
        keys[j] = kept[0, j, 64:128].T
    for i in range(4):
        query = kept[0, i, 0:64]
        scores = []
        for j in range(i + 1):
            raw = jnp.dot(keys[j], query, preferred_element_type=F32)
            scores.append(jnp.where(allowed_keys(starts, i, j), raw, MASKED))
        peak = functools.reduce(
            jnp.maximum, [jnp.max(s, axis=0, keepdims=True) for s in scores]
        )
        total = jnp.zeros((1, BLOCK), F32)
        acc = jnp.zeros((HEAD, BLOCK), F32)
        for j in range(i + 1):
            probs = jnp.exp(scores[j] - peak)
            total = total + jnp.sum(probs, axis=0, keepdims=True)
            acc = acc + jnp.dot(
                kept[0, j, 128:192], probs.astype(BF), preferred_element_type=F32
            )
        heads_out[0, i] = (acc / total).astype(BF)
        log_total[0, i] = peak + jnp.log(total)
    for step in SHIFTS:
        outs[step][...] = heads_out[0, lax.rem(place[0] + step, 4)]


def attend(place, came, places):
    return call(
        attend_body,
        place,
        (MICRO,),
        [lanes(piece) for piece in came] + [lanes(piece) for piece in places],
        [lanes_out((HEAD,), BF) for _ in SHIFTS]
        + [
            kept_in_hbm(by_micro_out((MICRO, 4, 192, BLOCK), BF)),
            kept_in_hbm(by_micro_out((MICRO, 4, HEAD, BLOCK), BF)),
            kept_in_hbm(by_micro_out((MICRO, 4, 1, BLOCK), F32)),
        ],
        [pltpu.VMEM((4, 1, BLOCK), jnp.int32), pltpu.VMEM((4, BLOCK, HEAD), BF)],
        flops=8_000_000_000,
        moved=4_000_000,
    )


def after_body(place, *refs):
    came = refs[0:4]
    proj, mlp_out, out, heads = refs[4:8]
    for step in SHIFTS:
        source = lax.rem(place[0] - step + 4, 4)
        at = pl.multiple_of(source * HEAD, HEAD)
        heads[pl.ds(at, HEAD), :] = came[step][...]
    held = heads[...]
    weight = proj[...]
    for side in range(2):
        span = slice(256 * side, 256 * side + 256)
        product = dims(held, weight[:, 32 * side : 32 * side + 32].reshape(256, 256), 0, 0)
        out[:, span] = mlp_out[:, span] + product


def after_layer(place, came, first, proj, mlp_out):
    return call(
        after_body,
        place,
        (MICRO,),
        [(piece, (HEAD, BLOCK), lambda m, _: (first, m)) for piece in came]
        + [proj_rows(proj), rows(mlp_out)],
        [rows_out(D, F32), lanes_out((256,), BF)],
        flops=800_000_000,
        moved=4_000_000,
    )


def heads_grad_body(place, grad, proj, *refs):
    outs, held = refs[0:4], refs[4]
    put_heads_grad(grad, proj, held, 0)
    for step in SHIFTS:
        outs[step][...] = held[lax.rem(place[0] + step, 4)]


def heads_grad(place, grad, proj):
    return call(
        heads_grad_body,
        place,
        (MICRO,),
        [rows(grad), proj_rows(proj)],
        [lanes_out((HEAD,), BF) for _ in SHIFTS],
        [pltpu.VMEM((4, HEAD, BLOCK), BF)],
        flops=800_000_000,
        moved=2_000_000,
    )


def put_proj(core, heads, other_heads, half_grad, pack, first):
    for side, held in ((core, heads), (1 - core, other_heads)):
        part = jnp.dot(held[...], half_grad[...], preferred_element_type=F32)
        pack[pl.ds(8 * side, 8), first : first + 32, :] = part.astype(BF).reshape(8, 32, 256)


def half_columns(grad):
    return (grad, (TOKENS, 256), lambda m, place: (0, place[1]))


def mlp_back_body(with_proj, place, grad, active, slope, mlp_in, up, down, *refs):
    out, pack = refs[-2:]
    step = pl.program_id(0)
    lower = down[...]
    both = jnp.concatenate(
        [lower[:, 0:64].reshape(256, 256), lower[:, 64:128].reshape(256, 256)], axis=1
    )
    active_grad = dims(grad[...], both, 1, 1)
    hidden_grad = (active_grad * slope[...]).astype(BF)
    product = dims(hidden_grad, up[...].reshape(D, 256), 1, 1)

    @pl.when(step == 0)
    def _():
        out[...] = product
        if with_proj:
            put_proj(place[1], *refs[:3], pack, 256)

    @pl.when(step > 0)
    def _():
        out[...] += product

    up_part = dims(mlp_in[...], hidden_grad, 0, 0).astype(BF).reshape(16, 32, 256)
    pack[:, pl.ds(pl.multiple_of(32 * step, 32), 32), :] = up_part
    down_part = dims(active[...], grad[...], 0, 0).astype(BF)
    for side in range(2):
        pack[pl.ds(4 * step, 4), 128 + 64 * side : 192 + 64 * side, :] = down_part[
            :, 256 * side : 256 * side + 256
        ].reshape(4, 64, 256)


def mlp_back(place, grad, active, slope, mlp_in, weights, heads=()):
    ins = [
        whole(grad),
        (in_hbm(active), (TOKENS, 256), lambda b, _: (0, b)),
        (in_hbm(slope), (TOKENS, 256), lambda b, _: (0, b)),
        whole(mlp_in),
        (in_hbm(weights), (16, 32, 256), lambda b, _: (0, b, 0)),
        (in_hbm(weights), (4, 128, 256), lambda b, _: (b, 1, 0)),
    ]
    depth = 256
    if heads:
        ins += [whole(array) for array in heads] + [half_columns(grad)]
        depth = 288
    return call(
        functools.partial(mlp_back_body, bool(heads)),
        place,
        (4,),
        ins,
        [whole_out((TOKENS, D), F32), whole_out((16, depth, 256), BF)],
        flops=8_000_000_000,
        moved=14_000_000,
    )


def attend_back_body(place, *refs):
    came, places = refs[0:4], refs[4:8]
    kept_ref, heads_out, log_total = refs[8:11]
    outs = refs[11:15]
    starts, keys, values, grads, acc = refs[15:20]
    for step in SHIFTS:
        source = lax.rem(place[0] - step + 4, 4)
        grads[source] = came[step][...]
    put_starts(place, places, starts)
    acc[...] = jnp.zeros_like(acc)
    for j in range(4):
        keys[j] = kept_ref[0, j, 64:128].T
        values[j] = kept_ref[0, j, 128:192].T
    for i in range(4):
        query = kept_ref[0, i, 0:64]
        grad = grads[i]
        log_row = log_total[0, i]
        centre = jnp.sum(
            grad.astype(F32) * heads_out[0, i].astype(F32), axis=0, keepdims=True
        )
        query_grad = jnp.zeros((HEAD, BLOCK), F32)
        for j in range(i + 1):
            raw = jnp.dot(keys[j], query, preferred_element_type=F32)
            probs = jnp.where(allowed_keys(starts, i, j), jnp.exp(raw - log_row), 0.0)
            probs_grad = jnp.dot(values[j], grad, preferred_element_type=F32)
            scores_grad = (probs * (probs_grad - centre)).astype(BF)
            acc[j, 128:192, :] += dims(grad, probs.astype(BF), 1, 1)
            acc[j, 64:128, :] += dims(query, scores_grad, 1, 1)
            query_grad = query_grad + jnp.dot(
                kept_ref[0, j, 64:128], scores_grad, preferred_element_type=F32
            )
        acc[i, 0:64, :] = query_grad * 0.125
    for step in SHIFTS:
        outs[step][...] = acc[lax.rem(place[0] + step, 4)].astype(BF)


def attend_back(place, came, places, kept, heads_out, log_total):
    return call(
        attend_back_body,
        place,
        (MICRO,),
        [lanes(piece) for piece in came]
        + [lanes(piece) for piece in places]
        + [by_micro(in_hbm(array)) for array in (kept, heads_out, log_total)],
        [lanes_out((192,), BF) for _ in SHIFTS],
        [
            pltpu.VMEM((4, 1, BLOCK), jnp.int32),
            pltpu.VMEM((4, BLOCK, HEAD), BF),
            pltpu.VMEM((4, BLOCK, HEAD), BF),
            pltpu.VMEM((4, HEAD, BLOCK), BF),
            pltpu.VMEM((4, 192, BLOCK), F32),
        ],
        flops=16_000_000_000,
        moved=5_000_000,
    )


def attend_both_body(place, *refs):
    came, places, outs = refs[0:4], refs[4:8], refs[8:12]
    starts, kept, keys, values, acc, out = refs[12:18]
    for step in SHIFTS:
        source = lax.rem(place[0] - step + 4, 4)
        kept[source] = came[step][...]
    put_starts(place, places, starts)
    acc[...] = jnp.zeros_like(acc)
    for j in range(4):
        keys[j] = kept[j, 64:128].T
        values[j] = kept[j, 128:192].T
    for i in range(4):
        query = kept[i, 0:64]
        grad = kept[i, 192:256]
        scores = []
        for j in range(i + 1):
            raw = jnp.dot(keys[j], query, preferred_element_type=F32)
            scores.append(jnp.where(allowed_keys(starts, i, j), raw, MASKED))
        peak = functools.reduce(
            jnp.maximum, [jnp.max(s, axis=0, keepdims=True) for s in scores]
        )
        exps = [jnp.exp(s - peak) for s in scores]
        total = functools.reduce(jnp.add, [jnp.sum(e, axis=0, keepdims=True) for e in exps])
        inverse = 1.0 / total
        result = jnp.zeros((HEAD, BLOCK), F32)
        probs = []
        for j in range(i + 1):
            prob = exps[j] * inverse
            low = prob.astype(BF)
            probs.append(prob)
            result = result + jnp.dot(kept[j, 128:192], low, preferred_element_type=F32)
            acc[j, 128:192, :] += dims(grad, low, 1, 1)
        out[i] = result.astype(BF)
        centre = jnp.sum(grad.astype(F32) * result, axis=0, keepdims=True)
        query_grad = jnp.zeros((HEAD, BLOCK), F32)
        for j in range(i + 1):
            probs_grad = jnp.dot(values[j], grad, preferred_element_type=F32)
            scores_grad = (probs[j] * (probs_grad - centre)).astype(BF)
            acc[j, 64:128, :] += dims(query, scores_grad, 1, 1)
            query_grad = query_grad + jnp.dot(
                kept[j, 64:128], scores_grad, preferred_element_type=F32
            )
        acc[i, 0:64, :] = query_grad * 0.125
    for step in SHIFTS:
        other = lax.rem(place[0] + step, 4)
        outs[step][0:192, :] = acc[other].astype(BF)
        outs[step][192:256, :] = out[other]


def attend_both(place, came, places):
    return call(
        attend_both_body,
        place,
        (MICRO,),
        [lanes(piece) for piece in came] + [lanes(piece) for piece in places],
        [lanes_out((256,), BF) for _ in SHIFTS],
        [
            pltpu.VMEM((4, 1, BLOCK), jnp.int32),
            pltpu.VMEM((4, 256, BLOCK), BF),
            pltpu.VMEM((4, BLOCK, HEAD), BF),
            pltpu.VMEM((4, BLOCK, HEAD), BF),
            pltpu.VMEM((4, 192, BLOCK), F32),
            pltpu.VMEM((4, HEAD, BLOCK), BF),
        ],
        flops=18_000_000_000,
        moved=5_000_000,
    )


def mixed_back_body(with_heads, place, *refs):
    came = refs[0:4]
    wq, wk, wv, norms, turns, states, mlp_grad = refs[4:11]
    out, mixed_ref, sums = refs[11:14]
    cosine, sine = turns[0], turns[1]
    for step in SHIFTS:
        head = lax.rem(place[0] - step + 4, 4)
        at = pl.multiple_of(head * HEAD, HEAD)
        for part in range(3):
            block = came[step][64 * part : 64 * part + 64]
            if part < 2:
                a, b = block[0:8].astype(F32), block[8:16].astype(F32)
                turned = jnp.concatenate(
                    [a * cosine + b * sine, b * cosine - a * sine], axis=0
                ).astype(BF)
                block = jnp.concatenate([turned, block[16:]], axis=0)
            mixed_ref[part, pl.ds(at, HEAD), :] = block
        if with_heads:
            refs[14][pl.ds(at, HEAD), :] = came[step][192:256]
    attn_grad = jnp.zeros((BLOCK, D), F32)
    for part, weight in enumerate((wq, wk, wv)):
        attn_grad = attn_grad + dims(mixed_ref[part], weight[...].reshape(D, 256), 0, 1)
    unit, _ = unit_of(states[...].astype(F32))
    other_grad = mlp_grad[...]
    out[...] = attn_grad * norms[0:1, :] + other_grad * norms[1:2, :]

    @pl.when(pl.program_id(0) == 0)
    def _():
        sums[...] = jnp.zeros_like(sums)

    sums[0:1, :] += jnp.sum(attn_grad * unit, axis=0, keepdims=True)
    sums[1:2, :] += jnp.sum(other_grad * unit, axis=0, keepdims=True)
    sums[2:3, :] += jnp.sum(attn_grad, axis=0, keepdims=True)
    sums[3:4, :] += jnp.sum(other_grad, axis=0, keepdims=True)


def mixed_back(place, came, weights, norms, turns, states, mlp_grad):
    with_heads = came[0].shape[0] == 256
    ins = [lanes(piece) for piece in came]
    ins += qkv_rows(weights)
    ins += [whole(norms), lanes(turns), rows(states), rows(mlp_grad)]
    return call(
        functools.partial(mixed_back_body, with_heads),
        place,
        (MICRO,),
        ins,
        [
            rows_out(D, F32),
            lanes_out((3, 256), BF),
            whole_out((8, D), F32),
        ]
        + [lanes_out((256,), BF)] * with_heads,
        flops=1_500_000_000,
        moved=6_000_000,
    )


def weight_back_body(with_rest, place, attn_in, mixed, sums, *refs):
    pack = refs[-1]
    first = 0
    if with_rest:
        pack[:, 0:256, :] = refs[0][...]
        put_proj(place[1], *refs[1:4], pack, 256)
        first = 288
    for part in range(3):
        product = dims(attn_in[...], mixed[part], 0, 1)
        at = first + 32 * part
        pack[:, at : at + 32, :] = product.astype(BF).reshape(16, 32, 256)
    at = first + 96
    pack[:, at : at + 16, :] = jnp.zeros((16, 16, 256), BF)
    for owner in range(16):
        tile, shift = owner // 4, owner % 4 * 32
        lines = sums[:, 128 * tile : 128 * tile + 128]
        if shift:
            lines = pltpu.roll(lines, 128 - shift, 1)
        lines = jnp.concatenate([lines, jnp.zeros_like(lines)], axis=0).astype(BF)
        pack[owner, at : at + 16, 0:128] = lines


def weight_back(place, attn_in, mixed, sums, rest=()):
    return call(
        functools.partial(weight_back_body, bool(rest)),
        place,
        (1,),
        [whole(attn_in), whole(mixed), whole(sums)]
        + [whole(array) for array in rest[:3]]
        + [half_columns(array) for array in rest[3:]],
        [(kept_in_hbm if rest else tuple)(whole_out((16, 400 if rest else 112, 256), BF))],
        flops=2_000_000_000,
        moved=6_000_000,
    )[0]


def end_body(place, states, grad, own, came, out):
    unit, scaled = unit_of(states[...].astype(F32))
    through = own[...] + came[...]
    back = scaled * (
        through
        - jnp.mean(through, axis=-1, keepdims=True)
        - unit * jnp.mean(through * unit, axis=-1, keepdims=True)
    )
    out[...] = (grad[...].astype(F32) + back).astype(BF)


def end_back(place, states, grad, own, came):
    return call(
        end_body,
        place,
        (MICRO,),
        [rows(states), rows(grad), rows(own), rows(came)],
        [rows_out(D, BF)],
        flops=100_000_000,
        moved=5_000_000,
    )[0]


def scatter_sum(pack):
    return jnp.sum(to_owners(pack).astype(F32), axis=0).astype(BF)


def choose_body(place, *refs):
    keep, send = refs[12:14]
    total = []
    for group in range(3):
        held = refs[4 * group][...].astype(F32)
        for step in range(1, 4):
            held = held + refs[4 * group + step][...].astype(F32)
        total.append(held)
    layer1 = total[0]
    layer0 = jnp.concatenate([total[1], total[2]], axis=0)
    first = place[1] == 0
    keep[...] = jnp.where(first, layer0, layer1)
    send[...] = jnp.where(first, layer1, layer0).astype(BF)


def choose(place, pieces):
    return call(
        choose_body,
        place,
        (1,),
        [whole(piece) for piece in pieces],
        [whole_out((400, 256), F32), whole_out((400, 256), BF)],
    )


def unpack_body(place, keep, got, qkv, proj, up, down, sums, total):
    core = place[1]
    total[core] = keep[...]
    total[1 - core] = got[...].astype(F32)
    low = lax.broadcasted_iota(jnp.int32, (32, 128), 1) < 64
    sums[...] = total[0, 384:392, 0:128] + total[1, 384:392, 0:128]
    for half in range(2):
        for part in range(3):
            at = 512 * part + 256 * half
            qkv[:, at : at + 256] = total[half, 288 + 32 * part : 320 + 32 * part]
        proj[:, 256 * half : 256 * half + 256] = total[half, 256:288]
        for side in range(2):
            down[64 * half : 64 * half + 64, 256 * side : 256 * side + 256] = total[
                half, 128 + 64 * side : 192 + 64 * side
            ]
    for tile in range(16):
        row = 32 * (tile // 4)
        at = 128 * (tile % 4 // 2)
        left = total[0, row : row + 32, at : at + 128]
        right = total[1, row : row + 32, at : at + 128]
        if tile % 2 == 0:
            joined = jnp.where(low, left, pltpu.roll(right, 64, 1))
        else:
            joined = jnp.where(low, pltpu.roll(left, 64, 1), right)
        up[:, 128 * tile : 128 * tile + 128] = joined


def unpack(place, keep, got):
    return call(
        unpack_body,
        place,
        (1,),
        [whole(keep), whole(got)],
        [
            whole_out((32, 1536), F32),
            whole_out((32, 512), F32),
            whole_out((32, 2048), F32),
            whole_out((128, 512), F32),
            whole_out((8, 128), F32),
        ],
        [pltpu.VMEM((2, 400, 256), F32)],
    )


def on_device(
    inputs,
    positions,
    cotangent,
    qkv_weight,
    proj_weight,
    up_weight,
    down_weight,
    norm_gain,
    norm_bias,
):
    core = lax.axis_index("section")
    chip_z = lax.axis_index("seq")
    shard = lax.axis_index("shard")
    first = core == 0
    place = jnp.stack([chip_z, core, shard // 4, shard % 4]).astype(jnp.int32)

    own_norms = jnp.concatenate([norm_gain[0], norm_bias[0]], axis=0).reshape(1, 128)
    mine, other = pack_weights(
        place,
        qkv_weight[0],
        proj_weight[0],
        up_weight[0],
        down_weight[0],
        jnp.broadcast_to(own_norms, (16, 128)),
    )
    early, middle, late = sort_weights(place, mine, swap_core(other))
    places_row = positions.reshape(1, TOKENS)
    gathered, places = lax.optimization_barrier(
        (to_owners(early), regroup([places_row] * 4))
    )
    middle_all = lax.all_gather(middle, "shard")
    late_all = lax.all_gather(late, "shard")
    norms = (
        gathered[:, 96, :]
        .reshape(16, 2, 4, 32)
        .transpose(1, 2, 0, 3)
        .reshape(2, 4, D)
        .astype(F32)
    )
    qkv_of = ((gathered, 0), (middle_all, 12))
    proj_of = ((middle_all, 4), (middle_all, 5))
    mlp_of = (middle_all, late_all)
    rates = 10000.0 ** (-jnp.arange(ROT // 2, dtype=F32) * 2.0 / ROT)
    angles = rates[:, None] * places_row.astype(F32)
    turns = jnp.stack([jnp.cos(angles), jnp.sin(angles)])

    states = inputs.reshape(TOKENS, D)
    grad = cotangent.reshape(TOKENS, D)
    extra = ()
    saved = []
    for layer in range(2):
        done = before_layer(place, states, extra, qkv_of[layer], norms[layer], turns)
        sent, attn_in, mlp_in = done[0:4], done[4], done[5]
        if layer == 1:
            states = done[6]
        came = regroup(sent)
        if layer == 1:
            sent = attend_both(place, came, places)
            mlp_in = after(mlp_in, sent)
            came = regroup(sent)
        mlp_out, active, slope = mlp_layer(place, mlp_in, mlp_of[layer])
        if layer == 0:
            done = attend(place, came, places)
            kept, heads_out, log_total = done[4:7]
            came = regroup(done[0:4])
        part, heads = after_layer(place, came, 3 * layer, proj_of[layer], mlp_out)
        parts = (part, swap_core(part))
        extra = (parts, grad, proj_of[1])
        saved.append((states, attn_in, mlp_in, active, slope, (heads, swap_core(heads))))
    result = (states.astype(F32) + (parts[0] + parts[1])).astype(BF)
    layer_out = jnp.where(first, saved[1][0], result)

    grads = [None, None]
    for layer in (1, 0):
        states, attn_in, mlp_in, active, slope, heads = saved[layer]
        if layer == 1:
            mlp_grad, pack = mlp_back(place, grad, active, slope, mlp_in, mlp_of[1])
        else:
            sent = heads_grad(place, grad, proj_of[0])
            came = regroup(sent)
            mlp_grad, pack = mlp_back(
                place, after(grad, sent), active, slope, mlp_in, mlp_of[0], heads
            )
            came = after(came, pack)
            sent = attend_back(place, came, places, kept, heads_out, log_total)
            sum_a = scatter_sum(pack)
            came = regroup(sent)
        through, mixed, norm_sums, *heads_of = mixed_back(
            place, came, qkv_of[layer], norms[layer], turns, states, mlp_grad
        )
        if layer == 1:
            pack = weight_back(place, attn_in, mixed, norm_sums, (pack, heads_of[0], swap_core(heads_of[0]), grad))
            total = lax.psum_scatter(pack, "shard", scatter_dimension=0, tiled=False)
            through = after(through, pack)
        else:
            pack, sum_a = lax.optimization_barrier(
                (weight_back(place, attn_in, mixed, norm_sums), sum_a)
            )
            pieces_a = regroup([sum_a] * 4)
            pieces_b = regroup([scatter_sum(pack)] * 4)
        grad = end_back(place, states, grad, through, swap_core(through))
        grads[layer] = grad
    grads_out = jnp.where(first, grads[0], grads[1])

    keep, send = choose(place, regroup([total] * 4) + pieces_a + pieces_b)
    qkv_grad, proj_grad, up_grad, down_grad, norm_sums = unpack(place, keep, swap_core(send))
    return (
        layer_out.reshape(1, MICRO, 1, BLOCK, D),
        grads_out.reshape(1, MICRO, 1, BLOCK, D),
        qkv_grad[None],
        proj_grad[None],
        up_grad[None],
        down_grad[None],
        norm_sums[None, 0:2, 0:32],
        norm_sums[None, 2:4, 0:32],
    )


def solution(mesh):
    placed = (
        P(None, "shard", "seq", None),
        P(None, "shard", "seq"),
        P(None, "shard", "seq", None),
        P("section", "shard", None),
        P("section", "shard", None),
        P("section", "shard", None),
        P("section", "shard", None),
        P("section", None, "shard"),
        P("section", None, "shard"),
    )
    return jax.shard_map(
        on_device,
        mesh=mesh,
        in_specs=placed,
        out_specs=(
            P("section", None, "shard", "seq", None),
            P("section", None, "shard", "seq", None),
            P("section", "shard", None),
            P("section", "shard", None),
            P("section", "shard", None),
            P("section", "shard", None),
            P("section", None, "shard"),
            P("section", None, "shard"),
        ),
        check_vma=False,
    )
```

```python
import functools

import jax
import jax.numpy as jnp
from jax import lax
from jax.experimental import pallas as pl
from jax.experimental.pallas import tpu as pltpu
from jax.sharding import PartitionSpec as P

D = 512
HEADS = 8
HEAD = 64
ROT = 16
MICRO = 3
BLOCK = 256
TOKENS = MICRO * BLOCK
NORM_EPS = 1e-05
MASKED = -1e30
BF = jnp.bfloat16
F32 = jnp.float32
SHIFTS = (0, 1, 2, 3)
VMEM_LIMIT = 24 * 1024 * 1024


def dims(left, right, left_dim, right_dim):
    return lax.dot_general(
        left, right, (((left_dim,), (right_dim,)), ((), ())), preferred_element_type=F32
    )


def struct(shape, dtype):
    return jax.ShapeDtypeStruct(shape, dtype)


def in_hbm(array):
    return pltpu.with_memory_space_constraint(array, pltpu.HBM)


def call(body, place, grid, ins, outs, scratch=(), flops=10**9, moved=4 * 10**6):
    specs = [pl.BlockSpec(block, index) for _, block, index in ins]
    out_specs = [pl.BlockSpec(out[2], out[3]) for out in outs]
    return pl.pallas_call(
        body,
        out_shape=[
            (pltpu.HBM if out[4:] else struct)(out[0], out[1]) for out in outs
        ],
        grid_spec=pltpu.PrefetchScalarGridSpec(
            num_scalar_prefetch=1,
            grid=grid,
            in_specs=specs,
            out_specs=out_specs,
            scratch_shapes=list(scratch),
        ),
        compiler_params=pltpu.CompilerParams(
            vmem_limit_bytes=VMEM_LIMIT, dimension_semantics=("arbitrary",) * len(grid)
        ),
        cost_estimate=pl.CostEstimate(flops=flops, bytes_accessed=moved, transcendentals=0),
    )(place, *[array for array, _, _ in ins])


def whole(array):
    rank = array.ndim
    return (array, array.shape, lambda *_: (0,) * rank)


def whole_out(shape, dtype):
    rank = len(shape)
    return (shape, dtype, shape, lambda *_: (0,) * rank)


def kept_in_hbm(out):
    return out + (True,)


def rows(array):
    return (array, (BLOCK, array.shape[1]), lambda m, _: (m, 0))


def rows_out(width, dtype):
    return ((TOKENS, width), dtype, (BLOCK, width), lambda m, _: (m, 0))


def lanes(array):
    lead = array.shape[:-1]
    rank = len(lead)
    return (array, lead + (BLOCK,), lambda m, _: (0,) * rank + (m,))


def lanes_out(lead, dtype):
    rank = len(lead)
    return (lead + (TOKENS,), dtype, lead + (BLOCK,), lambda m, _: (0,) * rank + (m,))


def by_micro(array):
    rank = array.ndim - 1
    return (array, (1,) + array.shape[1:], lambda m, _: (m,) + (0,) * rank)


def by_micro_out(shape, dtype):
    rank = len(shape) - 1
    return (shape, dtype, (1,) + shape[1:], lambda m, _: (m,) + (0,) * rank)


def pack_body(place, qkv, proj, up, down, norms, mine, other, held):
    low = lax.broadcasted_iota(jnp.int32, (32, 128), 1) < 64
    for half in range(2):
        for pair in range(8):
            first = up[:, 256 * pair : 256 * pair + 128].astype(F32)
            second = up[:, 256 * pair + 128 : 256 * pair + 256].astype(F32)
            if half == 0:
                cut = jnp.where(low, first, pltpu.roll(second, 64, 1))
            else:
                cut = jnp.where(low, pltpu.roll(first, 64, 1), second)
            at = 128 * (pair % 2)
            held[half, 32 * (pair // 2) : 32 * (pair // 2) + 32, at : at + 128] = cut.astype(BF)
        for side in range(2):
            held[half, 128 + 64 * side : 192 + 64 * side, :] = down[
                64 * half : 64 * half + 64, 256 * side : 256 * side + 256
            ]
            held[half, 256 + 32 * side : 288 + 32 * side, :] = proj[
                :, 256 * side : 256 * side + 256
            ]
        for part in range(3):
            at = 512 * part + 256 * half
            held[half, 320 + 32 * part : 352 + 32 * part, :] = qkv[:, at : at + 256]
        held[half, 416:432, 0:128] = norms[...]
        held[half, 416:432, 128:256] = norms[...]
    core = place[1]
    mine[...] = held[core]
    other[...] = held[1 - core]


def pack_weights(place, qkv, proj, up, down, norms):
    return call(
        pack_body,
        place,
        (1,),
        [whole(in_hbm(array)) for array in (qkv, proj, up, down)] + [whole(norms)],
        [whole_out((432, 256), BF), whole_out((432, 256), BF)],
        [pltpu.VMEM((2, 432, 256), BF)],
    )


def sort_body(place, mine, received, early, middle, late):
    first = place[1] == 0
    kept = mine[...]
    came = received[...]
    layer0 = jnp.where(first, kept, came)
    layer1 = jnp.where(first, came, kept)
    norms = jnp.concatenate([layer0[416:432, 0:128], layer1[416:432, 0:128]], axis=1)
    for peer in range(16):
        early[peer, 0:96, :] = layer0[320:416]
        early[peer, 96:112, :] = norms
    middle[0:320, :] = layer0[0:320]
    middle[320:480, :] = layer1[256:416]
    late[...] = layer1[0:256]


def sort_weights(place, mine, received):
    return call(
        sort_body,
        place,
        (1,),
        [whole(mine), whole(received)],
        [whole_out(shape, BF) for shape in ((16, 112, 256), (480, 256), (256, 256))],
    )


def shift_z(value, step):
    return lax.ppermute(value, "seq", [(z, (z + step) % 4) for z in range(4)])


def swap_core(value):
    return lax.ppermute(value, "section", [(0, 1), (1, 0)])


def to_owners(pack):
    return lax.all_to_all(pack, "shard", 0, 0, tiled=True)


def after(value, *others):
    return lax.optimization_barrier((value, others))[0]


def regroup(values):
    got = {0: values[0]}
    for step in (1, 3, 2):
        got[step] = shift_z(values[step], step)
    return [got[step] for step in SHIFTS]


def unit_of(states):
    centre = states - jnp.mean(states, axis=-1, keepdims=True)
    scaled = lax.rsqrt(jnp.mean(centre * centre, axis=-1, keepdims=True) + NORM_EPS)
    return centre * scaled, scaled


def qkv_rows(weights):
    array, first = weights
    return [
        (array, (16, 32, 256), functools.partial(lambda at, m, _: (0, at, 0), first + part))
        for part in range(3)
    ]


def proj_rows(weights):
    array, first = weights
    return (array, (8, 64, 256), lambda m, place: (place[1], first, 0))


def put_heads_grad(grad, proj, held, first):
    weight = proj[...]
    total = dims(weight[:, 0:32].reshape(256, 256), grad[:, 0:256], 1, 1) + dims(
        weight[:, 32:64].reshape(256, 256), grad[:, 256:512], 1, 1
    )
    for head in range(4):
        held[head, first : first + 64, :] = total[64 * head : 64 * head + 64].astype(BF)


def before_body(second, place, *refs):
    refs = list(refs)
    states = refs.pop(0)[...].astype(F32)
    if second:
        part_a, part_b, grad, proj = [refs.pop(0) for _ in range(4)]
        states = (states + (part_a[...] + part_b[...])).astype(BF)
    wq, wk, wv, norms, turns = refs[:5]
    outs = refs[5:9]
    attn_ref, mlp_ref = refs[9:11]
    held = refs[-1]
    if second:
        refs[11][...] = states
        states = states.astype(F32)
    unit, _ = unit_of(states)
    attn_in = (unit * norms[0:1, :] + norms[2:3, :]).astype(BF)
    attn_ref[...] = attn_in
    mlp_ref[...] = (unit * norms[1:2, :] + norms[3:4, :]).astype(BF)
    cosine, sine = turns[0], turns[1]
    for part, weight in enumerate((wq, wk, wv)):
        mixed = dims(weight[...].reshape(D, 256), attn_in, 0, 1)
        for head in range(4):
            block = mixed[64 * head : 64 * head + 64]
            if part < 2:
                a, b = block[0:8], block[8:16]
                block = jnp.concatenate(
                    [a * cosine - b * sine, b * cosine + a * sine, block[16:]], axis=0
                )
            if part == 0:
                block = block * 0.125
            held[head, 64 * part : 64 * part + 64, :] = block.astype(BF)
    if second:
        put_heads_grad(grad, proj, held, 192)
    for step in SHIFTS:
        outs[step][...] = held[lax.rem(place[0] + step, 4)]


def before_layer(place, states, extra, weights, norms, turns):
    array, first = weights
    ins = [rows(states)]
    depth = 192
    if extra:
        parts, grad, proj = extra
        ins += [rows(parts[0]), rows(parts[1]), rows(grad), proj_rows(proj)]
        depth = 256
    ins += qkv_rows(weights)
    ins += [whole(norms), lanes(turns)]
    outs = [lanes_out((depth,), BF) for _ in SHIFTS]
    outs += [kept_in_hbm(rows_out(D, BF)), kept_in_hbm(rows_out(D, BF))]
    if extra:
        outs.append(kept_in_hbm(rows_out(D, BF)))
    return call(
        functools.partial(before_body, bool(extra)),
        place,
        (MICRO,),
        ins,
        outs,
        [pltpu.VMEM((4, depth, BLOCK), BF)],
        flops=1_200_000_000,
        moved=6_000_000,
    )


def mlp_body(place, mlp_in, up, down, out, active_ref, slope_ref):
    step = pl.program_id(0)
    hidden = jnp.dot(mlp_in[...], up[...].reshape(D, 256), preferred_element_type=F32)
    cdf = 0.5 * (1.0 + lax.erf(hidden * 0.7071067811865476))
    pdf = jnp.exp(-0.5 * hidden * hidden) * 0.3989422804014327
    active = (hidden * cdf).astype(BF)
    active_ref[...] = active
    slope_ref[...] = cdf + hidden * pdf
    lower = down[...]
    both = jnp.concatenate(
        [lower[:, 0:64].reshape(256, 256), lower[:, 64:128].reshape(256, 256)], axis=1
    )
    product = jnp.dot(active, both, preferred_element_type=F32)

    @pl.when(step == 0)
    def _():
        out[...] = product

    @pl.when(step > 0)
    def _():
        out[...] += product


def mlp_layer(place, mlp_in, weights):
    return call(
        mlp_body,
        place,
        (4,),
        [
            whole(mlp_in),
            (in_hbm(weights), (16, 32, 256), lambda b, _: (0, b, 0)),
            (in_hbm(weights), (4, 128, 256), lambda b, _: (b, 1, 0)),
        ],
        [
            whole_out((TOKENS, D), F32),
            kept_in_hbm(((TOKENS, 1024), BF, (TOKENS, 256), lambda b, _: (0, b))),
            kept_in_hbm(((TOKENS, 1024), F32, (TOKENS, 256), lambda b, _: (0, b))),
        ],
        flops=6_000_000_000,
        moved=12_000_000,
    )


def put_starts(place, places, starts):
    along = lax.broadcasted_iota(jnp.int32, (1, BLOCK), 1)
    for step in SHIFTS:
        source = lax.rem(place[0] - step + 4, 4)
        starts[source] = along + BLOCK * source - places[step][...]


def allowed_keys(starts, query_block, key_block):
    keys = lax.broadcasted_iota(jnp.int32, (BLOCK, BLOCK), 0) + BLOCK * key_block
    allowed = keys >= starts[query_block]
    if query_block == key_block:
        queries = lax.broadcasted_iota(jnp.int32, (BLOCK, BLOCK), 1) + BLOCK * query_block
        allowed = allowed & (keys <= queries)
    return allowed


def attend_body(place, *refs):
    came, places = refs[0:4], refs[4:8]
    outs = refs[8:12]
    kept, heads_out, log_total = refs[12:15]
    starts, keys = refs[15:17]
    for step in SHIFTS:
        source = lax.rem(place[0] - step + 4, 4)
        kept[0, source] = came[step][...]
    put_starts(place, places, starts)
    for j in range(4):
        keys[j] = kept[0, j, 64:128].T
    for i in range(4):
        query = kept[0, i, 0:64]
        scores = []
        for j in range(i + 1):
            raw = jnp.dot(keys[j], query, preferred_element_type=F32)
            scores.append(jnp.where(allowed_keys(starts, i, j), raw, MASKED))
        peak = functools.reduce(
            jnp.maximum, [jnp.max(s, axis=0, keepdims=True) for s in scores]
        )
        total = jnp.zeros((1, BLOCK), F32)
        acc = jnp.zeros((HEAD, BLOCK), F32)
        for j in range(i + 1):
            probs = jnp.exp(scores[j] - peak)
            total = total + jnp.sum(probs, axis=0, keepdims=True)
            acc = acc + jnp.dot(
                kept[0, j, 128:192], probs.astype(BF), preferred_element_type=F32
            )
        heads_out[0, i] = (acc / total).astype(BF)
        log_total[0, i] = peak + jnp.log(total)
    for step in SHIFTS:
        outs[step][...] = heads_out[0, lax.rem(place[0] + step, 4)]


def attend(place, came, places):
    return call(
        attend_body,
        place,
        (MICRO,),
        [lanes(piece) for piece in came] + [lanes(piece) for piece in places],
        [lanes_out((HEAD,), BF) for _ in SHIFTS]
        + [
            kept_in_hbm(by_micro_out((MICRO, 4, 192, BLOCK), BF)),
            kept_in_hbm(by_micro_out((MICRO, 4, HEAD, BLOCK), BF)),
            kept_in_hbm(by_micro_out((MICRO, 4, 1, BLOCK), F32)),
        ],
        [pltpu.VMEM((4, 1, BLOCK), jnp.int32), pltpu.VMEM((4, BLOCK, HEAD), BF)],
        flops=8_000_000_000,
        moved=4_000_000,
    )


def after_body(place, *refs):
    came = refs[0:4]
    proj, mlp_out, out, heads = refs[4:8]
    for step in SHIFTS:
        source = lax.rem(place[0] - step + 4, 4)
        at = pl.multiple_of(source * HEAD, HEAD)
        heads[pl.ds(at, HEAD), :] = came[step][...]
    held = heads[...]
    weight = proj[...]
    for side in range(2):
        span = slice(256 * side, 256 * side + 256)
        product = dims(held, weight[:, 32 * side : 32 * side + 32].reshape(256, 256), 0, 0)
        out[:, span] = mlp_out[:, span] + product


def after_layer(place, came, first, proj, mlp_out):
    return call(
        after_body,
        place,
        (MICRO,),
        [(piece, (HEAD, BLOCK), lambda m, _: (first, m)) for piece in came]
        + [proj_rows(proj), rows(mlp_out)],
        [rows_out(D, F32), lanes_out((256,), BF)],
        flops=800_000_000,
        moved=4_000_000,
    )


def heads_grad_body(place, grad, proj, *refs):
    outs, held = refs[0:4], refs[4]
    put_heads_grad(grad, proj, held, 0)
    for step in SHIFTS:
        outs[step][...] = held[lax.rem(place[0] + step, 4)]


def heads_grad(place, grad, proj):
    return call(
        heads_grad_body,
        place,
        (MICRO,),
        [rows(grad), proj_rows(proj)],
        [lanes_out((HEAD,), BF) for _ in SHIFTS],
        [pltpu.VMEM((4, HEAD, BLOCK), BF)],
        flops=800_000_000,
        moved=2_000_000,
    )


def put_proj(core, heads, other_heads, half_grad, pack, first):
    for side, held in ((core, heads), (1 - core, other_heads)):
        part = jnp.dot(held[...], half_grad[...], preferred_element_type=F32)
        pack[pl.ds(8 * side, 8), first : first + 32, :] = part.astype(BF).reshape(8, 32, 256)


def half_columns(grad):
    return (grad, (TOKENS, 256), lambda m, place: (0, place[1]))


def mlp_back_body(with_proj, place, grad, active, slope, mlp_in, up, down, *refs):
    out, pack = refs[-2:]
    step = pl.program_id(0)
    lower = down[...]
    both = jnp.concatenate(
        [lower[:, 0:64].reshape(256, 256), lower[:, 64:128].reshape(256, 256)], axis=1
    )
    active_grad = dims(grad[...], both, 1, 1)
    hidden_grad = (active_grad * slope[...]).astype(BF)
    product = dims(hidden_grad, up[...].reshape(D, 256), 1, 1)

    @pl.when(step == 0)
    def _():
        out[...] = product
        if with_proj:
            put_proj(place[1], *refs[:3], pack, 256)

    @pl.when(step > 0)
    def _():
        out[...] += product

    up_part = dims(mlp_in[...], hidden_grad, 0, 0).astype(BF).reshape(16, 32, 256)
    pack[:, pl.ds(pl.multiple_of(32 * step, 32), 32), :] = up_part
    down_part = dims(active[...], grad[...], 0, 0).astype(BF)
    for side in range(2):
        pack[pl.ds(4 * step, 4), 128 + 64 * side : 192 + 64 * side, :] = down_part[
            :, 256 * side : 256 * side + 256
        ].reshape(4, 64, 256)


def mlp_back(place, grad, active, slope, mlp_in, weights, heads=()):
    ins = [
        whole(grad),
        (in_hbm(active), (TOKENS, 256), lambda b, _: (0, b)),
        (in_hbm(slope), (TOKENS, 256), lambda b, _: (0, b)),
        whole(mlp_in),
        (in_hbm(weights), (16, 32, 256), lambda b, _: (0, b, 0)),
        (in_hbm(weights), (4, 128, 256), lambda b, _: (b, 1, 0)),
    ]
    depth = 256
    if heads:
        ins += [whole(array) for array in heads] + [half_columns(grad)]
        depth = 288
    return call(
        functools.partial(mlp_back_body, bool(heads)),
        place,
        (4,),
        ins,
        [whole_out((TOKENS, D), F32), whole_out((16, depth, 256), BF)],
        flops=8_000_000_000,
        moved=14_000_000,
    )


def attend_back_body(place, *refs):
    came, places = refs[0:4], refs[4:8]
    kept_ref, heads_out, log_total = refs[8:11]
    outs = refs[11:15]
    starts, keys, values, grads, acc = refs[15:20]
    for step in SHIFTS:
        source = lax.rem(place[0] - step + 4, 4)
        grads[source] = came[step][...]
    put_starts(place, places, starts)
    acc[...] = jnp.zeros_like(acc)
    for j in range(4):
        keys[j] = kept_ref[0, j, 64:128].T
        values[j] = kept_ref[0, j, 128:192].T
    for i in range(4):
        query = kept_ref[0, i, 0:64]
        grad = grads[i]
        log_row = log_total[0, i]
        centre = jnp.sum(
            grad.astype(F32) * heads_out[0, i].astype(F32), axis=0, keepdims=True
        )
        query_grad = jnp.zeros((HEAD, BLOCK), F32)
        for j in range(i + 1):
            raw = jnp.dot(keys[j], query, preferred_element_type=F32)
            probs = jnp.where(allowed_keys(starts, i, j), jnp.exp(raw - log_row), 0.0)
            probs_grad = jnp.dot(values[j], grad, preferred_element_type=F32)
            scores_grad = (probs * (probs_grad - centre)).astype(BF)
            acc[j, 128:192, :] += dims(grad, probs.astype(BF), 1, 1)
            acc[j, 64:128, :] += dims(query, scores_grad, 1, 1)
            query_grad = query_grad + jnp.dot(
                kept_ref[0, j, 64:128], scores_grad, preferred_element_type=F32
            )
        acc[i, 0:64, :] = query_grad * 0.125
    for step in SHIFTS:
        outs[step][...] = acc[lax.rem(place[0] + step, 4)].astype(BF)


def attend_back(place, came, places, kept, heads_out, log_total):
    return call(
        attend_back_body,
        place,
        (MICRO,),
        [lanes(piece) for piece in came]
        + [lanes(piece) for piece in places]
        + [by_micro(in_hbm(array)) for array in (kept, heads_out, log_total)],
        [lanes_out((192,), BF) for _ in SHIFTS],
        [
            pltpu.VMEM((4, 1, BLOCK), jnp.int32),
            pltpu.VMEM((4, BLOCK, HEAD), BF),
            pltpu.VMEM((4, BLOCK, HEAD), BF),
            pltpu.VMEM((4, HEAD, BLOCK), BF),
            pltpu.VMEM((4, 192, BLOCK), F32),
        ],
        flops=16_000_000_000,
        moved=5_000_000,
    )


def attend_both_body(place, *refs):
    came, places, outs = refs[0:4], refs[4:8], refs[8:12]
    starts, kept, keys, values, acc, out = refs[12:18]
    for step in SHIFTS:
        source = lax.rem(place[0] - step + 4, 4)
        kept[source] = came[step][...]
    put_starts(place, places, starts)
    acc[...] = jnp.zeros_like(acc)
    for j in range(4):
        keys[j] = kept[j, 64:128].T
        values[j] = kept[j, 128:192].T
    for i in range(4):
        query = kept[i, 0:64]
        grad = kept[i, 192:256]
        scores = []
        for j in range(i + 1):
            raw = jnp.dot(keys[j], query, preferred_element_type=F32)
            scores.append(jnp.where(allowed_keys(starts, i, j), raw, MASKED))
        peak = functools.reduce(
            jnp.maximum, [jnp.max(s, axis=0, keepdims=True) for s in scores]
        )
        exps = [jnp.exp(s - peak) for s in scores]
        total = functools.reduce(jnp.add, [jnp.sum(e, axis=0, keepdims=True) for e in exps])
        inverse = 1.0 / total
        result = jnp.zeros((HEAD, BLOCK), F32)
        probs = []
        for j in range(i + 1):
            prob = exps[j] * inverse
            low = prob.astype(BF)
            probs.append(prob)
            result = result + jnp.dot(kept[j, 128:192], low, preferred_element_type=F32)
            acc[j, 128:192, :] += dims(grad, low, 1, 1)
        out[i] = result.astype(BF)
        centre = jnp.sum(grad.astype(F32) * result, axis=0, keepdims=True)
        query_grad = jnp.zeros((HEAD, BLOCK), F32)
        for j in range(i + 1):
            probs_grad = jnp.dot(values[j], grad, preferred_element_type=F32)
            scores_grad = (probs[j] * (probs_grad - centre)).astype(BF)
            acc[j, 64:128, :] += dims(query, scores_grad, 1, 1)
            query_grad = query_grad + jnp.dot(
                kept[j, 64:128], scores_grad, preferred_element_type=F32
            )
        acc[i, 0:64, :] = query_grad * 0.125
    for step in SHIFTS:
        other = lax.rem(place[0] + step, 4)
        outs[step][0:192, :] = acc[other].astype(BF)
        outs[step][192:256, :] = out[other]


def attend_both(place, came, places):
    return call(
        attend_both_body,
        place,
        (MICRO,),
        [lanes(piece) for piece in came] + [lanes(piece) for piece in places],
        [lanes_out((256,), BF) for _ in SHIFTS],
        [
            pltpu.VMEM((4, 1, BLOCK), jnp.int32),
            pltpu.VMEM((4, 256, BLOCK), BF),
            pltpu.VMEM((4, BLOCK, HEAD), BF),
            pltpu.VMEM((4, BLOCK, HEAD), BF),
            pltpu.VMEM((4, 192, BLOCK), F32),
            pltpu.VMEM((4, HEAD, BLOCK), BF),
        ],
        flops=18_000_000_000,
        moved=5_000_000,
    )


def mixed_back_body(with_heads, place, *refs):
    came = refs[0:4]
    wq, wk, wv, norms, turns, states, mlp_grad = refs[4:11]
    out, mixed_ref, sums = refs[11:14]
    cosine, sine = turns[0], turns[1]
    for step in SHIFTS:
        head = lax.rem(place[0] - step + 4, 4)
        at = pl.multiple_of(head * HEAD, HEAD)
        for part in range(3):
            block = came[step][64 * part : 64 * part + 64]
            if part < 2:
                a, b = block[0:8].astype(F32), block[8:16].astype(F32)
                turned = jnp.concatenate(
                    [a * cosine + b * sine, b * cosine - a * sine], axis=0
                ).astype(BF)
                block = jnp.concatenate([turned, block[16:]], axis=0)
            mixed_ref[part, pl.ds(at, HEAD), :] = block
        if with_heads:
            refs[14][pl.ds(at, HEAD), :] = came[step][192:256]
    attn_grad = jnp.zeros((BLOCK, D), F32)
    for part, weight in enumerate((wq, wk, wv)):
        attn_grad = attn_grad + dims(mixed_ref[part], weight[...].reshape(D, 256), 0, 1)
    unit, _ = unit_of(states[...].astype(F32))
    other_grad = mlp_grad[...]
    out[...] = attn_grad * norms[0:1, :] + other_grad * norms[1:2, :]

    @pl.when(pl.program_id(0) == 0)
    def _():
        sums[...] = jnp.zeros_like(sums)

    sums[0:1, :] += jnp.sum(attn_grad * unit, axis=0, keepdims=True)
    sums[1:2, :] += jnp.sum(other_grad * unit, axis=0, keepdims=True)
    sums[2:3, :] += jnp.sum(attn_grad, axis=0, keepdims=True)
    sums[3:4, :] += jnp.sum(other_grad, axis=0, keepdims=True)


def mixed_back(place, came, weights, norms, turns, states, mlp_grad):
    with_heads = came[0].shape[0] == 256
    ins = [lanes(piece) for piece in came]
    ins += qkv_rows(weights)
    ins += [whole(norms), lanes(turns), rows(states), rows(mlp_grad)]
    return call(
        functools.partial(mixed_back_body, with_heads),
        place,
        (MICRO,),
        ins,
        [
            kept_in_hbm(rows_out(D, F32)),
            lanes_out((3, 256), BF),
            whole_out((8, D), F32),
        ]
        + [lanes_out((256,), BF)] * with_heads,
        flops=1_500_000_000,
        moved=6_000_000,
    )


def weight_back_body(with_rest, place, attn_in, mixed, sums, *refs):
    pack = refs[-1]
    first = 0
    if with_rest:
        pack[:, 0:256, :] = refs[0][...]
        put_proj(place[1], *refs[1:4], pack, 256)
        first = 288
    for part in range(3):
        product = dims(attn_in[...], mixed[part], 0, 1)
        at = first + 32 * part
        pack[:, at : at + 32, :] = product.astype(BF).reshape(16, 32, 256)
    at = first + 96
    pack[:, at : at + 16, :] = jnp.zeros((16, 16, 256), BF)
    for owner in range(16):
        tile, shift = owner // 4, owner % 4 * 32
        lines = sums[:, 128 * tile : 128 * tile + 128]
        if shift:
            lines = pltpu.roll(lines, 128 - shift, 1)
        lines = jnp.concatenate([lines, jnp.zeros_like(lines)], axis=0).astype(BF)
        pack[owner, at : at + 16, 0:128] = lines


def weight_back(place, attn_in, mixed, sums, rest=()):
    return call(
        functools.partial(weight_back_body, bool(rest)),
        place,
        (1,),
        [whole(attn_in), whole(mixed), whole(sums)]
        + [whole(array) for array in rest[:3]]
        + [half_columns(array) for array in rest[3:]],
        [(kept_in_hbm if rest else tuple)(whole_out((16, 400 if rest else 112, 256), BF))],
        flops=2_000_000_000,
        moved=6_000_000,
    )[0]


def end_body(place, states, grad, own, came, out):
    unit, scaled = unit_of(states[...].astype(F32))
    through = own[...] + came[...]
    back = scaled * (
        through
        - jnp.mean(through, axis=-1, keepdims=True)
        - unit * jnp.mean(through * unit, axis=-1, keepdims=True)
    )
    out[...] = (grad[...].astype(F32) + back).astype(BF)


def end_back(place, states, grad, own, came):
    return call(
        end_body,
        place,
        (MICRO,),
        [rows(states), rows(grad), rows(own), rows(came)],
        [rows_out(D, BF)],
        flops=100_000_000,
        moved=5_000_000,
    )[0]


def scatter_sum(pack):
    return jnp.sum(to_owners(pack).astype(F32), axis=0).astype(BF)


def choose_body(place, *refs):
    keep, send = refs[12:14]
    total = []
    for group in range(3):
        held = refs[4 * group][...].astype(F32)
        for step in range(1, 4):
            held = held + refs[4 * group + step][...].astype(F32)
        total.append(held)
    layer1 = total[0]
    layer0 = jnp.concatenate([total[1], total[2]], axis=0)
    first = place[1] == 0
    keep[...] = jnp.where(first, layer0, layer1)
    send[...] = jnp.where(first, layer1, layer0).astype(BF)


def choose(place, pieces):
    return call(
        choose_body,
        place,
        (1,),
        [whole(piece) for piece in pieces],
        [whole_out((400, 256), F32), whole_out((400, 256), BF)],
    )


def unpack_body(place, keep, got, qkv, proj, up, down, sums, total):
    core = place[1]
    total[core] = keep[...]
    total[1 - core] = got[...].astype(F32)
    low = lax.broadcasted_iota(jnp.int32, (32, 128), 1) < 64
    sums[...] = total[0, 384:392, 0:128] + total[1, 384:392, 0:128]
    for half in range(2):
        for part in range(3):
            at = 512 * part + 256 * half
            qkv[:, at : at + 256] = total[half, 288 + 32 * part : 320 + 32 * part]
        proj[:, 256 * half : 256 * half + 256] = total[half, 256:288]
        for side in range(2):
            down[64 * half : 64 * half + 64, 256 * side : 256 * side + 256] = total[
                half, 128 + 64 * side : 192 + 64 * side
            ]
    for tile in range(16):
        row = 32 * (tile // 4)
        at = 128 * (tile % 4 // 2)
        left = total[0, row : row + 32, at : at + 128]
        right = total[1, row : row + 32, at : at + 128]
        if tile % 2 == 0:
            joined = jnp.where(low, left, pltpu.roll(right, 64, 1))
        else:
            joined = jnp.where(low, pltpu.roll(left, 64, 1), right)
        up[:, 128 * tile : 128 * tile + 128] = joined


def unpack(place, keep, got):
    return call(
        unpack_body,
        place,
        (1,),
        [whole(keep), whole(got)],
        [
            whole_out((32, 1536), F32),
            whole_out((32, 512), F32),
            whole_out((32, 2048), F32),
            whole_out((128, 512), F32),
            whole_out((8, 128), F32),
        ],
        [pltpu.VMEM((2, 400, 256), F32)],
    )


def on_device(
    inputs,
    positions,
    cotangent,
    qkv_weight,
    proj_weight,
    up_weight,
    down_weight,
    norm_gain,
    norm_bias,
):
    core = lax.axis_index("section")
    chip_z = lax.axis_index("seq")
    shard = lax.axis_index("shard")
    first = core == 0
    place = jnp.stack([chip_z, core, shard // 4, shard % 4]).astype(jnp.int32)

    own_norms = jnp.concatenate([norm_gain[0], norm_bias[0]], axis=0).reshape(1, 128)
    mine, other = pack_weights(
        place,
        qkv_weight[0],
        proj_weight[0],
        up_weight[0],
        down_weight[0],
        jnp.broadcast_to(own_norms, (16, 128)),
    )
    early, middle, late = sort_weights(place, mine, swap_core(other))
    places_row = positions.reshape(1, TOKENS)
    gathered, places = lax.optimization_barrier(
        (to_owners(early), regroup([places_row] * 4))
    )
    middle_all = lax.all_gather(middle, "shard")
    late_all = lax.all_gather(late, "shard")
    norms = (
        gathered[:, 96, :]
        .reshape(16, 2, 4, 32)
        .transpose(1, 2, 0, 3)
        .reshape(2, 4, D)
        .astype(F32)
    )
    qkv_of = ((gathered, 0), (middle_all, 12))
    proj_of = ((middle_all, 4), (middle_all, 5))
    mlp_of = (middle_all, late_all)
    rates = 10000.0 ** (-jnp.arange(ROT // 2, dtype=F32) * 2.0 / ROT)
    angles = rates[:, None] * places_row.astype(F32)
    turns = jnp.stack([jnp.cos(angles), jnp.sin(angles)])

    states = inputs.reshape(TOKENS, D)
    grad = cotangent.reshape(TOKENS, D)
    extra = ()
    saved = []
    for layer in range(2):
        done = before_layer(place, states, extra, qkv_of[layer], norms[layer], turns)
        sent, attn_in, mlp_in = done[0:4], done[4], done[5]
        if layer == 1:
            states = done[6]
        came = regroup(sent)
        if layer == 1:
            sent = attend_both(place, came, places)
            mlp_in = after(mlp_in, sent)
            came = regroup(sent)
        mlp_out, active, slope = mlp_layer(place, mlp_in, mlp_of[layer])
        if layer == 0:
            done = attend(place, came, places)
            kept, heads_out, log_total = done[4:7]
            came = regroup(done[0:4])
        part, heads = after_layer(place, came, 3 * layer, proj_of[layer], mlp_out)
        parts = (part, swap_core(part))
        extra = (parts, grad, proj_of[1])
        saved.append((states, attn_in, mlp_in, active, slope, (heads, swap_core(heads))))
    result = (states.astype(F32) + (parts[0] + parts[1])).astype(BF)
    layer_out = jnp.where(first, saved[1][0], result)

    grads = [None, None]
    for layer in (1, 0):
        states, attn_in, mlp_in, active, slope, heads = saved[layer]
        if layer == 1:
            mlp_grad, pack = mlp_back(place, grad, active, slope, mlp_in, mlp_of[1])
        else:
            sent = heads_grad(place, grad, proj_of[0])
            came = regroup(sent)
            mlp_grad, pack = mlp_back(
                place, after(grad, sent), active, slope, mlp_in, mlp_of[0], heads
            )
            came = after(came, pack)
            sent = attend_back(place, came, places, kept, heads_out, log_total)
            sum_a = scatter_sum(pack)
            came = regroup(sent)
        through, mixed, norm_sums, *heads_of = mixed_back(
            place, came, qkv_of[layer], norms[layer], turns, states, mlp_grad
        )
        if layer == 1:
            pack = weight_back(place, attn_in, mixed, norm_sums, (pack, heads_of[0], swap_core(heads_of[0]), grad))
            total = lax.psum_scatter(pack, "shard", scatter_dimension=0, tiled=False)
        else:
            pack, sum_a = lax.optimization_barrier(
                (weight_back(place, attn_in, mixed, norm_sums), sum_a)
            )
            pieces_a = regroup([sum_a] * 4)
            pieces_b = regroup([scatter_sum(pack)] * 4)
        swapped = swap_core(through)
        if layer == 1:
            swapped = after(swapped, pack)
        grad = end_back(place, states, grad, through, swapped)
        grads[layer] = grad
    grads_out = jnp.where(first, grads[0], grads[1])

    keep, send = choose(place, regroup([total] * 4) + pieces_a + pieces_b)
    qkv_grad, proj_grad, up_grad, down_grad, norm_sums = unpack(place, keep, swap_core(send))
    return (
        layer_out.reshape(1, MICRO, 1, BLOCK, D),
        grads_out.reshape(1, MICRO, 1, BLOCK, D),
        qkv_grad[None],
        proj_grad[None],
        up_grad[None],
        down_grad[None],
        norm_sums[None, 0:2, 0:32],
        norm_sums[None, 2:4, 0:32],
    )


def solution(mesh):
    placed = (
        P(None, "shard", "seq", None),
        P(None, "shard", "seq"),
        P(None, "shard", "seq", None),
        P("section", "shard", None),
        P("section", "shard", None),
        P("section", "shard", None),
        P("section", "shard", None),
        P("section", None, "shard"),
        P("section", None, "shard"),
    )
    return jax.shard_map(
        on_device,
        mesh=mesh,
        in_specs=placed,
        out_specs=(
            P("section", None, "shard", "seq", None),
            P("section", None, "shard", "seq", None),
            P("section", "shard", None),
            P("section", "shard", None),
            P("section", "shard", None),
            P("section", "shard", None),
            P("section", None, "shard"),
            P("section", None, "shard"),
        ),
        check_vma=False,
    )
```

```python
import functools

import jax
import jax.numpy as jnp
from jax import lax
from jax.experimental import pallas as pl
from jax.experimental.pallas import tpu as pltpu
from jax.sharding import PartitionSpec as P

D = 512
HEADS = 8
HEAD = 64
ROT = 16
MICRO = 3
BLOCK = 256
TOKENS = MICRO * BLOCK
NORM_EPS = 1e-05
MASKED = -1e30
BF = jnp.bfloat16
F32 = jnp.float32
SHIFTS = (0, 1, 2, 3)
VMEM_LIMIT = 24 * 1024 * 1024


def dims(left, right, left_dim, right_dim):
    return lax.dot_general(
        left, right, (((left_dim,), (right_dim,)), ((), ())), preferred_element_type=F32
    )


def struct(shape, dtype):
    return jax.ShapeDtypeStruct(shape, dtype)


def in_hbm(array):
    return pltpu.with_memory_space_constraint(array, pltpu.HBM)


def call(body, place, grid, ins, outs, scratch=(), flops=10**9, moved=4 * 10**6):
    specs = [pl.BlockSpec(block, index) for _, block, index in ins]
    out_specs = [pl.BlockSpec(out[2], out[3]) for out in outs]
    return pl.pallas_call(
        body,
        out_shape=[
            (pltpu.HBM if out[4:] else struct)(out[0], out[1]) for out in outs
        ],
        grid_spec=pltpu.PrefetchScalarGridSpec(
            num_scalar_prefetch=1,
            grid=grid,
            in_specs=specs,
            out_specs=out_specs,
            scratch_shapes=list(scratch),
        ),
        compiler_params=pltpu.CompilerParams(
            vmem_limit_bytes=VMEM_LIMIT, dimension_semantics=("arbitrary",) * len(grid)
        ),
        cost_estimate=pl.CostEstimate(flops=flops, bytes_accessed=moved, transcendentals=0),
    )(place, *[array for array, _, _ in ins])


def whole(array):
    rank = array.ndim
    return (array, array.shape, lambda *_: (0,) * rank)


def whole_out(shape, dtype):
    rank = len(shape)
    return (shape, dtype, shape, lambda *_: (0,) * rank)


def kept_in_hbm(out):
    return out + (True,)


def rows(array):
    return (array, (BLOCK, array.shape[1]), lambda m, _: (m, 0))


def rows_out(width, dtype):
    return ((TOKENS, width), dtype, (BLOCK, width), lambda m, _: (m, 0))


def lanes(array):
    lead = array.shape[:-1]
    rank = len(lead)
    return (array, lead + (BLOCK,), lambda m, _: (0,) * rank + (m,))


def lanes_out(lead, dtype):
    rank = len(lead)
    return (lead + (TOKENS,), dtype, lead + (BLOCK,), lambda m, _: (0,) * rank + (m,))


def by_micro(array):
    rank = array.ndim - 1
    return (array, (1,) + array.shape[1:], lambda m, _: (m,) + (0,) * rank)


def by_micro_out(shape, dtype):
    rank = len(shape) - 1
    return (shape, dtype, (1,) + shape[1:], lambda m, _: (m,) + (0,) * rank)


def pack_body(place, qkv, proj, up, down, norms, mine, other, held):
    low = lax.broadcasted_iota(jnp.int32, (32, 128), 1) < 64
    for half in range(2):
        for pair in range(8):
            first = up[:, 256 * pair : 256 * pair + 128].astype(F32)
            second = up[:, 256 * pair + 128 : 256 * pair + 256].astype(F32)
            if half == 0:
                cut = jnp.where(low, first, pltpu.roll(second, 64, 1))
            else:
                cut = jnp.where(low, pltpu.roll(first, 64, 1), second)
            at = 128 * (pair % 2)
            held[half, 32 * (pair // 2) : 32 * (pair // 2) + 32, at : at + 128] = cut.astype(BF)
        for side in range(2):
            held[half, 128 + 64 * side : 192 + 64 * side, :] = down[
                64 * half : 64 * half + 64, 256 * side : 256 * side + 256
            ]
            held[half, 256 + 32 * side : 288 + 32 * side, :] = proj[
                :, 256 * side : 256 * side + 256
            ]
        for part in range(3):
            at = 512 * part + 256 * half
            held[half, 320 + 32 * part : 352 + 32 * part, :] = qkv[:, at : at + 256]
        held[half, 416:432, 0:128] = norms[...]
        held[half, 416:432, 128:256] = norms[...]
    core = place[1]
    mine[...] = held[core]
    other[...] = held[1 - core]


def pack_weights(place, qkv, proj, up, down, norms):
    return call(
        pack_body,
        place,
        (1,),
        [whole(in_hbm(array)) for array in (qkv, proj, up, down)] + [whole(norms)],
        [whole_out((432, 256), BF), whole_out((432, 256), BF)],
        [pltpu.VMEM((2, 432, 256), BF)],
    )


def sort_body(place, mine, received, early, middle, late):
    first = place[1] == 0
    kept = mine[...]
    came = received[...]
    layer0 = jnp.where(first, kept, came)
    layer1 = jnp.where(first, came, kept)
    norms = jnp.concatenate([layer0[416:432, 0:128], layer1[416:432, 0:128]], axis=1)
    for peer in range(16):
        early[peer, 0:96, :] = layer0[320:416]
        early[peer, 96:112, :] = norms
    middle[0:320, :] = layer0[0:320]
    middle[320:480, :] = layer1[256:416]
    late[...] = layer1[0:256]


def sort_weights(place, mine, received):
    return call(
        sort_body,
        place,
        (1,),
        [whole(mine), whole(received)],
        [whole_out(shape, BF) for shape in ((16, 112, 256), (480, 256), (256, 256))],
    )


def shift_z(value, step):
    return lax.ppermute(value, "seq", [(z, (z + step) % 4) for z in range(4)])


def swap_core(value):
    return lax.ppermute(value, "section", [(0, 1), (1, 0)])


def to_owners(pack):
    return lax.all_to_all(pack, "shard", 0, 0, tiled=True)


def after(value, *others):
    return lax.optimization_barrier((value, others))[0]


def regroup(values):
    got = {0: values[0]}
    for step in (1, 3, 2):
        got[step] = shift_z(values[step], step)
    return [got[step] for step in SHIFTS]


def unit_of(states):
    centre = states - jnp.mean(states, axis=-1, keepdims=True)
    scaled = lax.rsqrt(jnp.mean(centre * centre, axis=-1, keepdims=True) + NORM_EPS)
    return centre * scaled, scaled


def qkv_rows(weights):
    array, first = weights
    return [
        (array, (16, 32, 256), functools.partial(lambda at, m, _: (0, at, 0), first + part))
        for part in range(3)
    ]


def proj_rows(weights):
    array, first = weights
    return (array, (8, 64, 256), lambda m, place: (place[1], first, 0))


def put_heads_grad(grad, proj, held, first):
    weight = proj[...]
    total = dims(weight[:, 0:32].reshape(256, 256), grad[:, 0:256], 1, 1) + dims(
        weight[:, 32:64].reshape(256, 256), grad[:, 256:512], 1, 1
    )
    for head in range(4):
        held[head, first : first + 64, :] = total[64 * head : 64 * head + 64].astype(BF)


def before_body(second, place, *refs):
    refs = list(refs)
    states = refs.pop(0)[...].astype(F32)
    if second:
        part_a, part_b, grad, proj = [refs.pop(0) for _ in range(4)]
        states = (states + (part_a[...] + part_b[...])).astype(BF)
    wq, wk, wv, norms, turns = refs[:5]
    outs = refs[5:9]
    attn_ref, mlp_ref = refs[9:11]
    held = refs[-1]
    if second:
        refs[11][...] = states
        states = states.astype(F32)
    unit, _ = unit_of(states)
    attn_in = (unit * norms[0:1, :] + norms[2:3, :]).astype(BF)
    attn_ref[...] = attn_in
    mlp_ref[...] = (unit * norms[1:2, :] + norms[3:4, :]).astype(BF)
    cosine, sine = turns[0], turns[1]
    for part, weight in enumerate((wq, wk, wv)):
        mixed = dims(weight[...].reshape(D, 256), attn_in, 0, 1)
        for head in range(4):
            block = mixed[64 * head : 64 * head + 64]
            if part < 2:
                a, b = block[0:8], block[8:16]
                block = jnp.concatenate(
                    [a * cosine - b * sine, b * cosine + a * sine, block[16:]], axis=0
                )
            if part == 0:
                block = block * 0.125
            held[head, 64 * part : 64 * part + 64, :] = block.astype(BF)
    if second:
        put_heads_grad(grad, proj, held, 192)
    for step in SHIFTS:
        outs[step][...] = held[lax.rem(place[0] + step, 4)]


def before_layer(place, states, extra, weights, norms, turns):
    array, first = weights
    ins = [rows(states)]
    depth = 192
    if extra:
        parts, grad, proj = extra
        ins += [rows(parts[0]), rows(parts[1]), rows(grad), proj_rows(proj)]
        depth = 256
    ins += qkv_rows(weights)
    ins += [whole(norms), lanes(turns)]
    outs = [lanes_out((depth,), BF) for _ in SHIFTS]
    outs += [kept_in_hbm(rows_out(D, BF)), kept_in_hbm(rows_out(D, BF))]
    if extra:
        outs.append(kept_in_hbm(rows_out(D, BF)))
    return call(
        functools.partial(before_body, bool(extra)),
        place,
        (MICRO,),
        ins,
        outs,
        [pltpu.VMEM((4, depth, BLOCK), BF)],
        flops=1_200_000_000,
        moved=6_000_000,
    )


def mlp_body(place, mlp_in, up, down, out, active_ref, slope_ref):
    step = pl.program_id(0)
    hidden = jnp.dot(mlp_in[...], up[...].reshape(D, 256), preferred_element_type=F32)
    cdf = 0.5 * (1.0 + lax.erf(hidden * 0.7071067811865476))
    pdf = jnp.exp(-0.5 * hidden * hidden) * 0.3989422804014327
    active = (hidden * cdf).astype(BF)
    active_ref[...] = active
    slope_ref[...] = cdf + hidden * pdf
    lower = down[...]
    both = jnp.concatenate(
        [lower[:, 0:64].reshape(256, 256), lower[:, 64:128].reshape(256, 256)], axis=1
    )
    product = jnp.dot(active, both, preferred_element_type=F32)

    @pl.when(step == 0)
    def _():
        out[...] = product

    @pl.when(step > 0)
    def _():
        out[...] += product


def mlp_layer(place, mlp_in, weights):
    return call(
        mlp_body,
        place,
        (4,),
        [
            whole(mlp_in),
            (in_hbm(weights), (16, 32, 256), lambda b, _: (0, b, 0)),
            (in_hbm(weights), (4, 128, 256), lambda b, _: (b, 1, 0)),
        ],
        [
            whole_out((TOKENS, D), F32),
            kept_in_hbm(((TOKENS, 1024), BF, (TOKENS, 256), lambda b, _: (0, b))),
            kept_in_hbm(((TOKENS, 1024), F32, (TOKENS, 256), lambda b, _: (0, b))),
        ],
        flops=6_000_000_000,
        moved=12_000_000,
    )


def put_starts(place, places, starts):
    along = lax.broadcasted_iota(jnp.int32, (1, BLOCK), 1)
    for step in SHIFTS:
        source = lax.rem(place[0] - step + 4, 4)
        starts[source] = along + BLOCK * source - places[step][...]


def allowed_keys(starts, query_block, key_block):
    keys = lax.broadcasted_iota(jnp.int32, (BLOCK, BLOCK), 0) + BLOCK * key_block
    allowed = keys >= starts[query_block]
    if query_block == key_block:
        queries = lax.broadcasted_iota(jnp.int32, (BLOCK, BLOCK), 1) + BLOCK * query_block
        allowed = allowed & (keys <= queries)
    return allowed


def attend_body(place, *refs):
    came, places = refs[0:4], refs[4:8]
    outs = refs[8:12]
    kept, heads_out, log_total = refs[12:15]
    starts, keys = refs[15:17]
    for step in SHIFTS:
        source = lax.rem(place[0] - step + 4, 4)
        kept[0, source] = came[step][...]
    put_starts(place, places, starts)
    for j in range(4):
        keys[j] = kept[0, j, 64:128].T
    for i in range(4):
        query = kept[0, i, 0:64]
        scores = []
        for j in range(i + 1):
            raw = jnp.dot(keys[j], query, preferred_element_type=F32)
            scores.append(jnp.where(allowed_keys(starts, i, j), raw, MASKED))
        peak = functools.reduce(
            jnp.maximum, [jnp.max(s, axis=0, keepdims=True) for s in scores]
        )
        total = jnp.zeros((1, BLOCK), F32)
        acc = jnp.zeros((HEAD, BLOCK), F32)
        for j in range(i + 1):
            probs = jnp.exp(scores[j] - peak)
            total = total + jnp.sum(probs, axis=0, keepdims=True)
            acc = acc + jnp.dot(
                kept[0, j, 128:192], probs.astype(BF), preferred_element_type=F32
            )
        heads_out[0, i] = (acc / total).astype(BF)
        log_total[0, i] = peak + jnp.log(total)
    for step in SHIFTS:
        outs[step][...] = heads_out[0, lax.rem(place[0] + step, 4)]


def attend(place, came, places):
    return call(
        attend_body,
        place,
        (MICRO,),
        [lanes(piece) for piece in came] + [lanes(piece) for piece in places],
        [lanes_out((HEAD,), BF) for _ in SHIFTS]
        + [
            kept_in_hbm(by_micro_out((MICRO, 4, 192, BLOCK), BF)),
            kept_in_hbm(by_micro_out((MICRO, 4, HEAD, BLOCK), BF)),
            kept_in_hbm(by_micro_out((MICRO, 4, 1, BLOCK), F32)),
        ],
        [pltpu.VMEM((4, 1, BLOCK), jnp.int32), pltpu.VMEM((4, BLOCK, HEAD), BF)],
        flops=8_000_000_000,
        moved=4_000_000,
    )


def after_body(place, *refs):
    came = refs[0:4]
    proj, mlp_out, out, heads = refs[4:8]
    for step in SHIFTS:
        source = lax.rem(place[0] - step + 4, 4)
        at = pl.multiple_of(source * HEAD, HEAD)
        heads[pl.ds(at, HEAD), :] = came[step][...]
    held = heads[...]
    weight = proj[...]
    for side in range(2):
        span = slice(256 * side, 256 * side + 256)
        product = dims(held, weight[:, 32 * side : 32 * side + 32].reshape(256, 256), 0, 0)
        out[:, span] = mlp_out[:, span] + product


def after_layer(place, came, first, proj, mlp_out):
    return call(
        after_body,
        place,
        (MICRO,),
        [(piece, (HEAD, BLOCK), lambda m, _: (first, m)) for piece in came]
        + [proj_rows(proj), rows(mlp_out)],
        [rows_out(D, F32), lanes_out((256,), BF)],
        flops=800_000_000,
        moved=4_000_000,
    )


def heads_grad_body(place, grad, proj, *refs):
    outs, held = refs[0:4], refs[4]
    put_heads_grad(grad, proj, held, 0)
    for step in SHIFTS:
        outs[step][...] = held[lax.rem(place[0] + step, 4)]


def heads_grad(place, grad, proj):
    return call(
        heads_grad_body,
        place,
        (MICRO,),
        [rows(grad), proj_rows(proj)],
        [lanes_out((HEAD,), BF) for _ in SHIFTS],
        [pltpu.VMEM((4, HEAD, BLOCK), BF)],
        flops=800_000_000,
        moved=2_000_000,
    )


def put_proj(core, heads, other_heads, half_grad, pack, first):
    for side, held in ((core, heads), (1 - core, other_heads)):
        part = jnp.dot(held[...], half_grad[...], preferred_element_type=F32)
        pack[pl.ds(8 * side, 8), first : first + 32, :] = part.astype(BF).reshape(8, 32, 256)


def half_columns(grad):
    return (grad, (TOKENS, 256), lambda m, place: (0, place[1]))


def mlp_back_body(with_proj, place, grad, active, slope, mlp_in, up, down, *refs):
    out, pack = refs[-2:]
    step = pl.program_id(0)
    lower = down[...]
    both = jnp.concatenate(
        [lower[:, 0:64].reshape(256, 256), lower[:, 64:128].reshape(256, 256)], axis=1
    )
    active_grad = dims(grad[...], both, 1, 1)
    hidden_grad = (active_grad * slope[...]).astype(BF)
    product = dims(hidden_grad, up[...].reshape(D, 256), 1, 1)

    @pl.when(step == 0)
    def _():
        out[...] = product
        if with_proj:
            put_proj(place[1], *refs[:3], pack, 256)

    @pl.when(step > 0)
    def _():
        out[...] += product

    up_part = dims(mlp_in[...], hidden_grad, 0, 0).astype(BF).reshape(16, 32, 256)
    pack[:, pl.ds(pl.multiple_of(32 * step, 32), 32), :] = up_part
    down_part = dims(active[...], grad[...], 0, 0).astype(BF)
    for side in range(2):
        pack[pl.ds(4 * step, 4), 128 + 64 * side : 192 + 64 * side, :] = down_part[
            :, 256 * side : 256 * side + 256
        ].reshape(4, 64, 256)


def mlp_back(place, grad, active, slope, mlp_in, weights, heads=()):
    ins = [
        whole(grad),
        (in_hbm(active), (TOKENS, 256), lambda b, _: (0, b)),
        (in_hbm(slope), (TOKENS, 256), lambda b, _: (0, b)),
        whole(mlp_in),
        (in_hbm(weights), (16, 32, 256), lambda b, _: (0, b, 0)),
        (in_hbm(weights), (4, 128, 256), lambda b, _: (b, 1, 0)),
    ]
    depth = 256
    if heads:
        ins += [whole(array) for array in heads] + [half_columns(grad)]
        depth = 288
    return call(
        functools.partial(mlp_back_body, bool(heads)),
        place,
        (4,),
        ins,
        [whole_out((TOKENS, D), F32), whole_out((16, depth, 256), BF)],
        flops=8_000_000_000,
        moved=14_000_000,
    )


def attend_back_body(place, *refs):
    came, places = refs[0:4], refs[4:8]
    kept_ref, heads_out, log_total = refs[8:11]
    outs = refs[11:15]
    starts, keys, values, grads, acc = refs[15:20]
    for step in SHIFTS:
        source = lax.rem(place[0] - step + 4, 4)
        grads[source] = came[step][...]
    put_starts(place, places, starts)
    acc[...] = jnp.zeros_like(acc)
    for j in range(4):
        keys[j] = kept_ref[0, j, 64:128].T
        values[j] = kept_ref[0, j, 128:192].T
    for i in range(4):
        query = kept_ref[0, i, 0:64]
        grad = grads[i]
        log_row = log_total[0, i]
        centre = jnp.sum(
            grad.astype(F32) * heads_out[0, i].astype(F32), axis=0, keepdims=True
        )
        query_grad = jnp.zeros((HEAD, BLOCK), F32)
        for j in range(i + 1):
            raw = jnp.dot(keys[j], query, preferred_element_type=F32)
            probs = jnp.where(allowed_keys(starts, i, j), jnp.exp(raw - log_row), 0.0)
            probs_grad = jnp.dot(values[j], grad, preferred_element_type=F32)
            scores_grad = (probs * (probs_grad - centre)).astype(BF)
            acc[j, 128:192, :] += dims(grad, probs.astype(BF), 1, 1)
            acc[j, 64:128, :] += dims(query, scores_grad, 1, 1)
            query_grad = query_grad + jnp.dot(
                kept_ref[0, j, 64:128], scores_grad, preferred_element_type=F32
            )
        acc[i, 0:64, :] = query_grad * 0.125
    for step in SHIFTS:
        outs[step][...] = acc[lax.rem(place[0] + step, 4)].astype(BF)


def attend_back(place, came, places, kept, heads_out, log_total):
    return call(
        attend_back_body,
        place,
        (MICRO,),
        [lanes(piece) for piece in came]
        + [lanes(piece) for piece in places]
        + [by_micro(in_hbm(array)) for array in (kept, heads_out, log_total)],
        [lanes_out((192,), BF) for _ in SHIFTS],
        [
            pltpu.VMEM((4, 1, BLOCK), jnp.int32),
            pltpu.VMEM((4, BLOCK, HEAD), BF),
            pltpu.VMEM((4, BLOCK, HEAD), BF),
            pltpu.VMEM((4, HEAD, BLOCK), BF),
            pltpu.VMEM((4, 192, BLOCK), F32),
        ],
        flops=16_000_000_000,
        moved=5_000_000,
    )


def attend_both_body(place, *refs):
    came, places, outs = refs[0:4], refs[4:8], refs[8:12]
    starts, kept, keys, values, acc, out = refs[12:18]
    for step in SHIFTS:
        source = lax.rem(place[0] - step + 4, 4)
        kept[source] = came[step][...]
    put_starts(place, places, starts)
    acc[...] = jnp.zeros_like(acc)
    for j in range(4):
        keys[j] = kept[j, 64:128].T
        values[j] = kept[j, 128:192].T
    for i in range(4):
        query = kept[i, 0:64]
        grad = kept[i, 192:256]
        scores = []
        for j in range(i + 1):
            raw = jnp.dot(keys[j], query, preferred_element_type=F32)
            scores.append(jnp.where(allowed_keys(starts, i, j), raw, MASKED))
        peak = functools.reduce(
            jnp.maximum, [jnp.max(s, axis=0, keepdims=True) for s in scores]
        )
        exps = [jnp.exp(s - peak) for s in scores]
        total = functools.reduce(jnp.add, [jnp.sum(e, axis=0, keepdims=True) for e in exps])
        inverse = 1.0 / total
        result = jnp.zeros((HEAD, BLOCK), F32)
        probs = []
        for j in range(i + 1):
            prob = exps[j] * inverse
            low = prob.astype(BF)
            probs.append(prob)
            result = result + jnp.dot(kept[j, 128:192], low, preferred_element_type=F32)
            acc[j, 128:192, :] += dims(grad, low, 1, 1)
        out[i] = result.astype(BF)
        centre = jnp.sum(grad.astype(F32) * result, axis=0, keepdims=True)
        query_grad = jnp.zeros((HEAD, BLOCK), F32)
        for j in range(i + 1):
            probs_grad = jnp.dot(values[j], grad, preferred_element_type=F32)
            scores_grad = (probs[j] * (probs_grad - centre)).astype(BF)
            acc[j, 64:128, :] += dims(query, scores_grad, 1, 1)
            query_grad = query_grad + jnp.dot(
                kept[j, 64:128], scores_grad, preferred_element_type=F32
            )
        acc[i, 0:64, :] = query_grad * 0.125
    for step in SHIFTS:
        other = lax.rem(place[0] + step, 4)
        outs[step][0:192, :] = acc[other].astype(BF)
        outs[step][192:256, :] = out[other]


def attend_both(place, came, places):
    return call(
        attend_both_body,
        place,
        (MICRO,),
        [lanes(piece) for piece in came] + [lanes(piece) for piece in places],
        [lanes_out((256,), BF) for _ in SHIFTS],
        [
            pltpu.VMEM((4, 1, BLOCK), jnp.int32),
            pltpu.VMEM((4, 256, BLOCK), BF),
            pltpu.VMEM((4, BLOCK, HEAD), BF),
            pltpu.VMEM((4, BLOCK, HEAD), BF),
            pltpu.VMEM((4, 192, BLOCK), F32),
            pltpu.VMEM((4, HEAD, BLOCK), BF),
        ],
        flops=18_000_000_000,
        moved=5_000_000,
    )


def mixed_back_body(with_heads, place, *refs):
    came = refs[0:4]
    wq, wk, wv, norms, turns, states, mlp_grad = refs[4:11]
    out, mixed_ref, sums = refs[11:14]
    cosine, sine = turns[0], turns[1]
    for step in SHIFTS:
        head = lax.rem(place[0] - step + 4, 4)
        at = pl.multiple_of(head * HEAD, HEAD)
        for part in range(3):
            block = came[step][64 * part : 64 * part + 64]
            if part < 2:
                a, b = block[0:8].astype(F32), block[8:16].astype(F32)
                turned = jnp.concatenate(
                    [a * cosine + b * sine, b * cosine - a * sine], axis=0
                ).astype(BF)
                block = jnp.concatenate([turned, block[16:]], axis=0)
            mixed_ref[part, pl.ds(at, HEAD), :] = block
        if with_heads:
            refs[14][pl.ds(at, HEAD), :] = came[step][192:256]
    attn_grad = jnp.zeros((BLOCK, D), F32)
    for part, weight in enumerate((wq, wk, wv)):
        attn_grad = attn_grad + dims(mixed_ref[part], weight[...].reshape(D, 256), 0, 1)
    unit, _ = unit_of(states[...].astype(F32))
    other_grad = mlp_grad[...]
    out[...] = attn_grad * norms[0:1, :] + other_grad * norms[1:2, :]

    @pl.when(pl.program_id(0) == 0)
    def _():
        sums[...] = jnp.zeros_like(sums)

    sums[0:1, :] += jnp.sum(attn_grad * unit, axis=0, keepdims=True)
    sums[1:2, :] += jnp.sum(other_grad * unit, axis=0, keepdims=True)
    sums[2:3, :] += jnp.sum(attn_grad, axis=0, keepdims=True)
    sums[3:4, :] += jnp.sum(other_grad, axis=0, keepdims=True)


def mixed_back(place, came, weights, norms, turns, states, mlp_grad):
    with_heads = came[0].shape[0] == 256
    ins = [lanes(piece) for piece in came]
    ins += qkv_rows(weights)
    ins += [whole(norms), lanes(turns), rows(states), rows(mlp_grad)]
    return call(
        functools.partial(mixed_back_body, with_heads),
        place,
        (MICRO,),
        ins,
        [
            kept_in_hbm(rows_out(D, F32)),
            lanes_out((3, 256), BF),
            whole_out((8, D), F32),
        ]
        + [lanes_out((256,), BF)] * with_heads,
        flops=1_500_000_000,
        moved=6_000_000,
    )


def weight_back_body(with_rest, place, attn_in, mixed, sums, *refs):
    pack = refs[-1]
    first = 0
    if with_rest:
        pack[:, 0:256, :] = refs[0][...]
        put_proj(place[1], *refs[1:4], pack, 256)
        first = 288
    for part in range(3):
        product = dims(attn_in[...], mixed[part], 0, 1)
        at = first + 32 * part
        pack[:, at : at + 32, :] = product.astype(BF).reshape(16, 32, 256)
    at = first + 96
    pack[:, at : at + 16, :] = jnp.zeros((16, 16, 256), BF)
    for owner in range(16):
        tile, shift = owner // 4, owner % 4 * 32
        lines = sums[:, 128 * tile : 128 * tile + 128]
        if shift:
            lines = pltpu.roll(lines, 128 - shift, 1)
        lines = jnp.concatenate([lines, jnp.zeros_like(lines)], axis=0).astype(BF)
        pack[owner, at : at + 16, 0:128] = lines


def weight_back(place, attn_in, mixed, sums, rest=()):
    return call(
        functools.partial(weight_back_body, bool(rest)),
        place,
        (1,),
        [whole(attn_in), whole(mixed), whole(sums)]
        + [whole(array) for array in rest[:3]]
        + [half_columns(array) for array in rest[3:]],
        [(kept_in_hbm if rest else tuple)(whole_out((16, 400 if rest else 112, 256), BF))],
        flops=2_000_000_000,
        moved=6_000_000,
    )[0]


def end_body(place, states, grad, own, came, out):
    unit, scaled = unit_of(states[...].astype(F32))
    through = own[...] + came[...]
    back = scaled * (
        through
        - jnp.mean(through, axis=-1, keepdims=True)
        - unit * jnp.mean(through * unit, axis=-1, keepdims=True)
    )
    out[...] = (grad[...].astype(F32) + back).astype(BF)


def end_back(place, states, grad, own, came):
    return call(
        end_body,
        place,
        (MICRO,),
        [rows(states), rows(grad), rows(own), rows(came)],
        [rows_out(D, BF)],
        flops=100_000_000,
        moved=5_000_000,
    )[0]


def add_up(got):
    return jnp.sum(got.astype(F32), axis=0).astype(BF)


def scatter_sum(pack):
    return add_up(to_owners(pack))


def choose_body(place, *refs):
    keep, send = refs[12:14]
    total = []
    for group in range(3):
        held = refs[4 * group][...].astype(F32)
        for step in range(1, 4):
            held = held + refs[4 * group + step][...].astype(F32)
        total.append(held)
    layer1 = total[0]
    layer0 = jnp.concatenate([total[1], total[2]], axis=0)
    first = place[1] == 0
    keep[...] = jnp.where(first, layer0, layer1)
    send[...] = jnp.where(first, layer1, layer0).astype(BF)


def choose(place, pieces):
    return call(
        choose_body,
        place,
        (1,),
        [whole(piece) for piece in pieces],
        [whole_out((400, 256), F32), whole_out((400, 256), BF)],
    )


def unpack_body(place, keep, got, qkv, proj, up, down, sums, total):
    core = place[1]
    total[core] = keep[...]
    total[1 - core] = got[...].astype(F32)
    low = lax.broadcasted_iota(jnp.int32, (32, 128), 1) < 64
    sums[...] = total[0, 384:392, 0:128] + total[1, 384:392, 0:128]
    for half in range(2):
        for part in range(3):
            at = 512 * part + 256 * half
            qkv[:, at : at + 256] = total[half, 288 + 32 * part : 320 + 32 * part]
        proj[:, 256 * half : 256 * half + 256] = total[half, 256:288]
        for side in range(2):
            down[64 * half : 64 * half + 64, 256 * side : 256 * side + 256] = total[
                half, 128 + 64 * side : 192 + 64 * side
            ]
    for tile in range(16):
        row = 32 * (tile // 4)
        at = 128 * (tile % 4 // 2)
        left = total[0, row : row + 32, at : at + 128]
        right = total[1, row : row + 32, at : at + 128]
        if tile % 2 == 0:
            joined = jnp.where(low, left, pltpu.roll(right, 64, 1))
        else:
            joined = jnp.where(low, pltpu.roll(left, 64, 1), right)
        up[:, 128 * tile : 128 * tile + 128] = joined


def unpack(place, keep, got):
    return call(
        unpack_body,
        place,
        (1,),
        [whole(keep), whole(got)],
        [
            whole_out((32, 1536), F32),
            whole_out((32, 512), F32),
            whole_out((32, 2048), F32),
            whole_out((128, 512), F32),
            whole_out((8, 128), F32),
        ],
        [pltpu.VMEM((2, 400, 256), F32)],
    )


def on_device(
    inputs,
    positions,
    cotangent,
    qkv_weight,
    proj_weight,
    up_weight,
    down_weight,
    norm_gain,
    norm_bias,
):
    core = lax.axis_index("section")
    chip_z = lax.axis_index("seq")
    shard = lax.axis_index("shard")
    first = core == 0
    place = jnp.stack([chip_z, core, shard // 4, shard % 4]).astype(jnp.int32)

    own_norms = jnp.concatenate([norm_gain[0], norm_bias[0]], axis=0).reshape(1, 128)
    mine, other = pack_weights(
        place,
        qkv_weight[0],
        proj_weight[0],
        up_weight[0],
        down_weight[0],
        jnp.broadcast_to(own_norms, (16, 128)),
    )
    early, middle, late = sort_weights(place, mine, swap_core(other))
    places_row = positions.reshape(1, TOKENS)
    gathered, places = lax.optimization_barrier(
        (to_owners(early), regroup([places_row] * 4))
    )
    middle_all = lax.all_gather(middle, "shard")
    late_all = lax.all_gather(late, "shard")
    norms = (
        gathered[:, 96, :]
        .reshape(16, 2, 4, 32)
        .transpose(1, 2, 0, 3)
        .reshape(2, 4, D)
        .astype(F32)
    )
    qkv_of = ((gathered, 0), (middle_all, 12))
    proj_of = ((middle_all, 4), (middle_all, 5))
    mlp_of = (middle_all, late_all)
    rates = 10000.0 ** (-jnp.arange(ROT // 2, dtype=F32) * 2.0 / ROT)
    angles = rates[:, None] * places_row.astype(F32)
    turns = jnp.stack([jnp.cos(angles), jnp.sin(angles)])

    states = inputs.reshape(TOKENS, D)
    grad = cotangent.reshape(TOKENS, D)
    extra = ()
    saved = []
    for layer in range(2):
        done = before_layer(place, states, extra, qkv_of[layer], norms[layer], turns)
        sent, attn_in, mlp_in = done[0:4], done[4], done[5]
        if layer == 1:
            states = done[6]
        came = regroup(sent)
        if layer == 1:
            sent = attend_both(place, came, places)
            mlp_in = after(mlp_in, sent)
            came = regroup(sent)
        mlp_out, active, slope = mlp_layer(place, mlp_in, mlp_of[layer])
        if layer == 0:
            done = attend(place, came, places)
            kept, heads_out, log_total = done[4:7]
            came = regroup(done[0:4])
        part, heads = after_layer(place, came, 3 * layer, proj_of[layer], mlp_out)
        parts = (part, swap_core(part))
        extra = (parts, grad, proj_of[1])
        saved.append((states, attn_in, mlp_in, active, slope, (heads, swap_core(heads))))
    result = (states.astype(F32) + (parts[0] + parts[1])).astype(BF)
    layer_out = jnp.where(first, saved[1][0], result)

    grads = [None, None]
    for layer in (1, 0):
        states, attn_in, mlp_in, active, slope, heads = saved[layer]
        if layer == 1:
            mlp_grad, pack = mlp_back(place, grad, active, slope, mlp_in, mlp_of[1])
        else:
            sent = heads_grad(place, grad, proj_of[0])
            came = regroup(sent)
            mlp_grad, pack = mlp_back(
                place, after(grad, sent), active, slope, mlp_in, mlp_of[0], heads
            )
            came = after(came, pack)
            sent = attend_back(place, came, places, kept, heads_out, log_total)
            got_a = to_owners(pack)
            came = regroup(sent)
        through, mixed, norm_sums, *heads_of = mixed_back(
            place, came, qkv_of[layer], norms[layer], turns, states, mlp_grad
        )
        if layer == 1:
            pack = weight_back(place, attn_in, mixed, norm_sums, (pack, heads_of[0], swap_core(heads_of[0]), grad))
            total = lax.psum_scatter(pack, "shard", scatter_dimension=0, tiled=False)
        else:
            pack, got_a = lax.optimization_barrier(
                (weight_back(place, attn_in, mixed, norm_sums), got_a)
            )
            pieces_a = regroup([add_up(got_a)] * 4)
            pieces_b = regroup([scatter_sum(pack)] * 4)
        swapped = swap_core(through)
        if layer == 1:
            swapped = after(swapped, pack)
        grad = end_back(place, states, grad, through, swapped)
        grads[layer] = grad
    grads_out = jnp.where(first, grads[0], grads[1])

    keep, send = choose(place, regroup([total] * 4) + pieces_a + pieces_b)
    qkv_grad, proj_grad, up_grad, down_grad, norm_sums = unpack(place, keep, swap_core(send))
    return (
        layer_out.reshape(1, MICRO, 1, BLOCK, D),
        grads_out.reshape(1, MICRO, 1, BLOCK, D),
        qkv_grad[None],
        proj_grad[None],
        up_grad[None],
        down_grad[None],
        norm_sums[None, 0:2, 0:32],
        norm_sums[None, 2:4, 0:32],
    )


def solution(mesh):
    placed = (
        P(None, "shard", "seq", None),
        P(None, "shard", "seq"),
        P(None, "shard", "seq", None),
        P("section", "shard", None),
        P("section", "shard", None),
        P("section", "shard", None),
        P("section", "shard", None),
        P("section", None, "shard"),
        P("section", None, "shard"),
    )
    return jax.shard_map(
        on_device,
        mesh=mesh,
        in_specs=placed,
        out_specs=(
            P("section", None, "shard", "seq", None),
            P("section", None, "shard", "seq", None),
            P("section", "shard", None),
            P("section", "shard", None),
            P("section", "shard", None),
            P("section", "shard", None),
            P("section", None, "shard"),
            P("section", None, "shard"),
        ),
        check_vma=False,
    )
```
